32 devices in a mesh: gy: 8 (over z, x), gx: 4 (over y, core).
Axes of the slice: x: 2, y: 2, z: 4, core: 2. Of those that a mesh axis runs over, the one named last changes fastest.
Arguments:
- ensemble: float32 [64, 64, 512], P(None, 'gy', 'gx'), may hold values from -6 to 6
- flow: float32 [3, 64, 512], P(None, 'gy', 'gx')
- obs_cell: int32 [8, 4, 4], P('gy', 'gx'), may hold values from 0 to 1023
- obs_value: float32 [8, 4, 4], P('gy', 'gx'), may hold values from -6 to 6
- obs_var: float32 [8, 4, 4], P('gy', 'gx'), may hold values from 4 to 16
Outputs:
- analysis: float32 [64, 64, 512], P(None, 'gy', 'gx')
The draws below stay inside these ranges and needn't reach their ends.
All inputs are finite; a program needn't handle non-finite values.
Results may differ from the reference program's by a relative error of at most 0.0001.
Values sent between devices are 32-bit elements; how exact they have to be, the bound alone decides.
No kernel may reach another device: no remote copies, remote signals or barrier semaphores. Data moves between devices by JAX's collectives and lax.ppermute only.
A program may use at most 64 MiB of HBM per device.

```python
import math
import jax
import jax.numpy as jnp
from jax import lax

M = 64
CY = 8
CX = 128
OBS_DEV = 4
NY = 64
NX = 512
N_GY = 8
N_GX = 4


def draw_flow(key, part):
    keys = jax.random.split(key, 3)
    level = jax.random.uniform(keys[0], (NY, NX), jnp.float32, jnp.log(0.02), jnp.log(0.2))
    diffusivity = jnp.exp(level)
    along = jax.random.uniform(keys[1], (NY, NX), jnp.float32, -0.2, 0.2)
    across = jax.random.uniform(keys[2], (NY, NX), jnp.float32, -0.2, 0.2)
    return jnp.stack([diffusivity, along, across]).astype(jnp.float32)


def set_ends(entries, key, least, high):
    index_at = [jax.random.randint(jax.random.fold_in(key, axis), (), 0, length) for axis, length in enumerate(entries.shape)]
    longest = entries.shape.index(max(entries.shape))
    neighbour = index_at[:longest] + [(index_at[longest] + 1) % entries.shape[longest]] + index_at[longest + 1:]
    return entries.at[tuple(index_at)].set(least).at[tuple(neighbour)].set(high)


def steps_of(stream_key, extent, shards, smallest, high):
    level, own = 1.0, jax.random.fold_in(stream_key, 6)
    for dim, shards_of in shards:
        heights = jnp.exp(jax.random.uniform(jax.random.fold_in(own, dim), (shards_of,), jnp.float32, smallest / len(shards), high / len(shards)))
        level = level * jnp.repeat(heights, extent[dim] // shards_of).reshape([-1 if axis == dim else 1 for axis in range(len(extent))])
    return level


def noise(key, shape, scale, limit, cuts=(), held_as=jnp.bfloat16):
    level = steps_of(key, shape, cuts, -0.22, 0.18) if cuts else 1.0
    result = jax.random.normal(key, shape, jnp.float32) * scale * level
    return jnp.minimum(jnp.maximum(result, -limit), limit).astype(held_as)


def setup_inputs(seed: int = 0) -> dict:
    arg_keys = jax.random.split(jax.random.key(seed), 6)
    ensemble = noise(arg_keys[0], (M, NY, NX), 1.0, 6.0, ((1, 8), (2, 4)), jnp.float32)
    flow = draw_flow(jax.random.fold_in(arg_keys[5], 71), 0)
    obs_cell = set_ends(jax.random.randint(arg_keys[2], (N_GY, N_GX, OBS_DEV), 0, CY * CX), jax.random.fold_in(arg_keys[2], 1), 0, (CY * CX) - 1).astype(jnp.int32)
    obs_value = noise(arg_keys[3], (N_GY, N_GX, OBS_DEV), 1.0, 6.0, ((0, 8), (1, 4)), jnp.float32)
    obs_var = jnp.clip(jnp.exp(math.log(16.0) - 1.3862944 * jax.random.uniform(arg_keys[4], (N_GY, N_GX, OBS_DEV), jnp.float32) ** steps_of(arg_keys[4], (N_GY, N_GX, OBS_DEV), ((0, 8), (1, 4)), -0.2, 0.2)), 4.0, 16.0)
    return {"ensemble": ensemble, "flow": flow, "obs_cell": obs_cell, "obs_value": obs_value, "obs_var": obs_var}


def prediction_update(state_grid, flow):
    padded = jnp.pad(state_grid, 1)
    north = padded[:-2, 1:-1]
    south = padded[2:, 1:-1]
    west = padded[1:-1, :-2]
    east = padded[1:-1, 2:]
    spread = flow[0] * (north + south + west + east - 4.0 * state_grid)
    return state_grid + spread - 0.5 * flow[1] * (east - west) - 0.5 * flow[2] * (south - north)

def tri_solve(matrix, rhs, lower, flipped):
    return lax.linalg.triangular_solve(matrix, rhs, left_side=True, lower=lower, transpose_a=flipped)

def reference(ensemble, flow, obs_cell, obs_value, obs_var):

    def ensemble_sample(state_grid):
        return prediction_update(prediction_update(state_grid, flow), flow)
    predicted_state = lax.map(ensemble_sample, ensemble)
    ensemble_average = lax.optimization_barrier(jnp.mean(predicted_state, axis=0))
    member_deviation = predicted_state - ensemble_average
    tile_row = lax.broadcasted_iota(jnp.int32, obs_cell.shape, 0)
    tile_col = lax.broadcasted_iota(jnp.int32, obs_cell.shape, 1)
    rows = (tile_row * CY + obs_cell // CX).reshape(-1).astype(jnp.int32)
    cols = (tile_col * CX + obs_cell % CX).reshape(-1).astype(jnp.int32)
    factor = lax.rsqrt(obs_var.reshape(-1))
    scaled = member_deviation[:, rows, cols] * factor
    innovation = (obs_value.reshape(-1) - ensemble_average[rows, cols]) * factor
    eye = jnp.eye(M, dtype=jnp.float32)
    gram = jnp.dot(scaled, scaled.T, precision=lax.Precision.HIGHEST) + (M - 1.0) * eye
    target = jnp.dot(scaled, innovation, precision=lax.Precision.HIGHEST)
    lower = jnp.linalg.cholesky(gram)
    inverse = tri_solve(lower, eye, True, True)
    weights = jnp.dot(inverse, jnp.dot(inverse.T, target, precision=lax.Precision.HIGHEST), precision=lax.Precision.HIGHEST)
    transform = jnp.sqrt(M - 1.0) * inverse + weights[:, None]
    update = jnp.dot(transform.T, member_deviation.reshape(M, -1), precision=lax.Precision.HIGHEST)
    return ensemble_average + update.reshape(member_deviation.shape)
```

```python
import functools

import jax
import jax.numpy as jnp
from jax import lax
from jax.experimental import pallas as pl
from jax.experimental.pallas import tpu as pltpu
from jax.sharding import PartitionSpec as P

F32 = jnp.float32
HIGHEST = lax.Precision.HIGHEST
PARAMS = pltpu.CompilerParams(vmem_limit_bytes=24 * 1024 * 1024)
VMEM = pl.BlockSpec(memory_space=pltpu.VMEM)
SMEM = pl.BlockSpec(memory_space=pltpu.SMEM)


def lanes(shape):
    return lax.broadcasted_iota(jnp.int32, shape, len(shape) - 1)


def rows_of(shape):
    return lax.broadcasted_iota(jnp.int32, shape, len(shape) - 2)


def shifted(x, amount):
    return pltpu.roll(x, amount % x.shape[-1], x.ndim - 1)


def grid_row(ref, row, members, count):
    return ref[pl.ds(row, members, stride=count), :]


def to_row(column):
    n = column.shape[0]
    wide = jnp.broadcast_to(column, (n, 128))
    return jnp.sum(jnp.where(lanes(wide.shape) == rows_of(wide.shape), wide, 0.0), axis=0, keepdims=True)


def pack_rows(members, count, ens_ref, flow_ref, even_ref, odd_ref):
    is_even = lax.axis_index("gy") % 2 == 0
    top, bottom = [
        (grid_row(ens_ref, a, members, count), grid_row(ens_ref, b, members, count), flow_ref[:, a, :])
        for a, b in ((0, 1), (count - 1, count - 2))
    ]
    for ref, first in ((even_ref, is_even), (odd_ref, jnp.logical_not(is_even))):
        near, second, flow = [jnp.where(first, low, high) for low, high in zip(bottom, top)]
        ref[0:members, :] = near
        ref[members : 2 * members, :] = second
        ref[2 * members : 2 * members + 3, :] = flow
        ref[2 * members + 3 :, :] = jnp.zeros((5, 128), F32)


def halo_rows(even_ref, odd_ref, members):
    is_even = lax.axis_index("gy") % 2 == 0
    parts = []
    for lo, hi in ((0, members), (members, 2 * members), (2 * members, 2 * members + 3)):
        e, o = even_ref[lo:hi, :], odd_ref[lo:hi, :]
        parts.append((jnp.where(is_even, o, e), jnp.where(is_even, e, o)))
    return tuple(p[0] for p in parts), tuple(p[1] for p in parts)


def pack_columns(members, count, ens_ref, flow_ref, row_even_ref, row_odd_ref, even_ref, odd_ref):
    is_even = lax.axis_index("gx") % 2 == 0
    north, south = halo_rows(row_even_ref, row_odd_ref, members)
    field = [north[0]] + [grid_row(ens_ref, r, members, count) for r in range(count)] + [south[0]]
    lane = lanes((members, 128))
    for ref, first in ((even_ref, is_even), (odd_ref, jnp.logical_not(is_even))):
        near_lane = jnp.where(first, 127, 0)
        second_lane = jnp.where(first, 126, 1)
        packed = jnp.zeros((members, 128), F32)
        for i, x in enumerate(field):
            packed = jnp.where(lane == i, pltpu.roll(x, (i + 128 - near_lane) % 128, 1), packed)
            packed = jnp.where(lane == 16 + i, pltpu.roll(x, (16 + i + 128 - second_lane) % 128, 1), packed)
        ref[0:members, :] = packed
        flow_rows = []
        for k in range(3):
            column = jnp.sum(jnp.where(lanes((count, 128)) == near_lane, flow_ref[k], 0.0), axis=1, keepdims=True)
            flow_rows.append(shifted(to_row(column), 1))
        flow_rows.append(jnp.zeros((5, 128), F32))
        ref[members : members + 8, :] = jnp.concatenate(flow_rows, axis=0)


def coefficients(k, u, v):
    return 1.0 - 4.0 * k, k + 0.5 * v, k - 0.5 * v, k + 0.5 * u, k - 0.5 * u


def combine(c, own, north, south, west, east):
    return c[0] * own + c[1] * north + c[2] * south + c[3] * west + c[4] * east


def forecast(
    members, count, n_obs, ens_ref, flow_ref, rows_even_ref, rows_odd_ref, cols_even_ref, cols_odd_ref,
    cell_ref, value_ref, var_ref, out_ref, packet_ref,
):
    north, south = halo_rows(rows_even_ref, rows_odd_ref, members)
    is_even = lax.axis_index("gx") % 2 == 0
    cols_even, cols_odd = cols_even_ref[...], cols_odd_ref[...]
    west = jnp.where(is_even, cols_odd, cols_even)
    east = jnp.where(is_even, cols_even, cols_odd)
    zero = jnp.zeros((members, 128), F32)
    field = [north[1], north[0]] + [grid_row(ens_ref, r, members, count) for r in range(count)] + [south[0], south[1]]
    flows = [[north[2][k : k + 1] for k in range(3)]]
    flows += [[flow_ref[k, r : r + 1, :] for k in range(3)] for r in range(count)]
    flows += [[south[2][k : k + 1] for k in range(3)]]
    coeffs = [coefficients(*f) for f in flows]
    lane = lanes((members, 128))

    def neighbours(x, west_col, east_col, i):
        w = jnp.where(lane == 0, shifted(west_col, -i), shifted(x, 1))
        e = jnp.where(lane == 127, shifted(east_col, 127 - i), shifted(x, -1))
        return w, e

    def own_column(which):
        packed = zero
        for r in range(count):
            packed = jnp.where(lane == r + 1, shifted(field[r + 2], r + 1 - which), packed)
        return packed

    west_x, east_x = west[:members], east[:members]
    middle = []
    for i in range(count + 2):
        x = field[i + 1]
        middle.append(combine(coeffs[i], x, field[i], field[i + 2], *neighbours(x, west_x, east_x, i)))
    side = []
    for block, which in ((west, 0), (east, 127)):
        x = block[:members]
        c = coefficients(*[block[members + k : members + k + 1] for k in range(3)])
        second, own = shifted(x, -16), own_column(which)
        pair = (second, own) if which == 0 else (own, second)
        side.append(combine(c, x, shifted(x, 1), shifted(x, -1), *pair))
    for r in range(count):
        x = middle[r + 1]
        out_ref[r * members : (r + 1) * members, :] = combine(
            coeffs[r + 1], x, middle[r], middle[r + 2], *neighbours(x, side[0], side[1], r + 1)
        )
    sub = rows_of((n_obs, 128))
    at = jnp.zeros((n_obs, 128), F32)
    value = jnp.zeros((n_obs, 128), F32)
    var = jnp.ones((n_obs, 128), F32)
    for j in range(n_obs):
        cell = cell_ref[j]
        row, col = cell // 128, cell % 128
        x = out_ref[pl.ds(pl.multiple_of(row * members, members), members), :]
        column = jnp.sum(jnp.where(lane == col, x, 0.0), axis=1, keepdims=True)
        at = jnp.where(sub == j, to_row(column), at)
        value = jnp.where(sub == j, value_ref[j], value)
        var = jnp.where(sub == j, var_ref[j], var)
    mean = jnp.sum(at, axis=1, keepdims=True) * (1.0 / members)
    obs_lane = lanes((n_obs, 128))
    raw = jnp.where(obs_lane < members, at - mean, jnp.where(obs_lane == members, value - mean, 0.0))
    packet_ref[...] = raw * lax.rsqrt(var)


def analyse(members, count, f_ref, obs_ref, out_ref):
    scaled = obs_ref[...]
    full = lax.dot_general(
        scaled, scaled, (((0,), (0,)), ((), ())), precision=HIGHEST, preferred_element_type=F32
    )
    lane, sub = lanes((members, 128)), rows_of((members, 128))
    a = full[:members, :] + jnp.where(lane == sub, members - 1.0, 0.0)
    for j in range(members):
        row = a[j : j + 1, :]
        column = a[:, j : j + 1]
        below = sub > j
        factor = jnp.where(below, column * (1.0 / row[:, j : j + 1]), 0.0)
        unit = jnp.where(lane[:1] == j, 1.0, row)
        a = jnp.where(below & (lane == j), 0.0, a) - factor * unit
    diagonal = jnp.sum(jnp.where(lane == sub, a, 0.0), axis=1, keepdims=True)
    scale = lax.rsqrt(diagonal)
    inverse = scale * jnp.where(lane < sub, a, jnp.where(lane == sub, 1.0, 0.0))
    reduced = scale * a[:, members : members + 1]
    weights = jnp.sum(reduced * inverse, axis=0, keepdims=True)
    transform = jnp.sqrt(members - 1.0) * inverse + weights
    share = (1.0 - jnp.sum(jnp.where(lane < members, transform, 0.0), axis=1, keepdims=True)) * (1.0 / members)
    transform = (transform + share)[:, :members]
    for r in range(count):
        out_ref[pl.ds(r, members, stride=count), :] = jnp.dot(
            transform, f_ref[r * members : (r + 1) * members, :], precision=HIGHEST, preferred_element_type=F32
        )


def swap(x, axis, offset):
    pairs = [(i, i + 1) for i in range(offset, lax.axis_size(axis) - 1, 2)]
    return lax.ppermute(x, axis, pairs + [(b, a) for a, b in pairs])


def gathered(packet):
    for axis in ("gx", "gy"):
        size = lax.axis_size(axis)
        if size & (size - 1):
            packet = lax.all_gather(packet, axis, tiled=True)
            continue
        step = 1
        while step < size:
            other = lax.ppermute(packet, axis, [(i, i ^ step) for i in range(size)])
            packet = jnp.concatenate([packet, other], axis=0)
            step *= 2
    return packet


def body(ensemble, flow, obs_cell, obs_value, obs_var):
    members, count, width = ensemble.shape
    n_obs = obs_cell.shape[-1]
    ens = ensemble.reshape(members * count, width)
    call = functools.partial(pl.pallas_call, compiler_params=PARAMS)

    def shape(rows):
        return jax.ShapeDtypeStruct((rows, width), F32)

    rows_even, rows_odd = call(
        functools.partial(pack_rows, members, count),
        out_shape=[shape(2 * members + 8)] * 2,
        in_specs=[VMEM] * 2,
        out_specs=[VMEM] * 2,
        name="pack_rows",
    )(ens, flow)
    rows_even, rows_odd = swap(rows_even, "gy", 0), swap(rows_odd, "gy", 1)
    cols_even, cols_odd = call(
        functools.partial(pack_columns, members, count),
        out_shape=[shape(members + 8)] * 2,
        in_specs=[VMEM] * 4,
        out_specs=[VMEM] * 2,
        name="pack_columns",
    )(ens, flow, rows_even, rows_odd)
    cols_even, cols_odd = swap(cols_even, "gx", 0), swap(cols_odd, "gx", 1)
    field, packet = call(
        functools.partial(forecast, members, count, n_obs),
        out_shape=[shape(members * count), shape(n_obs)],
        in_specs=[VMEM] * 6 + [SMEM] * 3,
        out_specs=[VMEM] * 2,
        name="forecast",
    )(ens, flow, rows_even, rows_odd, cols_even, cols_odd, obs_cell.reshape(-1), obs_value.reshape(-1), obs_var.reshape(-1))
    scaled = gathered(packet)
    out = call(
        functools.partial(analyse, members, count),
        out_shape=shape(members * count),
        in_specs=[VMEM] * 2,
        out_specs=VMEM,
        name="analyse",
    )(field, scaled)
    return out.reshape(ensemble.shape)


def solution(mesh):
    return jax.shard_map(
        body,
        mesh=mesh,
        in_specs=(
            P(None, "gy", "gx"),
            P(None, "gy", "gx"),
            P("gy", "gx", None),
            P("gy", "gx", None),
            P("gy", "gx", None),
        ),
        out_specs=P(None, "gy", "gx"),
        check_vma=False,
    )
```

```python
import functools

import jax
import jax.numpy as jnp
from jax import lax
from jax.experimental import pallas as pl
from jax.experimental.pallas import tpu as pltpu
from jax.sharding import PartitionSpec as P

F32 = jnp.float32
HIGHEST = lax.Precision.HIGHEST
PARAMS = pltpu.CompilerParams(vmem_limit_bytes=24 * 1024 * 1024)
VMEM = pl.BlockSpec(memory_space=pltpu.VMEM)
SMEM = pl.BlockSpec(memory_space=pltpu.SMEM)


def lanes(shape):
    return lax.broadcasted_iota(jnp.int32, shape, len(shape) - 1)


def rows_of(shape):
    return lax.broadcasted_iota(jnp.int32, shape, len(shape) - 2)


def shifted(x, amount):
    return pltpu.roll(x, amount % x.shape[-1], x.ndim - 1)


EDGE = 16
BLOCK = 4 * EDGE + 8
LEFT, RIGHT, LEFT_MID, RIGHT_MID, OBS = 0, EDGE, 2 * EDGE, 3 * EDGE, 4 * EDGE
ANY = pl.BlockSpec(memory_space=pl.ANY)


def coefficients(k, u, v):
    return 1.0 - 4.0 * k, k + 0.5 * v, k - 0.5 * v, k + 0.5 * u, k - 0.5 * u


def combine(c, own, north, south, west, east):
    return c[0] * own + c[1] * north + c[2] * south + c[3] * west + c[4] * east


def transposed(x):
    return jnp.concatenate([x, jnp.zeros((128 - x.shape[0], 128), F32)], axis=0).T


def load(
    members, count, n_obs, ens_hbm, flow_hbm, cell_hbm, value_hbm, var_hbm,
    field_ref, flow_ref, obs_ref, even_ref, odd_ref, cell_ref, value_ref, var_ref, sems,
):
    order = [0, count - 1, 1, count - 2] + list(range(2, count - 2))
    copies = [pltpu.make_async_copy(flow_hbm, flow_ref, sems.at[count])]
    copies += [
        pltpu.make_async_copy(ens_hbm.at[:, r, :], field_ref.at[pl.ds(r * members, members), :], sems.at[r]) for r in order
    ]
    small = [
        pltpu.make_async_copy(src, dst, sems.at[count + 1 + i])
        for i, (src, dst) in enumerate(((cell_hbm, cell_ref), (value_hbm, value_ref), (var_hbm, var_ref)))
    ]
    for copy in copies + small:
        copy.start()
    for copy in copies + small:
        copy.wait()
    is_even = lax.axis_index("gy") % 2 == 0

    def grid_row(r):
        return field_ref[r * members : (r + 1) * members, :]

    top, bottom = [(grid_row(a), grid_row(b), flow_ref[:, a, :]) for a, b in ((0, 1), (count - 1, count - 2))]
    for ref, first in ((even_ref, is_even), (odd_ref, jnp.logical_not(is_even))):
        near, second, flow = [jnp.where(first, low, high) for low, high in zip(bottom, top)]
        ref[0:members, :] = near
        ref[members : 2 * members, :] = second
        ref[2 * members : 2 * members + 3, :] = flow
        ref[2 * members + 3 :, :] = jnp.zeros((5, 128), F32)
    sub = rows_of((8, 128))
    for i, (ref, rest) in enumerate(((cell_ref, 0.0), (value_ref, 0.0), (var_ref, 1.0))):
        block = jnp.full((8, 128), rest, F32)
        for j in range(n_obs):
            block = jnp.where(sub == j, ref[j].astype(F32), block)
        obs_ref[8 * i : 8 * i + 8, :] = block


def halo_rows(even_ref, odd_ref, members):
    is_even = lax.axis_index("gy") % 2 == 0
    parts = []
    for lo, hi in ((0, members), (members, 2 * members), (2 * members, 2 * members + 3)):
        e, o = even_ref[lo:hi, :], odd_ref[lo:hi, :]
        parts.append((jnp.where(is_even, o, e), jnp.where(is_even, e, o)))
    return tuple(p[0] for p in parts), tuple(p[1] for p in parts)


def tall_coefficients(scratch, flow_ref, north_flow, south_flow, count):
    for k in range(3):
        scratch[k] = jnp.zeros((EDGE, 128), F32)
        scratch[k, 1:2, :] = north_flow[k : k + 1]
        scratch[k, 2 : 2 + count, :] = flow_ref[k]
        scratch[k, 2 + count : 3 + count, :] = south_flow[k : k + 1]
    return coefficients(*[scratch[k] for k in range(3)])


def observe(members, count, n_obs, field_ref, flow_ref, obs_ref, even_ref, odd_ref, out_ref, tall_ref):
    north, south = halo_rows(even_ref, odd_ref, members)
    field = [north[1], north[0]]
    field += [field_ref[r * members : (r + 1) * members, :] for r in range(count)] + [south[0], south[1]]
    coeffs = tall_coefficients(tall_ref, flow_ref, north[2], south[2], count)
    lane, sub = lanes((EDGE, 128)), rows_of((EDGE, 128))
    wide = lanes((members, 128))
    own, up, down, left, right = coeffs
    has_west = lax.axis_index("gx") > 0
    has_east = lax.axis_index("gx") < lax.axis_size("gx") - 1
    zero = jnp.zeros((EDGE, 128), F32)

    def spread(w):
        to_west, to_east = left * w, right * w
        inside = (
            own * w
            + pltpu.roll(up * w, EDGE - 1, 0)
            + pltpu.roll(down * w, 1, 0)
            + jnp.where(lane == 127, 0.0, shifted(to_west, -1))
            + jnp.where(lane == 0, 0.0, shifted(to_east, 1))
        )
        return inside, jnp.where(has_west, to_west[:, 0:1], 0.0), jnp.where(has_east, to_east[:, 127:128], 0.0)

    packed = jnp.zeros((members, 128), F32)
    second = jnp.zeros((members, 128), F32)
    for i in range(1, count + 3):
        x = field[i]
        packed = jnp.where(wide == i, shifted(x, i), packed)
        packed = jnp.where(wide == EDGE + i, shifted(x, EDGE + i - 127), packed)
        if 2 <= i < count + 2:
            second = jnp.where(wide == i, shifted(x, i - 1), second)
            second = jnp.where(wide == EDGE + i, shifted(x, EDGE + i - 126), second)

    def edge_row(low, high):
        both = jnp.where(lane == sub, low[:, 0:1], jnp.where(lane == sub + EDGE, high[:, 127:128], 0.0))
        return jnp.sum(both, axis=0, keepdims=True)

    middle = (
        edge_row(own, own) * packed
        + edge_row(up, up) * shifted(packed, 1)
        + edge_row(down, down) * shifted(packed, -1)
        + edge_row(right, left) * second
    )
    packed = jnp.where(wide < 2 * EDGE, packed, jnp.where(wide < 4 * EDGE, shifted(middle, 2 * EDGE), 0.0))
    meta = jnp.where(lane == 80, left[:, 0:1], jnp.where(lane == 81, right[:, 127:128], zero))
    position = ((sub - 2) * 128 + lane).astype(F32)
    inner = (sub >= 2) & (sub < 2 + count)
    for j in range(n_obs):
        here = jnp.where(inner & (position == obs_ref[j : j + 1, :]), 1.0, 0.0)
        w, mid_west, mid_east = spread(here)
        w, west, east = spread(w)
        total = w[0:1, :] * field[0]
        for i in range(1, count + 4):
            total = total + w[i : i + 1, :] * field[i]
        packed = jnp.where(wide == OBS + j, jnp.sum(total, axis=1, keepdims=True), packed)
        for at, column in ((64, west), (68, east), (72, mid_west), (76, mid_east)):
            meta = jnp.where(lane == at + j, column, meta)
    turned = transposed(packed)
    out_ref[0:EDGE, :] = turned[0:EDGE, :] + meta
    out_ref[EDGE:OBS, :] = turned[EDGE:OBS, :]
    top_lane = lanes((8, 128))
    value, factor = obs_ref[8:16, :], lax.rsqrt(obs_ref[16:24, :])
    out_ref[OBS : OBS + 8, :] = jnp.where(
        top_lane == 64, value, jnp.where(top_lane == 65, factor, turned[OBS : OBS + 8, :])
    )


def place(tile, size):
    return tile if size & (size - 1) else jnp.bitwise_xor(lax.axis_index("gx"), tile)


def block_rows(ref, start, tile, size, rows=EDGE):
    return ref[pl.ds(pl.multiple_of(place(tile, size) * BLOCK + start, 8), rows), :]


def side_columns(ref, tile, size):
    west, east = jnp.maximum(tile - 1, 0), jnp.minimum(tile + 1, size - 1)
    west_meta, east_meta = block_rows(ref, 0, west, size), block_rows(ref, 0, east, size)
    west_mid = block_rows(ref, RIGHT_MID, west, size) + west_meta[:, 81:82] * block_rows(ref, LEFT, tile, size)
    east_mid = block_rows(ref, LEFT_MID, east, size) + east_meta[:, 80:81] * block_rows(ref, RIGHT, tile, size)
    return block_rows(ref, RIGHT, west, size), west_mid, block_rows(ref, LEFT, east, size), east_mid


def complete(members, n_obs, size, blocks_ref, out_ref):
    lane = lanes((n_obs, 128))
    for tile in range(size):
        west, west_mid, east, east_mid = side_columns(blocks_ref, jnp.int32(tile), size)
        meta = block_rows(blocks_ref, 0, jnp.int32(tile), size)
        block = block_rows(blocks_ref, OBS, jnp.int32(tile), size, 8)[:n_obs]
        added = []
        for j in range(n_obs):
            terms = (
                meta[:, 64 + j : 65 + j] * west
                + meta[:, 68 + j : 69 + j] * east
                + meta[:, 72 + j : 73 + j] * west_mid
                + meta[:, 76 + j : 77 + j] * east_mid
            )
            added.append(jnp.sum(terms, axis=0, keepdims=True))
        at = jnp.where(lane < members, block + jnp.concatenate(added, axis=0), 0.0)
        mean = jnp.sum(at, axis=1, keepdims=True) * (1.0 / members)
        raw = jnp.where(lane < members, at - mean, jnp.where(lane == members, block[:, 64:65] - mean, 0.0))
        out_ref[n_obs * tile : n_obs * (tile + 1), :] = raw * block[:, 65:66]


def forecast(members, count, size, field_ref, flow_ref, even_ref, odd_ref, blocks_ref, out_ref, tall_ref):
    north, south = halo_rows(even_ref, odd_ref, members)
    tile = lax.axis_index("gx")
    west, west_mid, east, east_mid = side_columns(blocks_ref, tile, size)
    sides = jnp.concatenate(
        [jnp.where(tile > 0, x, 0.0) for x in (west, west_mid)]
        + [jnp.where(tile < size - 1, x, 0.0) for x in (east, east_mid)],
        axis=0,
    )
    sides = transposed(sides)[:members]
    field = [north[1], north[0]]
    field += [field_ref[r * members : (r + 1) * members, :] for r in range(count)] + [south[0], south[1]]
    tall = tall_coefficients(tall_ref, flow_ref, north[2], south[2], count)
    lane = lanes((members, 128))

    def step(rows, i, start):
        w = jnp.where(lane == 0, shifted(sides, -(start + i)), shifted(rows[i], 1))
        e = jnp.where(lane == 127, shifted(sides, 127 - (start + 2 * EDGE + i)), shifted(rows[i], -1))
        return combine([c[i : i + 1, :] for c in tall], rows[i], rows[i - 1], rows[i + 1], w, e)

    middle = {i: step(field, i, 0) for i in range(1, count + 3)}
    for r in range(count):
        out_ref[r * members : (r + 1) * members, :] = step(middle, r + 2, EDGE)


def analyse(members, count, f_ref, obs_ref, out_ref):
    scaled = obs_ref[...]
    full = lax.dot_general(
        scaled, scaled, (((0,), (0,)), ((), ())), precision=HIGHEST, preferred_element_type=F32
    )
    lane, sub = lanes((members, 128)), rows_of((members, 128))
    a = full[:members, :] + jnp.where(lane == sub, members - 1.0, 0.0)
    for j in range(members):
        row = a[j : j + 1, :]
        column = a[:, j : j + 1]
        below = sub > j
        factor = jnp.where(below, column * (1.0 / row[:, j : j + 1]), 0.0)
        unit = jnp.where(lane[:1] == j, 1.0, row)
        a = jnp.where(below & (lane == j), 0.0, a) - factor * unit
    diagonal = jnp.sum(jnp.where(lane == sub, a, 0.0), axis=1, keepdims=True)
    scale = lax.rsqrt(diagonal)
    inverse = scale * jnp.where(lane < sub, a, jnp.where(lane == sub, 1.0, 0.0))
    reduced = scale * a[:, members : members + 1]
    weights = jnp.sum(reduced * inverse, axis=0, keepdims=True)
    transform = jnp.sqrt(members - 1.0) * inverse + weights
    share = (1.0 - jnp.sum(jnp.where(lane < members, transform, 0.0), axis=1, keepdims=True)) * (1.0 / members)
    transform = (transform + share)[:, :members]
    for r in range(count):
        out_ref[pl.ds(r, members, stride=count), :] = jnp.dot(
            transform, f_ref[r * members : (r + 1) * members, :], precision=HIGHEST, preferred_element_type=F32
        )


def swap(x, axis, offset):
    pairs = [(i, i + 1) for i in range(offset, lax.axis_size(axis) - 1, 2)]
    return lax.ppermute(x, axis, pairs + [(b, a) for a, b in pairs])


def gathered(x, axis):
    size = lax.axis_size(axis)
    if size & (size - 1):
        return lax.all_gather(x, axis, tiled=True)
    step = 1
    while step < size:
        other = lax.ppermute(x, axis, [(i, i ^ step) for i in range(size)])
        x = jnp.concatenate([x, other], axis=0)
        step *= 2
    return x


def body(ensemble, flow, obs_cell, obs_value, obs_var):
    members, count, width = ensemble.shape
    n_obs = obs_cell.shape[-1]
    size = lax.axis_size("gx")
    call = functools.partial(pl.pallas_call, compiler_params=PARAMS)

    def shape(*dims):
        return jax.ShapeDtypeStruct(dims + (width,), F32)

    field, tile_flow, obs, rows_even, rows_odd = call(
        functools.partial(load, members, count, n_obs),
        out_shape=[shape(members * count), shape(3, count), shape(24)] + [shape(2 * members + 8)] * 2,
        in_specs=[ANY] * 5,
        out_specs=[VMEM] * 5,
        scratch_shapes=[pltpu.SMEM((n_obs,), jnp.int32)]
        + [pltpu.SMEM((n_obs,), F32)] * 2
        + [pltpu.SemaphoreType.DMA((count + 4,))],
        name="load",
    )(ensemble, flow, obs_cell.reshape(-1), obs_value.reshape(-1), obs_var.reshape(-1))
    rows_odd = swap(rows_odd, "gy", 1)
    rows_even = swap(rows_even, "gy", 0)
    tall = pltpu.VMEM((3, EDGE, width), F32)
    block = call(
        functools.partial(observe, members, count, n_obs),
        out_shape=shape(BLOCK),
        in_specs=[VMEM] * 5,
        out_specs=VMEM,
        scratch_shapes=[tall],
        name="observe",
    )(field, tile_flow, obs, rows_even, rows_odd)
    blocks = gathered(block, "gx")
    packet = call(
        functools.partial(complete, members, n_obs, size),
        out_shape=shape(n_obs * size),
        in_specs=[VMEM],
        out_specs=VMEM,
        name="complete",
    )(blocks)
    predicted = call(
        functools.partial(forecast, members, count, size),
        out_shape=shape(members * count),
        in_specs=[VMEM] * 5,
        out_specs=VMEM,
        scratch_shapes=[tall],
        cost_estimate=pl.CostEstimate(flops=4 * 10**6, bytes_accessed=6 * 10**5, transcendentals=0),
        name="forecast",
    )(field, tile_flow, rows_even, rows_odd, blocks)
    scaled = gathered(packet, "gy")
    out = call(
        functools.partial(analyse, members, count),
        out_shape=shape(members * count),
        in_specs=[VMEM] * 2,
        out_specs=VMEM,
        name="analyse",
    )(predicted, scaled)
    return out.reshape(ensemble.shape)


def solution(mesh):
    return jax.shard_map(
        body,
        mesh=mesh,
        in_specs=(
            P(None, "gy", "gx"),
            P(None, "gy", "gx"),
            P("gy", "gx", None),
            P("gy", "gx", None),
            P("gy", "gx", None),
        ),
        out_specs=P(None, "gy", "gx"),
        check_vma=False,
    )
```

```python
import functools

import jax
import jax.numpy as jnp
from jax import lax
from jax.experimental import pallas as pl
from jax.experimental.pallas import tpu as pltpu
from jax.sharding import PartitionSpec as P

F32 = jnp.float32
HIGHEST = lax.Precision.HIGHEST
PARAMS = pltpu.CompilerParams(vmem_limit_bytes=24 * 1024 * 1024)
VMEM = pl.BlockSpec(memory_space=pltpu.VMEM)
SMEM = pl.BlockSpec(memory_space=pltpu.SMEM)


def lanes(shape):
    return lax.broadcasted_iota(jnp.int32, shape, len(shape) - 1)


def rows_of(shape):
    return lax.broadcasted_iota(jnp.int32, shape, len(shape) - 2)


def shifted(x, amount):
    return pltpu.roll(x, amount % x.shape[-1], x.ndim - 1)


EDGE = 16
BLOCK = 4 * EDGE + 8
LEFT, RIGHT, LEFT_MID, RIGHT_MID, OBS = 0, EDGE, 2 * EDGE, 3 * EDGE, 4 * EDGE
HBM = pl.BlockSpec(memory_space=pltpu.HBM)


def coefficients(k, u, v):
    return 1.0 - 4.0 * k, k + 0.5 * v, k - 0.5 * v, k + 0.5 * u, k - 0.5 * u


def combine(c, own, north, south, west, east):
    return c[0] * own + c[1] * north + c[2] * south + c[3] * west + c[4] * east


def transposed(x):
    return jnp.concatenate([x, jnp.zeros((128 - x.shape[0], 128), F32)], axis=0).T


def load(
    members, count, n_obs, ens_hbm, flow_hbm, cell_hbm, value_hbm, var_hbm,
    field_ref, flow_ref, obs_ref, even_ref, odd_ref, cell_ref, value_ref, var_ref, sems,
):
    order = [0, count - 1, 1, count - 2] + list(range(2, count - 2))
    copies = [pltpu.make_async_copy(flow_hbm, flow_ref, sems.at[count])]
    copies += [
        pltpu.make_async_copy(ens_hbm.at[:, r, :], field_ref.at[pl.ds(r * members, members), :], sems.at[r]) for r in order
    ]
    small = [
        pltpu.make_async_copy(src, dst, sems.at[count + 1 + i])
        for i, (src, dst) in enumerate(((cell_hbm, cell_ref), (value_hbm, value_ref), (var_hbm, var_ref)))
    ]
    for copy in copies + small:
        copy.start()
    for copy in copies + small:
        copy.wait()
    is_even = lax.axis_index("gy") % 2 == 0

    def grid_row(r):
        return field_ref[r * members : (r + 1) * members, :]

    top, bottom = [(grid_row(a), grid_row(b), flow_ref[:, a, :]) for a, b in ((0, 1), (count - 1, count - 2))]
    for ref, first in ((even_ref, is_even), (odd_ref, jnp.logical_not(is_even))):
        near, second, flow = [jnp.where(first, low, high) for low, high in zip(bottom, top)]
        ref[0:members, :] = near
        ref[members : 2 * members, :] = second
        ref[2 * members : 2 * members + 3, :] = flow
        ref[2 * members + 3 :, :] = jnp.zeros((5, 128), F32)
    sub = rows_of((8, 128))
    for i, (ref, rest) in enumerate(((cell_ref, 0.0), (value_ref, 0.0), (var_ref, 1.0))):
        block = jnp.full((8, 128), rest, F32)
        for j in range(n_obs):
            block = jnp.where(sub == j, ref[j].astype(F32), block)
        obs_ref[8 * i : 8 * i + 8, :] = block


def halo_rows(even_ref, odd_ref, members):
    is_even = lax.axis_index("gy") % 2 == 0
    parts = []
    for lo, hi in ((0, members), (members, 2 * members), (2 * members, 2 * members + 3)):
        e, o = even_ref[lo:hi, :], odd_ref[lo:hi, :]
        parts.append((jnp.where(is_even, o, e), jnp.where(is_even, e, o)))
    return tuple(p[0] for p in parts), tuple(p[1] for p in parts)


def tall_coefficients(scratch, flow_ref, north_flow, south_flow, count):
    for k in range(3):
        scratch[k] = jnp.zeros((EDGE, 128), F32)
        scratch[k, 1:2, :] = north_flow[k : k + 1]
        scratch[k, 2 : 2 + count, :] = flow_ref[k]
        scratch[k, 2 + count : 3 + count, :] = south_flow[k : k + 1]
    return coefficients(*[scratch[k] for k in range(3)])


def observe(members, count, n_obs, field_ref, flow_ref, obs_ref, odd_ref, even_ref, out_ref, tall_ref):
    north, south = halo_rows(even_ref, odd_ref, members)
    field = [north[1], north[0]]
    field += [field_ref[r * members : (r + 1) * members, :] for r in range(count)] + [south[0], south[1]]
    coeffs = tall_coefficients(tall_ref, flow_ref, north[2], south[2], count)
    lane, sub = lanes((EDGE, 128)), rows_of((EDGE, 128))
    wide = lanes((members, 128))
    own, up, down, left, right = coeffs
    has_west = lax.axis_index("gx") > 0
    has_east = lax.axis_index("gx") < lax.axis_size("gx") - 1
    zero = jnp.zeros((EDGE, 128), F32)

    def spread(w):
        to_west, to_east = left * w, right * w
        inside = (
            own * w
            + pltpu.roll(up * w, EDGE - 1, 0)
            + pltpu.roll(down * w, 1, 0)
            + jnp.where(lane == 127, 0.0, shifted(to_west, -1))
            + jnp.where(lane == 0, 0.0, shifted(to_east, 1))
        )
        return inside, jnp.where(has_west, to_west[:, 0:1], 0.0), jnp.where(has_east, to_east[:, 127:128], 0.0)

    packed = jnp.zeros((members, 128), F32)
    second = jnp.zeros((members, 128), F32)
    for i in range(1, count + 3):
        x = field[i]
        packed = jnp.where(wide == i, shifted(x, i), packed)
        packed = jnp.where(wide == EDGE + i, shifted(x, EDGE + i - 127), packed)
        if 2 <= i < count + 2:
            second = jnp.where(wide == i, shifted(x, i - 1), second)
            second = jnp.where(wide == EDGE + i, shifted(x, EDGE + i - 126), second)

    def edge_row(low, high):
        both = jnp.where(lane == sub, low[:, 0:1], jnp.where(lane == sub + EDGE, high[:, 127:128], 0.0))
        return jnp.sum(both, axis=0, keepdims=True)

    middle = (
        edge_row(own, own) * packed
        + edge_row(up, up) * shifted(packed, 1)
        + edge_row(down, down) * shifted(packed, -1)
        + edge_row(right, left) * second
    )
    packed = jnp.where(wide < 2 * EDGE, packed, jnp.where(wide < 4 * EDGE, shifted(middle, 2 * EDGE), 0.0))
    meta = jnp.where(lane == 80, left[:, 0:1], jnp.where(lane == 81, right[:, 127:128], zero))
    position = ((sub - 2) * 128 + lane).astype(F32)
    inner = (sub >= 2) & (sub < 2 + count)
    for j in range(n_obs):
        here = jnp.where(inner & (position == obs_ref[j : j + 1, :]), 1.0, 0.0)
        w, mid_west, mid_east = spread(here)
        w, west, east = spread(w)
        total = w[0:1, :] * field[0]
        for i in range(1, count + 4):
            total = total + w[i : i + 1, :] * field[i]
        packed = jnp.where(wide == OBS + j, jnp.sum(total, axis=1, keepdims=True), packed)
        for at, column in ((64, west), (68, east), (72, mid_west), (76, mid_east)):
            meta = jnp.where(lane == at + j, column, meta)
    turned = transposed(packed)
    out_ref[0:EDGE, :] = turned[0:EDGE, :] + meta
    out_ref[EDGE:OBS, :] = turned[EDGE:OBS, :]
    top_lane = lanes((8, 128))
    value, factor = obs_ref[8:16, :], lax.rsqrt(obs_ref[16:24, :])
    out_ref[OBS : OBS + 8, :] = jnp.where(
        top_lane == 64, value, jnp.where(top_lane == 65, factor, turned[OBS : OBS + 8, :])
    )


def place(tile, size):
    return tile if size & (size - 1) else jnp.bitwise_xor(lax.axis_index("gx"), tile)


def block_rows(ref, start, tile, size, rows=EDGE):
    return ref[pl.ds(pl.multiple_of(place(tile, size) * BLOCK + start, 8), rows), :]


def side_columns(ref, tile, size):
    west, east = jnp.maximum(tile - 1, 0), jnp.minimum(tile + 1, size - 1)
    west_meta, east_meta = block_rows(ref, 0, west, size), block_rows(ref, 0, east, size)
    west_mid = block_rows(ref, RIGHT_MID, west, size) + west_meta[:, 81:82] * block_rows(ref, LEFT, tile, size)
    east_mid = block_rows(ref, LEFT_MID, east, size) + east_meta[:, 80:81] * block_rows(ref, RIGHT, tile, size)
    return block_rows(ref, RIGHT, west, size), west_mid, block_rows(ref, LEFT, east, size), east_mid


def complete(members, n_obs, size, blocks_ref, out_ref):
    lane = lanes((n_obs, 128))
    for tile in range(size):
        west, west_mid, east, east_mid = side_columns(blocks_ref, jnp.int32(tile), size)
        meta = block_rows(blocks_ref, 0, jnp.int32(tile), size)
        block = block_rows(blocks_ref, OBS, jnp.int32(tile), size, 8)[:n_obs]
        added = []
        for j in range(n_obs):
            terms = (
                meta[:, 64 + j : 65 + j] * west
                + meta[:, 68 + j : 69 + j] * east
                + meta[:, 72 + j : 73 + j] * west_mid
                + meta[:, 76 + j : 77 + j] * east_mid
            )
            added.append(jnp.sum(terms, axis=0, keepdims=True))
        at = jnp.where(lane < members, block + jnp.concatenate(added, axis=0), 0.0)
        mean = jnp.sum(at, axis=1, keepdims=True) * (1.0 / members)
        raw = jnp.where(lane < members, at - mean, jnp.where(lane == members, block[:, 64:65] - mean, 0.0))
        out_ref[n_obs * tile : n_obs * (tile + 1), :] = raw * block[:, 65:66]


def forecast(members, count, size, field_ref, flow_ref, odd_ref, even_ref, blocks_ref, out_ref, tall_ref):
    north, south = halo_rows(even_ref, odd_ref, members)
    tile = lax.axis_index("gx")
    west, west_mid, east, east_mid = side_columns(blocks_ref, tile, size)
    sides = jnp.concatenate(
        [jnp.where(tile > 0, x, 0.0) for x in (west, west_mid)]
        + [jnp.where(tile < size - 1, x, 0.0) for x in (east, east_mid)],
        axis=0,
    )
    sides = transposed(sides)[:members]
    field = [north[1], north[0]]
    field += [field_ref[r * members : (r + 1) * members, :] for r in range(count)] + [south[0], south[1]]
    tall = tall_coefficients(tall_ref, flow_ref, north[2], south[2], count)
    lane = lanes((members, 128))

    def step(rows, i, start):
        w = jnp.where(lane == 0, shifted(sides, -(start + i)), shifted(rows[i], 1))
        e = jnp.where(lane == 127, shifted(sides, 127 - (start + 2 * EDGE + i)), shifted(rows[i], -1))
        return combine([c[i : i + 1, :] for c in tall], rows[i], rows[i - 1], rows[i + 1], w, e)

    middle = {i: step(field, i, 0) for i in range(1, count + 3)}
    for r in range(count):
        out_ref[r * members : (r + 1) * members, :] = step(middle, r + 2, EDGE)


def eliminated(a, members):
    size = 8
    lane, sub = lanes((size, 128)), rows_of((size, 128))
    part = [a[size * q : size * (q + 1), :] for q in range(members // size)]
    for p in range(len(part)):
        column = {
            (q, j): jnp.broadcast_to(part[q][:, size * p + j : size * p + j + 1], (size, 128))
            for q in range(p, len(part))
            for j in range(size)
        }
        for j in range(size):
            at = size * p + j
            inverse = 1.0 / column[p, j][j : j + 1, :]
            unit = jnp.where(lane[:1] == at, 1.0, part[p][j : j + 1, :])
            pivots = [column[p, k][j : j + 1, :] for k in range(j + 1, size)]
            for q in range(p, len(part)):
                factor = column[q, j] * inverse
                if q == p:
                    factor = jnp.where(sub > j, factor, 0.0)
                for k in range(j + 1, size):
                    column[q, k] = column[q, k] - factor * pivots[k - j - 1]
                cleared = (lane == at) & (sub > j) if q == p else lane == at
                part[q] = jnp.where(cleared, 0.0, part[q]) - factor * unit
    return jnp.concatenate(part, axis=0)


def analyse(members, count, f_ref, obs_ref, out_ref):
    scaled = obs_ref[...]
    full = lax.dot_general(
        scaled, scaled, (((0,), (0,)), ((), ())), precision=HIGHEST, preferred_element_type=F32
    )
    lane, sub = lanes((members, 128)), rows_of((members, 128))
    a = full[:members, :] + jnp.where(lane == sub, members - 1.0, 0.0)
    a = eliminated(a, members)
    diagonal = jnp.sum(jnp.where(lane == sub, a, 0.0), axis=1, keepdims=True)
    scale = lax.rsqrt(diagonal)
    inverse = scale * jnp.where(lane < sub, a, jnp.where(lane == sub, 1.0, 0.0))
    reduced = scale * a[:, members : members + 1]
    weights = jnp.sum(reduced * inverse, axis=0, keepdims=True)
    transform = jnp.sqrt(members - 1.0) * inverse + weights
    share = (1.0 - jnp.sum(jnp.where(lane < members, transform, 0.0), axis=1, keepdims=True)) * (1.0 / members)
    transform = (transform + share)[:, :members]
    for r in range(count):
        out_ref[pl.ds(r, members, stride=count), :] = jnp.dot(
            transform, f_ref[r * members : (r + 1) * members, :], precision=HIGHEST, preferred_element_type=F32
        )


def swap(x, axis, offset):
    pairs = [(i, i + 1) for i in range(offset, lax.axis_size(axis) - 1, 2)]
    return lax.ppermute(x, axis, pairs + [(b, a) for a, b in pairs])


def gathered(x, axis):
    size = lax.axis_size(axis)
    if size & (size - 1):
        return lax.all_gather(x, axis, tiled=True)
    step = 1
    while step < size:
        other = lax.ppermute(x, axis, [(i, i ^ step) for i in range(size)])
        x = jnp.concatenate([x, other], axis=0)
        step *= 2
    return x


def body(ensemble, flow, obs_cell, obs_value, obs_var):
    members, count, width = ensemble.shape
    n_obs = obs_cell.shape[-1]
    size = lax.axis_size("gx")
    call = functools.partial(pl.pallas_call, compiler_params=PARAMS)

    def shape(*dims):
        return jax.ShapeDtypeStruct(dims + (width,), F32)

    field, tile_flow, obs, rows_even, rows_odd = pl.pallas_call(
        functools.partial(load, members, count, n_obs),
        compiler_params=PARAMS,
        out_shape=[shape(members * count), shape(3, count), shape(24)] + [shape(2 * members + 8)] * 2,
        in_specs=[HBM] * 5,
        out_specs=[VMEM] * 5,
        scratch_shapes=[pltpu.SMEM((n_obs,), jnp.int32)]
        + [pltpu.SMEM((n_obs,), F32)] * 2
        + [pltpu.SemaphoreType.DMA((count + 4,))],
        name="load",
    )(*[
        pltpu.with_memory_space_constraint(x, pltpu.HBM)
        for x in (ensemble, flow, obs_cell.reshape(-1), obs_value.reshape(-1), obs_var.reshape(-1))
    ])
    rows_odd = swap(rows_odd, "gy", 1)
    rows_even = swap(rows_even, "gy", 0)
    tall = pltpu.VMEM((3, EDGE, width), F32)
    block = call(
        functools.partial(observe, members, count, n_obs),
        out_shape=shape(BLOCK),
        in_specs=[VMEM] * 5,
        out_specs=VMEM,
        scratch_shapes=[tall],
        name="observe",
    )(field, tile_flow, obs, rows_odd, rows_even)
    blocks = gathered(block, "gx")
    packet = call(
        functools.partial(complete, members, n_obs, size),
        out_shape=shape(n_obs * size),
        in_specs=[VMEM],
        out_specs=VMEM,
        name="complete",
    )(blocks)
    predicted = call(
        functools.partial(forecast, members, count, size),
        out_shape=shape(members * count),
        in_specs=[VMEM] * 5,
        out_specs=VMEM,
        scratch_shapes=[tall],
        cost_estimate=pl.CostEstimate(flops=4 * 10**6, bytes_accessed=6 * 10**5, transcendentals=0),
        name="forecast",
    )(field, tile_flow, rows_odd, rows_even, blocks)
    scaled = gathered(packet, "gy")
    out = call(
        functools.partial(analyse, members, count),
        out_shape=shape(members * count),
        in_specs=[VMEM] * 2,
        out_specs=VMEM,
        name="analyse",
    )(predicted, scaled)
    return out.reshape(ensemble.shape)


def solution(mesh):
    return jax.shard_map(
        body,
        mesh=mesh,
        in_specs=(
            P(None, "gy", "gx"),
            P(None, "gy", "gx"),
            P("gy", "gx", None),
            P("gy", "gx", None),
            P("gy", "gx", None),
        ),
        out_specs=P(None, "gy", "gx"),
        check_vma=False,
    )
```

```python
import functools

import jax
import jax.numpy as jnp
from jax import lax
from jax.experimental import pallas as pl
from jax.experimental.pallas import tpu as pltpu
from jax.sharding import PartitionSpec as P

F32 = jnp.float32
HIGHEST = lax.Precision.HIGHEST
PARAMS = pltpu.CompilerParams(vmem_limit_bytes=24 * 1024 * 1024)
VMEM = pl.BlockSpec(memory_space=pltpu.VMEM)
SMEM = pl.BlockSpec(memory_space=pltpu.SMEM)


def lanes(shape):
    return lax.broadcasted_iota(jnp.int32, shape, len(shape) - 1)


def rows_of(shape):
    return lax.broadcasted_iota(jnp.int32, shape, len(shape) - 2)


def shifted(x, amount):
    return pltpu.roll(x, amount % x.shape[-1], x.ndim - 1)


EDGE = 16
BLOCK = EDGE + 16
MID, OBS = EDGE, EDGE + 8
VALUE, FACTOR, TO_WEST, TO_EAST, WEIGHTS = 64, 65, 66, 67, 72
HBM = pl.BlockSpec(memory_space=pltpu.HBM)
ANY = pl.BlockSpec(memory_space=pl.ANY)


def coefficients(k, u, v):
    return 1.0 - 4.0 * k, k + 0.5 * v, k - 0.5 * v, k + 0.5 * u, k - 0.5 * u


def combine(c, own, north, south, west, east):
    return c[0] * own + c[1] * north + c[2] * south + c[3] * west + c[4] * east


def transposed(x):
    return jnp.concatenate([x, jnp.zeros((128 - x.shape[0], 128), F32)], axis=0).T


def load(
    members, count, n_obs, ens_hbm, flow_hbm, cell_hbm, value_hbm, var_hbm,
    field_ref, flow_ref, obs_ref, even_ref, odd_ref, cell_ref, value_ref, var_ref, sems,
):
    order = [0, count - 1, 1, count - 2] + list(range(2, count - 2))
    copies = [pltpu.make_async_copy(flow_hbm, flow_ref, sems.at[count])]
    copies += [
        pltpu.make_async_copy(ens_hbm.at[:, r, :], field_ref.at[pl.ds(r * members, members), :], sems.at[r]) for r in order
    ]
    small = [
        pltpu.make_async_copy(src, dst, sems.at[count + 1 + i])
        for i, (src, dst) in enumerate(((cell_hbm, cell_ref), (value_hbm, value_ref), (var_hbm, var_ref)))
    ]
    for copy in copies + small:
        copy.start()
    for copy in copies + small:
        copy.wait()
    is_even = lax.axis_index("gy") % 2 == 0

    def grid_row(r):
        return field_ref[r * members : (r + 1) * members, :]

    top, bottom = [(grid_row(a), grid_row(b), flow_ref[:, a, :]) for a, b in ((0, 1), (count - 1, count - 2))]
    for ref, first in ((even_ref, is_even), (odd_ref, jnp.logical_not(is_even))):
        near, second, flow = [jnp.where(first, low, high) for low, high in zip(bottom, top)]
        ref[0:members, :] = near
        ref[members : 2 * members, :] = second
        ref[2 * members : 2 * members + 3, :] = flow
        ref[2 * members + 3 :, :] = jnp.zeros((5, 128), F32)
    sub = rows_of((8, 128))
    for i, (ref, rest) in enumerate(((cell_ref, 0.0), (value_ref, 0.0), (var_ref, 1.0))):
        block = jnp.full((8, 128), rest, F32)
        for j in range(n_obs):
            block = jnp.where(sub == j, ref[j].astype(F32), block)
        obs_ref[8 * i : 8 * i + 8, :] = block


def halo_rows(even_ref, odd_ref, members):
    is_even = lax.axis_index("gy") % 2 == 0
    parts = []
    for lo, hi in ((0, members), (members, 2 * members), (2 * members, 2 * members + 3)):
        e, o = even_ref[lo:hi, :], odd_ref[lo:hi, :]
        parts.append((jnp.where(is_even, o, e), jnp.where(is_even, e, o)))
    return tuple(p[0] for p in parts), tuple(p[1] for p in parts)


def tall_coefficients(scratch, flow_ref, north_flow, south_flow, count):
    for k in range(3):
        scratch[k, 0:count, :] = flow_ref[k]
        scratch[k, count:, :] = jnp.zeros((EDGE - count, 128), F32)
        scratch[k, count : count + 1, :] = south_flow[k : k + 1]
        scratch[k, EDGE - 1 : EDGE, :] = north_flow[k : k + 1]
    return coefficients(*[scratch[k] for k in range(3)])


def tall_field(field_ref, north, south, members, count):
    field = {-2: north[1], -1: north[0], count: south[0], count + 1: south[1]}
    field.update({r: field_ref[r * members : (r + 1) * members, :] for r in range(count)})
    return field


def observe(members, count, n_obs, field_ref, flow_ref, obs_ref, odd_ref, even_ref, out_ref, tall_ref):
    north, south = halo_rows(even_ref, odd_ref, members)
    field = tall_field(field_ref, north, south, members, count)
    own, up, down, left, right = tall_coefficients(tall_ref, flow_ref, north[2], south[2], count)
    lane, sub = lanes((EDGE, 128)), rows_of((EDGE, 128))
    wide = lanes((members, 128))
    has_west = lax.axis_index("gx") > 0
    has_east = lax.axis_index("gx") < lax.axis_size("gx") - 1

    def spread(w):
        to_west, to_east = left * w, right * w
        inside = (
            own * w
            + pltpu.roll(up * w, EDGE - 1, 0)
            + pltpu.roll(down * w, 1, 0)
            + jnp.where(lane == 127, 0.0, shifted(to_west, -1))
            + jnp.where(lane == 0, 0.0, shifted(to_east, 1))
        )
        return inside, jnp.where(has_west, to_west[:, 0:1], 0.0), jnp.where(has_east, to_east[:, 127:128], 0.0)

    packed = jnp.zeros((members, 128), F32)
    second = jnp.zeros((members, 128), F32)
    for r in range(-1, count + 1):
        x, at = field[r], r % EDGE
        packed = jnp.where(wide == at, shifted(x, at), packed)
        packed = jnp.where(wide == EDGE + at, shifted(x, EDGE + at - 127), packed)
        if 0 <= r < count:
            second = jnp.where(wide == at, shifted(x, at - 1), second)
            second = jnp.where(wide == EDGE + at, shifted(x, EDGE + at - 126), second)

    def edge_row(low, high):
        both = jnp.where(lane == sub, low[:, 0:1], jnp.where(lane == sub + EDGE, high[:, 127:128], 0.0))
        return jnp.sum(both, axis=0, keepdims=True)

    middle = (
        edge_row(own, own) * packed
        + edge_row(up, up) * jnp.where(wide % EDGE == 0, shifted(packed, 1 - EDGE), shifted(packed, 1))
        + edge_row(down, down) * shifted(packed, -1)
        + edge_row(right, left) * second
    )
    packed = jnp.where(wide < 2 * EDGE, packed, 0.0)
    packed = jnp.where((wide >= 32) & (wide < 40), shifted(middle, 32), packed)
    packed = jnp.where((wide >= 40) & (wide < 48), shifted(middle, 24), packed)
    top_lane = lane[:8]
    meta = jnp.where(top_lane == VALUE, obs_ref[8:16, :], 0.0)
    meta = jnp.where(top_lane == FACTOR, lax.rsqrt(obs_ref[16:24, :]), meta)
    meta = jnp.where(top_lane == TO_WEST, left[:8, 0:1], meta)
    meta = jnp.where(top_lane == TO_EAST, right[:8, 127:128], meta)
    position = (sub * 128 + lane).astype(F32)
    for j in range(n_obs):
        here = jnp.where((sub < count) & (position == obs_ref[j : j + 1, :]), 1.0, 0.0)
        w, mid_west, mid_east = spread(here)
        w, west, east = spread(w)
        total = w[EDGE - 2 : EDGE - 1, :] * field[-2]
        for r in range(-1, count + 2):
            total = total + w[r % EDGE : r % EDGE + 1, :] * field[r]
        packed = jnp.where(wide == 48 + j, jnp.sum(total, axis=1, keepdims=True), packed)
        for k, column in enumerate((west[:8], west[8:], east[:8], east[8:], mid_west[:8], mid_east[:8])):
            meta = jnp.where(top_lane == WEIGHTS + k * n_obs + j, column, meta)
    turned = jnp.concatenate([packed, jnp.zeros((128 - members, 128), F32)], axis=0).T
    out_ref[0:EDGE, :] = turned[0:EDGE] + shifted(turned[EDGE : 2 * EDGE], 64)
    out_ref[MID : MID + 8, :] = turned[32:40] + shifted(turned[40:48], 64)
    out_ref[OBS : OBS + 8, :] = turned[48:56] + meta


def block_rows(ref, start, tile, size, rows):
    place = tile if size & (size - 1) else jnp.bitwise_xor(lax.axis_index("gx") | 1, tile)
    return ref[pl.ds(pl.multiple_of(place * BLOCK + start, 8), rows), :]


def side_columns(ref, tile, size):
    west, east = jnp.maximum(tile - 1, 0), jnp.minimum(tile + 1, size - 1)
    own = block_rows(ref, 0, tile, size, EDGE)
    west_x = shifted(block_rows(ref, 0, west, size, EDGE), 64)
    east_x = block_rows(ref, 0, east, size, EDGE)
    west_mid = shifted(block_rows(ref, MID, west, size, 8), 64)
    west_mid += block_rows(ref, OBS, west, size, 8)[:, TO_EAST : TO_EAST + 1] * own[:8]
    east_mid = block_rows(ref, MID, east, size, 8)
    east_mid += block_rows(ref, OBS, east, size, 8)[:, TO_WEST : TO_WEST + 1] * shifted(own[:8], 64)
    return west_x, east_x, west_mid, east_mid


def complete(members, n_obs, size, blocks_ref, out_ref):
    lane = lanes((n_obs, 128))
    for tile in range(size):
        west, east, west_mid, east_mid = side_columns(blocks_ref, jnp.int32(tile), size)
        block = block_rows(blocks_ref, OBS, jnp.int32(tile), size, 8)
        terms = (west[:8], west[8:], east[:8], east[8:], west_mid, east_mid)
        added = []
        for j in range(n_obs):
            at = [WEIGHTS + k * n_obs + j for k in range(len(terms))]
            total = sum(block[:, a : a + 1] * term for a, term in zip(at, terms))
            added.append(jnp.sum(total, axis=0, keepdims=True))
        block = block[:n_obs]
        at = jnp.where(lane < members, block + jnp.concatenate(added, axis=0), 0.0)
        mean = jnp.sum(at, axis=1, keepdims=True) * (1.0 / members)
        raw = jnp.where(lane < members, at - mean, jnp.where(lane == members, block[:, VALUE : VALUE + 1] - mean, 0.0))
        out_ref[n_obs * tile : n_obs * (tile + 1), :] = raw * block[:, FACTOR : FACTOR + 1]


def forecast(members, count, size, field_ref, flow_ref, odd_ref, even_ref, blocks_ref, out_ref, tall_ref):
    north, south = halo_rows(even_ref, odd_ref, members)
    tile = lax.axis_index("gx")
    west, east, west_mid, east_mid = side_columns(blocks_ref, tile, size)
    has_west, has_east = tile > 0, tile < size - 1
    sides = [jnp.where(has_west, west, 0.0), jnp.where(has_east, east, 0.0)]
    sides += [jnp.where(has_west, west_mid, 0.0), jnp.where(has_east, east_mid, 0.0), jnp.zeros((80, 128), F32)]
    sides = jnp.concatenate(sides, axis=0).T[:members]
    field = tall_field(field_ref, north, south, members, count)
    tall = tall_coefficients(tall_ref, flow_ref, north[2], south[2], count)
    lane = lanes((members, 128))

    def step(rows, r, west_at, east_at):
        w = jnp.where(lane == 0, shifted(sides, -west_at), shifted(rows[r], 1))
        e = jnp.where(lane == 127, shifted(sides, 127 - east_at), shifted(rows[r], -1))
        at = r % EDGE
        return combine([c[at : at + 1, :] for c in tall], rows[r], rows[r - 1], rows[r + 1], w, e)

    middle = {r: step(field, r, r % EDGE, EDGE + r % EDGE) for r in range(-1, count + 1)}
    for r in range(count):
        out_ref[r * members : (r + 1) * members, :] = step(middle, r, 2 * EDGE + r, 2 * EDGE + 8 + r)


def eliminated(a, members):
    size = 8
    lane, sub = lanes((size, 128)), rows_of((size, 128))
    part = [a[size * q : size * (q + 1), :] for q in range(members // size)]
    for p in range(len(part)):
        column = {
            (q, j): jnp.broadcast_to(part[q][:, size * p + j : size * p + j + 1], (size, 128))
            for q in range(p, len(part))
            for j in range(size)
        }
        for j in range(size):
            at = size * p + j
            inverse = 1.0 / column[p, j][j : j + 1, :]
            unit = jnp.where(lane[:1] == at, 1.0, part[p][j : j + 1, :])
            pivots = [column[p, k][j : j + 1, :] for k in range(j + 1, size)]
            for q in range(p, len(part)):
                factor = column[q, j] * inverse
                if q == p:
                    factor = jnp.where(sub > j, factor, 0.0)
                for k in range(j + 1, size):
                    column[q, k] = column[q, k] - factor * pivots[k - j - 1]
                cleared = (lane == at) & (sub > j) if q == p else lane == at
                part[q] = jnp.where(cleared, 0.0, part[q]) - factor * unit
    return jnp.concatenate(part, axis=0)


def analyse(members, count, f_ref, obs_ref, even_obs_ref, out_ref):
    scaled = jnp.where(lax.axis_index("gx") % 2 == 0, even_obs_ref[...], obs_ref[...])
    full = lax.dot_general(
        scaled, scaled, (((0,), (0,)), ((), ())), precision=HIGHEST, preferred_element_type=F32
    )
    lane, sub = lanes((members, 128)), rows_of((members, 128))
    a = full[:members, :] + jnp.where(lane == sub, members - 1.0, 0.0)
    a = eliminated(a, members)
    diagonal = jnp.sum(jnp.where(lane == sub, a, 0.0), axis=1, keepdims=True)
    scale = lax.rsqrt(diagonal)
    inverse = scale * jnp.where(lane < sub, a, jnp.where(lane == sub, 1.0, 0.0))
    reduced = scale * a[:, members : members + 1]
    weights = jnp.sum(reduced * inverse, axis=0, keepdims=True)
    transform = jnp.sqrt(members - 1.0) * inverse + weights
    share = (1.0 - jnp.sum(jnp.where(lane < members, transform, 0.0), axis=1, keepdims=True)) * (1.0 / members)
    transform = (transform + share)[:, :members]
    for r in range(count):
        out_ref[pl.ds(r, members, stride=count), :] = jnp.dot(
            transform, f_ref[r * members : (r + 1) * members, :], precision=HIGHEST, preferred_element_type=F32
        )


def swap(x, axis, offset):
    pairs = [(i, i + 1) for i in range(offset, lax.axis_size(axis) - 1, 2)]
    return lax.ppermute(x, axis, pairs + [(b, a) for a, b in pairs])


def stack(x_ref, other_ref, *refs):
    out_ref = refs[-1]
    out_ref[: x_ref.shape[0], :] = x_ref[...]
    out_ref[x_ref.shape[0] :, :] = other_ref[...]


def stacked(x, other, *ahead):
    return pl.pallas_call(
        stack,
        out_shape=jax.ShapeDtypeStruct((2 * x.shape[0], x.shape[1]), x.dtype),
        in_specs=[VMEM] * 2 + [ANY] * len(ahead),
        out_specs=VMEM,
        compiler_params=PARAMS,
        name="stack",
    )(x, other, *ahead)


def doubled(x, axis, step, *ahead):
    ny, nx = lax.axis_size("gy"), lax.axis_size("gx")
    flip = (step, 0) if axis == "gy" else (0, step)
    pairs = [(a * nx + b, (a ^ flip[0]) * nx + (b ^ flip[1])) for a in range(ny) for b in range(1, nx, 2)]
    return stacked(x, lax.ppermute(x, ("gy", "gx"), pairs), *ahead)


def handed_on(x):
    return lax.ppermute(x, "gx", [(i, i - 1) for i in range(1, lax.axis_size("gx"), 2)])


def two_power(size):
    return size & (size - 1) == 0


def row_blocks(block):
    size = lax.axis_size("gx")
    if size == 1 or not two_power(size):
        blocks = lax.all_gather(block, "gx", tiled=True)
        return blocks, blocks
    blocks = jnp.concatenate([block, lax.ppermute(block, "gx", [(i, i ^ 1) for i in range(size)])], axis=0)
    step = 2
    while step < size:
        blocks = doubled(blocks, "gx", step)
        step *= 2
    return blocks, handed_on(blocks)


def all_rows(packet, early, late):
    size = lax.axis_size("gy")
    if lax.axis_size("gx") == 1 or not two_power(lax.axis_size("gx")) or not two_power(size):
        if two_power(lax.axis_size("gx")) and lax.axis_size("gx") > 1:
            own = handed_on(packet)
            packet = jnp.where(lax.axis_index("gx") % 2 == 0, own, packet)
        packets = lax.all_gather(packet, "gy", tiled=True)
        return packets, packets
    step = 1
    while step < size:
        ahead = ([early] if step == 1 else []) + ([late] if 2 * step == size else [])
        packet = doubled(packet, "gy", step, *ahead)
        step *= 2
    return packet, handed_on(packet)


def body(ensemble, flow, obs_cell, obs_value, obs_var):
    members, count, width = ensemble.shape
    n_obs = obs_cell.shape[-1]
    size = lax.axis_size("gx")
    is_even = lax.axis_index("gx") % 2 == 0
    call = functools.partial(pl.pallas_call, compiler_params=PARAMS)

    def shape(*dims):
        return jax.ShapeDtypeStruct(dims + (width,), F32)

    field, tile_flow, obs, rows_even, rows_odd = call(
        functools.partial(load, members, count, n_obs),
        out_shape=[shape(members * count), shape(3, count), shape(24)] + [shape(2 * members + 8)] * 2,
        in_specs=[HBM] * 5,
        out_specs=[VMEM] * 5,
        scratch_shapes=[pltpu.SMEM((n_obs,), jnp.int32)]
        + [pltpu.SMEM((n_obs,), F32)] * 2
        + [pltpu.SemaphoreType.DMA((count + 4,))],
        name="load",
    )(*[
        pltpu.with_memory_space_constraint(x, pltpu.HBM)
        for x in (ensemble, flow, obs_cell.reshape(-1), obs_value.reshape(-1), obs_var.reshape(-1))
    ])
    rows_odd = swap(rows_odd, "gy", 1)
    rows_even = swap(rows_even, "gy", 0)
    tall = pltpu.VMEM((3, EDGE, width), F32)
    block = call(
        functools.partial(observe, members, count, n_obs),
        out_shape=shape(BLOCK),
        in_specs=[VMEM] * 5,
        out_specs=VMEM,
        scratch_shapes=[tall],
        name="observe",
    )(field, tile_flow, obs, rows_odd, rows_even)
    blocks, blocks_even = row_blocks(block)
    packet = call(
        functools.partial(complete, members, n_obs, size),
        out_shape=shape(n_obs * size),
        in_specs=[VMEM],
        out_specs=VMEM,
        name="complete",
    )(blocks)
    predicted = call(
        functools.partial(forecast, members, count, size),
        out_shape=shape(members * count),
        in_specs=[VMEM] * 5,
        out_specs=VMEM,
        scratch_shapes=[tall],
        cost_estimate=pl.CostEstimate(flops=4 * 10**6, bytes_accessed=6 * 10**5, transcendentals=0),
        name="forecast",
    )(field, tile_flow, rows_odd, rows_even, jnp.where(is_even, blocks_even, blocks))
    out = call(
        functools.partial(analyse, members, count),
        out_shape=shape(members * count),
        in_specs=[VMEM] * 3,
        out_specs=VMEM,
        name="analyse",
    )(predicted, *all_rows(packet, blocks_even, predicted))
    return out.reshape(ensemble.shape)


def solution(mesh):
    return jax.shard_map(
        body,
        mesh=mesh,
        in_specs=(
            P(None, "gy", "gx"),
            P(None, "gy", "gx"),
            P("gy", "gx", None),
            P("gy", "gx", None),
            P("gy", "gx", None),
        ),
        out_specs=P(None, "gy", "gx"),
        check_vma=False,
    )
```

```python
import functools

import jax
import jax.numpy as jnp
from jax import lax
from jax.experimental import pallas as pl
from jax.experimental.pallas import tpu as pltpu
from jax.sharding import PartitionSpec as P

F32 = jnp.float32
HIGHEST = lax.Precision.HIGHEST
PARAMS = pltpu.CompilerParams(vmem_limit_bytes=24 * 1024 * 1024)
VMEM = pl.BlockSpec(memory_space=pltpu.VMEM)
SMEM = pl.BlockSpec(memory_space=pltpu.SMEM)


def lanes(shape):
    return lax.broadcasted_iota(jnp.int32, shape, len(shape) - 1)


def rows_of(shape):
    return lax.broadcasted_iota(jnp.int32, shape, len(shape) - 2)


def shifted(x, amount):
    return pltpu.roll(x, amount % x.shape[-1], x.ndim - 1)


EDGE = 16
BLOCK = EDGE + 16
MID, OBS = EDGE, EDGE + 8
VALUE, FACTOR, TO_WEST, TO_EAST, WEIGHTS = 64, 65, 66, 67, 72
HBM = pl.BlockSpec(memory_space=pltpu.HBM)


def coefficients(k, u, v):
    return 1.0 - 4.0 * k, k + 0.5 * v, k - 0.5 * v, k + 0.5 * u, k - 0.5 * u


def combine(c, own, north, south, west, east):
    return c[0] * own + c[1] * north + c[2] * south + c[3] * west + c[4] * east


def transposed(x):
    return jnp.concatenate([x, jnp.zeros((128 - x.shape[0], 128), F32)], axis=0).T


def load(
    members, count, n_obs, ens_hbm, flow_hbm, cell_hbm, value_hbm, var_hbm,
    field_ref, flow_ref, obs_ref, even_ref, odd_ref, cell_ref, value_ref, var_ref, sems,
):
    order = [0, count - 1, 1, count - 2] + list(range(2, count - 2))
    copies = [pltpu.make_async_copy(flow_hbm, flow_ref, sems.at[count])]
    copies += [
        pltpu.make_async_copy(ens_hbm.at[:, r, :], field_ref.at[pl.ds(r * members, members), :], sems.at[r]) for r in order
    ]
    small = [
        pltpu.make_async_copy(src, dst, sems.at[count + 1 + i])
        for i, (src, dst) in enumerate(((cell_hbm, cell_ref), (value_hbm, value_ref), (var_hbm, var_ref)))
    ]
    for copy in copies + small:
        copy.start()
    for copy in copies + small:
        copy.wait()
    is_even = lax.axis_index("gy") % 2 == 0

    def grid_row(r):
        return field_ref[r * members : (r + 1) * members, :]

    top, bottom = [(grid_row(a), grid_row(b), flow_ref[:, a, :]) for a, b in ((0, 1), (count - 1, count - 2))]
    for ref, first in ((even_ref, is_even), (odd_ref, jnp.logical_not(is_even))):
        near, second, flow = [jnp.where(first, low, high) for low, high in zip(bottom, top)]
        ref[0:members, :] = near
        ref[members : 2 * members, :] = second
        ref[2 * members : 2 * members + 3, :] = flow
        ref[2 * members + 3 :, :] = jnp.zeros((5, 128), F32)
    sub = rows_of((8, 128))
    for i, (ref, rest) in enumerate(((cell_ref, 0.0), (value_ref, 0.0), (var_ref, 1.0))):
        block = jnp.full((8, 128), rest, F32)
        for j in range(n_obs):
            block = jnp.where(sub == j, ref[j].astype(F32), block)
        obs_ref[8 * i : 8 * i + 8, :] = block


def halo_rows(even_ref, odd_ref, members):
    at = lax.axis_index("gy")
    is_even = at % 2 == 0
    inside = at > 0, at < lax.axis_size("gy") - 1
    parts = []
    for lo, hi in ((0, members), (members, 2 * members), (2 * members, 2 * members + 3)):
        e, o = even_ref[lo:hi, :], odd_ref[lo:hi, :]
        pair = jnp.where(is_even, o, e), jnp.where(is_even, e, o)
        parts.append([jnp.where(here, x, 0.0) for here, x in zip(inside, pair)])
    return tuple(p[0] for p in parts), tuple(p[1] for p in parts)


def tall_coefficients(scratch, flow_ref, north_flow, south_flow, count):
    for k in range(3):
        scratch[k, 0:count, :] = flow_ref[k]
        scratch[k, count:, :] = jnp.zeros((EDGE - count, 128), F32)
        scratch[k, count : count + 1, :] = south_flow[k : k + 1]
        scratch[k, EDGE - 1 : EDGE, :] = north_flow[k : k + 1]
    return coefficients(*[scratch[k] for k in range(3)])


def tall_field(field_ref, north, south, members, count):
    field = {-2: north[1], -1: north[0], count: south[0], count + 1: south[1]}
    field.update({r: field_ref[r * members : (r + 1) * members, :] for r in range(count)})
    return field


def observe(members, count, n_obs, field_ref, flow_ref, obs_ref, odd_ref, even_ref, out_ref, tall_ref):
    north, south = halo_rows(even_ref, odd_ref, members)
    field = tall_field(field_ref, north, south, members, count)
    own, up, down, left, right = tall_coefficients(tall_ref, flow_ref, north[2], south[2], count)
    lane, sub = lanes((EDGE, 128)), rows_of((EDGE, 128))
    wide = lanes((members, 128))
    has_west = lax.axis_index("gx") > 0
    has_east = lax.axis_index("gx") < lax.axis_size("gx") - 1

    def spread(w):
        to_west, to_east = left * w, right * w
        inside = (
            own * w
            + pltpu.roll(up * w, EDGE - 1, 0)
            + pltpu.roll(down * w, 1, 0)
            + jnp.where(lane == 127, 0.0, shifted(to_west, -1))
            + jnp.where(lane == 0, 0.0, shifted(to_east, 1))
        )
        return inside, jnp.where(has_west, to_west[:, 0:1], 0.0), jnp.where(has_east, to_east[:, 127:128], 0.0)

    packed = jnp.zeros((members, 128), F32)
    second = jnp.zeros((members, 128), F32)
    for r in range(-1, count + 1):
        x, at = field[r], r % EDGE
        packed = jnp.where(wide == at, shifted(x, at), packed)
        packed = jnp.where(wide == EDGE + at, shifted(x, EDGE + at - 127), packed)
        if 0 <= r < count:
            second = jnp.where(wide == at, shifted(x, at - 1), second)
            second = jnp.where(wide == EDGE + at, shifted(x, EDGE + at - 126), second)

    def edge_row(low, high):
        both = jnp.where(lane == sub, low[:, 0:1], jnp.where(lane == sub + EDGE, high[:, 127:128], 0.0))
        return jnp.sum(both, axis=0, keepdims=True)

    middle = (
        edge_row(own, own) * packed
        + edge_row(up, up) * jnp.where(wide % EDGE == 0, shifted(packed, 1 - EDGE), shifted(packed, 1))
        + edge_row(down, down) * shifted(packed, -1)
        + edge_row(right, left) * second
    )
    packed = jnp.where(wide < 2 * EDGE, packed, 0.0)
    packed = jnp.where((wide >= 32) & (wide < 40), shifted(middle, 32), packed)
    packed = jnp.where((wide >= 40) & (wide < 48), shifted(middle, 24), packed)
    top_lane = lane[:8]
    meta = jnp.where(top_lane == VALUE, obs_ref[8:16, :], 0.0)
    meta = jnp.where(top_lane == FACTOR, lax.rsqrt(obs_ref[16:24, :]), meta)
    meta = jnp.where(top_lane == TO_WEST, left[:8, 0:1], meta)
    meta = jnp.where(top_lane == TO_EAST, right[:8, 127:128], meta)
    position = (sub * 128 + lane).astype(F32)
    for j in range(n_obs):
        here = jnp.where((sub < count) & (position == obs_ref[j : j + 1, :]), 1.0, 0.0)
        w, mid_west, mid_east = spread(here)
        w, west, east = spread(w)
        total = w[EDGE - 2 : EDGE - 1, :] * field[-2]
        for r in range(-1, count + 2):
            total = total + w[r % EDGE : r % EDGE + 1, :] * field[r]
        packed = jnp.where(wide == 48 + j, jnp.sum(total, axis=1, keepdims=True), packed)
        for k, column in enumerate((west[:8], west[8:], east[:8], east[8:], mid_west[:8], mid_east[:8])):
            meta = jnp.where(top_lane == WEIGHTS + k * n_obs + j, column, meta)
    turned = jnp.concatenate([packed, jnp.zeros((128 - members, 128), F32)], axis=0).T
    out_ref[0:EDGE, :] = turned[0:EDGE] + shifted(turned[EDGE : 2 * EDGE], 64)
    out_ref[MID : MID + 8, :] = turned[32:40] + shifted(turned[40:48], 64)
    out_ref[OBS : OBS + 8, :] = turned[48:56] + meta


def block_rows(ref, start, tile, size, rows):
    return ref[pl.ds(pl.multiple_of(place_of(tile, size) * BLOCK + start, 8), rows), :]


def side_columns(ref, tile, size):
    west, east = jnp.maximum(tile - 1, 0), jnp.minimum(tile + 1, size - 1)
    own = block_rows(ref, 0, tile, size, EDGE)
    west_x = shifted(block_rows(ref, 0, west, size, EDGE), 64)
    east_x = block_rows(ref, 0, east, size, EDGE)
    west_mid = shifted(block_rows(ref, MID, west, size, 8), 64)
    west_mid += block_rows(ref, OBS, west, size, 8)[:, TO_EAST : TO_EAST + 1] * own[:8]
    east_mid = block_rows(ref, MID, east, size, 8)
    east_mid += block_rows(ref, OBS, east, size, 8)[:, TO_WEST : TO_WEST + 1] * shifted(own[:8], 64)
    return west_x, east_x, west_mid, east_mid


def complete(members, n_obs, size, blocks_ref, out_ref):
    lane = lanes((n_obs, 128))
    for tile in range(size):
        west, east, west_mid, east_mid = side_columns(blocks_ref, jnp.int32(tile), size)
        block = block_rows(blocks_ref, OBS, jnp.int32(tile), size, 8)
        terms = (west[:8], west[8:], east[:8], east[8:], west_mid, east_mid)
        added = []
        for j in range(n_obs):
            at = [WEIGHTS + k * n_obs + j for k in range(len(terms))]
            total = sum(block[:, a : a + 1] * term for a, term in zip(at, terms))
            added.append(jnp.sum(total, axis=0, keepdims=True))
        block = block[:n_obs]
        at = jnp.where(lane < members, block + jnp.concatenate(added, axis=0), 0.0)
        mean = jnp.sum(at, axis=1, keepdims=True) * (1.0 / members)
        raw = jnp.where(lane < members, at - mean, jnp.where(lane == members, block[:, VALUE : VALUE + 1] - mean, 0.0))
        out_ref[n_obs * tile : n_obs * (tile + 1), :] = raw * block[:, FACTOR : FACTOR + 1]


def forecast(members, count, size, field_ref, flow_ref, odd_ref, even_ref, blocks_ref, out_ref, tall_ref):
    north, south = halo_rows(even_ref, odd_ref, members)
    tile = lax.axis_index("gx")
    west, east, west_mid, east_mid = side_columns(blocks_ref, tile, size)
    has_west, has_east = tile > 0, tile < size - 1
    sides = [jnp.where(has_west, west, 0.0), jnp.where(has_east, east, 0.0)]
    sides += [jnp.where(has_west, west_mid, 0.0), jnp.where(has_east, east_mid, 0.0), jnp.zeros((80, 128), F32)]
    sides = jnp.concatenate(sides, axis=0).T[:members]
    field = tall_field(field_ref, north, south, members, count)
    tall = tall_coefficients(tall_ref, flow_ref, north[2], south[2], count)
    lane = lanes((members, 128))

    def step(rows, r, west_at, east_at):
        w = jnp.where(lane == 0, shifted(sides, -west_at), shifted(rows[r], 1))
        e = jnp.where(lane == 127, shifted(sides, 127 - east_at), shifted(rows[r], -1))
        at = r % EDGE
        return combine([c[at : at + 1, :] for c in tall], rows[r], rows[r - 1], rows[r + 1], w, e)

    middle = {r: step(field, r, r % EDGE, EDGE + r % EDGE) for r in range(-1, count + 1)}
    for r in range(count):
        out_ref[r * members : (r + 1) * members, :] = step(middle, r, 2 * EDGE + r, 2 * EDGE + 8 + r)


def eliminated(a, members):
    size = 8
    lane, sub = lanes((size, 128)), rows_of((size, 128))
    part = [a[size * q : size * (q + 1), :] for q in range(members // size)]
    for p in range(len(part)):
        column = {
            (q, j): jnp.broadcast_to(part[q][:, size * p + j : size * p + j + 1], (size, 128))
            for q in range(p, len(part))
            for j in range(size)
        }
        for j in range(size):
            at = size * p + j
            inverse = 1.0 / column[p, j][j : j + 1, :]
            unit = jnp.where(lane[:1] == at, 1.0, part[p][j : j + 1, :])
            pivots = [column[p, k][j : j + 1, :] for k in range(j + 1, size)]
            for q in range(p, len(part)):
                factor = column[q, j] * inverse
                if q == p:
                    factor = jnp.where(sub > j, factor, 0.0)
                for k in range(j + 1, size):
                    column[q, k] = column[q, k] - factor * pivots[k - j - 1]
                cleared = (lane == at) & (sub > j) if q == p else lane == at
                part[q] = jnp.where(cleared, 0.0, part[q]) - factor * unit
    return jnp.concatenate(part, axis=0)


def analyse(members, count, f_ref, obs_ref, out_ref):
    scaled = obs_ref[...]
    full = lax.dot_general(
        scaled, scaled, (((0,), (0,)), ((), ())), precision=HIGHEST, preferred_element_type=F32
    )
    lane, sub = lanes((members, 128)), rows_of((members, 128))
    a = full[:members, :] + jnp.where(lane == sub, members - 1.0, 0.0)
    a = eliminated(a, members)
    diagonal = jnp.sum(jnp.where(lane == sub, a, 0.0), axis=1, keepdims=True)
    scale = lax.rsqrt(diagonal)
    inverse = scale * jnp.where(lane < sub, a, jnp.where(lane == sub, 1.0, 0.0))
    reduced = scale * a[:, members : members + 1]
    weights = jnp.sum(reduced * inverse, axis=0, keepdims=True)
    transform = jnp.sqrt(members - 1.0) * inverse + weights
    share = (1.0 - jnp.sum(jnp.where(lane < members, transform, 0.0), axis=1, keepdims=True)) * (1.0 / members)
    transform = (transform + share)[:, :members]
    for r in range(count):
        out_ref[pl.ds(r, members, stride=count), :] = jnp.dot(
            transform, f_ref[r * members : (r + 1) * members, :], precision=HIGHEST, preferred_element_type=F32
        )


def swap(x, axis, offset):
    ny, nx = lax.axis_size("gy"), lax.axis_size("gx")
    partner = {i: i for i in range(ny)}
    for i in range(offset, ny - 1, 2):
        partner[i], partner[i + 1] = i + 1, i
    pairs = []
    for a in range(ny):
        for b in range(nx):
            if partner[a] != a:
                pairs.append((a * nx + b, partner[a] * nx + b))
            elif nx % 2 == 0:
                pairs.append((a * nx + b, a * nx + (b ^ 1)))
    return lax.ppermute(x, ("gy", "gx"), pairs)


def two_power(size):
    return size & (size - 1) == 0


def doubled(x, flip_y, flip_x):
    ny, nx = lax.axis_size("gy"), lax.axis_size("gx")
    pairs = [(a * nx + b, (a ^ flip_y) * nx + (b ^ flip_x)) for a in range(ny) for b in range(nx)]
    return jnp.concatenate([x, lax.ppermute(x, ("gy", "gx"), pairs)], axis=0)


def row_blocks(block):
    size, step = lax.axis_size("gx"), 1
    if not two_power(size):
        return lax.all_gather(block, "gx", tiled=True)
    while step < size:
        block = doubled(block, 0, step | 1)
        step *= 2
    return block


def place_of(tile, size):
    if not two_power(size):
        return tile
    distance = jnp.bitwise_xor(lax.axis_index("gx"), tile)
    place, bit = distance, 2
    while bit < size:
        place = jnp.bitwise_xor(place, (distance // bit) % 2)
        bit *= 2
    return place


def all_rows(packet):
    size, step = lax.axis_size("gy"), 1
    if not two_power(size):
        return lax.all_gather(packet, "gy", tiled=True)
    while step < size:
        packet = doubled(packet, step, 1 - lax.axis_size("gx") % 2)
        step *= 2
    return packet


def body(ensemble, flow, obs_cell, obs_value, obs_var):
    members, count, width = ensemble.shape
    n_obs = obs_cell.shape[-1]
    size = lax.axis_size("gx")
    call = functools.partial(pl.pallas_call, compiler_params=PARAMS)

    def shape(*dims):
        return jax.ShapeDtypeStruct(dims + (width,), F32)

    field, tile_flow, obs, rows_even, rows_odd = call(
        functools.partial(load, members, count, n_obs),
        out_shape=[shape(members * count), shape(3, count), shape(24)] + [shape(2 * members + 8)] * 2,
        in_specs=[HBM] * 5,
        out_specs=[VMEM] * 5,
        scratch_shapes=[pltpu.SMEM((n_obs,), jnp.int32)]
        + [pltpu.SMEM((n_obs,), F32)] * 2
        + [pltpu.SemaphoreType.DMA((count + 4,))],
        name="load",
    )(*[
        pltpu.with_memory_space_constraint(x, pltpu.HBM)
        for x in (ensemble, flow, obs_cell.reshape(-1), obs_value.reshape(-1), obs_var.reshape(-1))
    ])
    rows_odd = swap(rows_odd, "gy", 1)
    rows_even = swap(rows_even, "gy", 0)
    tall = pltpu.VMEM((3, EDGE, width), F32)
    block = call(
        functools.partial(observe, members, count, n_obs),
        out_shape=shape(BLOCK),
        in_specs=[VMEM] * 5,
        out_specs=VMEM,
        scratch_shapes=[tall],
        name="observe",
    )(field, tile_flow, obs, rows_odd, rows_even)
    blocks = row_blocks(block)
    packet = call(
        functools.partial(complete, members, n_obs, size),
        out_shape=shape(n_obs * size),
        in_specs=[VMEM],
        out_specs=VMEM,
        name="complete",
    )(blocks)
    predicted = call(
        functools.partial(forecast, members, count, size),
        out_shape=shape(members * count),
        in_specs=[VMEM] * 5,
        out_specs=VMEM,
        scratch_shapes=[tall],
        cost_estimate=pl.CostEstimate(flops=4 * 10**6, bytes_accessed=6 * 10**5, transcendentals=0),
        name="forecast",
    )(field, tile_flow, rows_odd, rows_even, blocks)
    out = call(
        functools.partial(analyse, members, count),
        out_shape=shape(members * count),
        in_specs=[VMEM] * 2,
        out_specs=VMEM,
        name="analyse",
    )(predicted, all_rows(packet))
    return out.reshape(ensemble.shape)


def solution(mesh):
    return jax.shard_map(
        body,
        mesh=mesh,
        in_specs=(
            P(None, "gy", "gx"),
            P(None, "gy", "gx"),
            P("gy", "gx", None),
            P("gy", "gx", None),
            P("gy", "gx", None),
        ),
        out_specs=P(None, "gy", "gx"),
        check_vma=False,
    )
```

```python
import functools

import jax
import jax.numpy as jnp
from jax import lax
from jax.experimental import pallas as pl
from jax.experimental.pallas import tpu as pltpu
from jax.sharding import PartitionSpec as P

F32 = jnp.float32
HIGHEST = lax.Precision.HIGHEST
PARAMS = pltpu.CompilerParams(vmem_limit_bytes=24 * 1024 * 1024)
VMEM = pl.BlockSpec(memory_space=pltpu.VMEM)
SMEM = pl.BlockSpec(memory_space=pltpu.SMEM)


def lanes(shape):
    return lax.broadcasted_iota(jnp.int32, shape, len(shape) - 1)


def rows_of(shape):
    return lax.broadcasted_iota(jnp.int32, shape, len(shape) - 2)


def shifted(x, amount):
    return pltpu.roll(x, amount % x.shape[-1], x.ndim - 1)


EDGE = 16
BLOCK = EDGE + 16
MID, OBS = EDGE, EDGE + 8
VALUE, FACTOR, TO_WEST, TO_EAST, WEIGHTS = 64, 65, 66, 67, 72
HBM = pl.BlockSpec(memory_space=pltpu.HBM)


def coefficients(k, u, v):
    return 1.0 - 4.0 * k, k + 0.5 * v, k - 0.5 * v, k + 0.5 * u, k - 0.5 * u


def combine(c, own, north, south, west, east):
    return c[0] * own + c[1] * north + c[2] * south + c[3] * west + c[4] * east


def transposed(x):
    return jnp.concatenate([x, jnp.zeros((128 - x.shape[0], 128), F32)], axis=0).T


def load(
    members, count, n_obs, ens_hbm, flow_hbm, cell_hbm, value_hbm, var_hbm,
    field_ref, flow_ref, obs_ref, even_ref, odd_ref, cell_ref, value_ref, var_ref, sems,
):
    order = [0, count - 1, 1, count - 2] + list(range(2, count - 2))
    copies = [pltpu.make_async_copy(flow_hbm, flow_ref, sems.at[count])]
    copies += [
        pltpu.make_async_copy(ens_hbm.at[:, r, :], field_ref.at[pl.ds(r * members, members), :], sems.at[r]) for r in order
    ]
    small = [
        pltpu.make_async_copy(src, dst, sems.at[count + 1 + i])
        for i, (src, dst) in enumerate(((cell_hbm, cell_ref), (value_hbm, value_ref), (var_hbm, var_ref)))
    ]
    for copy in copies + small:
        copy.start()
    for copy in copies + small:
        copy.wait()
    is_even = lax.axis_index("gy") % 2 == 0

    def grid_row(r):
        return field_ref[r * members : (r + 1) * members, :]

    top, bottom = [(grid_row(a), grid_row(b), flow_ref[:, a, :]) for a, b in ((0, 1), (count - 1, count - 2))]
    for ref, first in ((even_ref, is_even), (odd_ref, jnp.logical_not(is_even))):
        near, second, flow = [jnp.where(first, low, high) for low, high in zip(bottom, top)]
        ref[0:members, :] = near
        ref[members : 2 * members, :] = second
        ref[2 * members : 2 * members + 3, :] = flow
        ref[2 * members + 3 :, :] = jnp.zeros((5, 128), F32)
    sub = rows_of((8, 128))
    for i, (ref, rest) in enumerate(((cell_ref, 0.0), (value_ref, 0.0), (var_ref, 1.0))):
        block = jnp.full((8, 128), rest, F32)
        for j in range(n_obs):
            block = jnp.where(sub == j, ref[j].astype(F32), block)
        obs_ref[8 * i : 8 * i + 8, :] = block


def halo_rows(even_ref, odd_ref, members):
    at = lax.axis_index("gy")
    is_even = at % 2 == 0
    inside = at > 0, at < lax.axis_size("gy") - 1
    parts = []
    for lo, hi in ((0, members), (members, 2 * members), (2 * members, 2 * members + 3)):
        e, o = even_ref[lo:hi, :], odd_ref[lo:hi, :]
        pair = jnp.where(is_even, o, e), jnp.where(is_even, e, o)
        parts.append([jnp.where(here, x, 0.0) for here, x in zip(inside, pair)])
    return tuple(p[0] for p in parts), tuple(p[1] for p in parts)


def tall_coefficients(scratch, flow_ref, north_flow, south_flow, count):
    for k in range(3):
        scratch[k, 0:count, :] = flow_ref[k]
        scratch[k, count:, :] = jnp.zeros((EDGE - count, 128), F32)
        scratch[k, count : count + 1, :] = south_flow[k : k + 1]
        scratch[k, EDGE - 1 : EDGE, :] = north_flow[k : k + 1]
    return coefficients(*[scratch[k] for k in range(3)])


def tall_field(field_ref, north, south, members, count):
    field = {-2: north[1], -1: north[0], count: south[0], count + 1: south[1]}
    field.update({r: field_ref[r * members : (r + 1) * members, :] for r in range(count)})
    return field


def observe(members, count, n_obs, field_ref, flow_ref, obs_ref, odd_ref, even_ref, out_ref, tall_ref):
    north, south = halo_rows(even_ref, odd_ref, members)
    field = tall_field(field_ref, north, south, members, count)
    own, up, down, left, right = tall_coefficients(tall_ref, flow_ref, north[2], south[2], count)
    lane, sub = lanes((EDGE, 128)), rows_of((EDGE, 128))
    wide = lanes((members, 128))
    has_west = lax.axis_index("gx") > 0
    has_east = lax.axis_index("gx") < lax.axis_size("gx") - 1

    def spread(w):
        to_west, to_east = left * w, right * w
        inside = (
            own * w
            + pltpu.roll(up * w, EDGE - 1, 0)
            + pltpu.roll(down * w, 1, 0)
            + jnp.where(lane == 127, 0.0, shifted(to_west, -1))
            + jnp.where(lane == 0, 0.0, shifted(to_east, 1))
        )
        return inside, jnp.where(has_west, to_west[:, 0:1], 0.0), jnp.where(has_east, to_east[:, 127:128], 0.0)

    packed = jnp.zeros((members, 128), F32)
    second = jnp.zeros((members, 128), F32)
    for r in range(-1, count + 1):
        x, at = field[r], r % EDGE
        packed = jnp.where(wide == at, shifted(x, at), packed)
        packed = jnp.where(wide == EDGE + at, shifted(x, EDGE + at - 127), packed)
        if 0 <= r < count:
            second = jnp.where(wide == at, shifted(x, at - 1), second)
            second = jnp.where(wide == EDGE + at, shifted(x, EDGE + at - 126), second)

    def edge_row(low, high):
        both = jnp.where(lane == sub, low[:, 0:1], jnp.where(lane == sub + EDGE, high[:, 127:128], 0.0))
        return jnp.sum(both, axis=0, keepdims=True)

    middle = (
        edge_row(own, own) * packed
        + edge_row(up, up) * jnp.where(wide % EDGE == 0, shifted(packed, 1 - EDGE), shifted(packed, 1))
        + edge_row(down, down) * shifted(packed, -1)
        + edge_row(right, left) * second
    )
    packed = jnp.where(wide < 2 * EDGE, packed, 0.0)
    packed = jnp.where((wide >= 32) & (wide < 40), shifted(middle, 32), packed)
    packed = jnp.where((wide >= 40) & (wide < 48), shifted(middle, 24), packed)
    top_lane = lane[:8]
    meta = jnp.where(top_lane == VALUE, obs_ref[8:16, :], 0.0)
    meta = jnp.where(top_lane == FACTOR, lax.rsqrt(obs_ref[16:24, :]), meta)
    meta = jnp.where(top_lane == TO_WEST, left[:8, 0:1], meta)
    meta = jnp.where(top_lane == TO_EAST, right[:8, 127:128], meta)
    position = (sub * 128 + lane).astype(F32)
    for j in range(n_obs):
        here = jnp.where((sub < count) & (position == obs_ref[j : j + 1, :]), 1.0, 0.0)
        w, mid_west, mid_east = spread(here)
        w, west, east = spread(w)
        total = w[EDGE - 2 : EDGE - 1, :] * field[-2]
        for r in range(-1, count + 2):
            total = total + w[r % EDGE : r % EDGE + 1, :] * field[r]
        packed = jnp.where(wide == 48 + j, jnp.sum(total, axis=1, keepdims=True), packed)
        for k, column in enumerate((west[:8], west[8:], east[:8], east[8:], mid_west[:8], mid_east[:8])):
            meta = jnp.where(top_lane == WEIGHTS + k * n_obs + j, column, meta)
    turned = jnp.concatenate([packed, jnp.zeros((128 - members, 128), F32)], axis=0).T
    out_ref[0:EDGE, :] = turned[0:EDGE] + shifted(turned[EDGE : 2 * EDGE], 64)
    out_ref[MID : MID + 8, :] = turned[32:40] + shifted(turned[40:48], 64)
    out_ref[OBS : OBS + 8, :] = turned[48:56] + meta


def block_rows(ref, start, tile, size, rows):
    return ref[pl.ds(pl.multiple_of(place_of(tile, size) * BLOCK + start, 8), rows), :]


def side_columns(ref, tile, size):
    west, east = jnp.maximum(tile - 1, 0), jnp.minimum(tile + 1, size - 1)
    own = block_rows(ref, 0, tile, size, EDGE)
    west_x = shifted(block_rows(ref, 0, west, size, EDGE), 64)
    east_x = block_rows(ref, 0, east, size, EDGE)
    west_mid = shifted(block_rows(ref, MID, west, size, 8), 64)
    west_mid += block_rows(ref, OBS, west, size, 8)[:, TO_EAST : TO_EAST + 1] * own[:8]
    east_mid = block_rows(ref, MID, east, size, 8)
    east_mid += block_rows(ref, OBS, east, size, 8)[:, TO_WEST : TO_WEST + 1] * shifted(own[:8], 64)
    return west_x, east_x, west_mid, east_mid


def complete(members, n_obs, size, blocks_ref, out_ref):
    lane = lanes((n_obs, 128))
    for tile in range(size):
        west, east, west_mid, east_mid = side_columns(blocks_ref, jnp.int32(tile), size)
        block = block_rows(blocks_ref, OBS, jnp.int32(tile), size, 8)
        terms = (west[:8], west[8:], east[:8], east[8:], west_mid, east_mid)
        added = []
        for j in range(n_obs):
            at = [WEIGHTS + k * n_obs + j for k in range(len(terms))]
            total = sum(block[:, a : a + 1] * term for a, term in zip(at, terms))
            added.append(jnp.sum(total, axis=0, keepdims=True))
        block = block[:n_obs]
        at = jnp.where(lane < members, block + jnp.concatenate(added, axis=0), 0.0)
        mean = jnp.sum(at, axis=1, keepdims=True) * (1.0 / members)
        raw = jnp.where(lane < members, at - mean, jnp.where(lane == members, block[:, VALUE : VALUE + 1] - mean, 0.0))
        out_ref[n_obs * tile : n_obs * (tile + 1), :] = raw * block[:, FACTOR : FACTOR + 1]


def forecast(members, count, size, field_ref, flow_ref, odd_ref, even_ref, blocks_ref, out_ref, mean_ref, tall_ref):
    north, south = halo_rows(even_ref, odd_ref, members)
    tile = lax.axis_index("gx")
    west, east, west_mid, east_mid = side_columns(blocks_ref, tile, size)
    has_west, has_east = tile > 0, tile < size - 1
    sides = [jnp.where(has_west, west, 0.0), jnp.where(has_east, east, 0.0)]
    sides += [jnp.where(has_west, west_mid, 0.0), jnp.where(has_east, east_mid, 0.0), jnp.zeros((80, 128), F32)]
    sides = jnp.concatenate(sides, axis=0).T[:members]
    field = tall_field(field_ref, north, south, members, count)
    tall = tall_coefficients(tall_ref, flow_ref, north[2], south[2], count)
    lane = lanes((members, 128))

    def step(rows, r, west_at, east_at):
        w = jnp.where(lane == 0, shifted(sides, -west_at), shifted(rows[r], 1))
        e = jnp.where(lane == 127, shifted(sides, 127 - east_at), shifted(rows[r], -1))
        at = r % EDGE
        return combine([c[at : at + 1, :] for c in tall], rows[r], rows[r - 1], rows[r + 1], w, e)

    middle = {r: step(field, r, r % EDGE, EDGE + r % EDGE) for r in range(-1, count + 1)}
    for r in range(count):
        x = step(middle, r, 2 * EDGE + r, 2 * EDGE + 8 + r)
        mean = jnp.sum(x, axis=0, keepdims=True) * (1.0 / members)
        mean_ref[r : r + 1, :] = mean
        x = x - mean
        high = x.astype(jnp.bfloat16)
        at = slice(128 * r, 128 * (r + 1))
        out_ref[0:members, at] = high
        out_ref[members : 2 * members, at] = (x - high.astype(F32)).astype(jnp.bfloat16)
        out_ref[2 * members :, at] = high


def eliminated(a, members):
    size = 8
    lane, sub = lanes((size, 128)), rows_of((size, 128))
    part = [a[size * q : size * (q + 1), :] for q in range(members // size)]
    pivot = []

    def spread(q, c):
        return jnp.broadcast_to(part[q][:, c : c + 1], (size, 128))

    ahead = {(0, c): spread(0, c) for c in range(size)}
    for p in range(len(part)):
        start, end = size * p, size * (p + 1)
        rest = range(p, len(part))
        column = {(q, c): spread(q, c) for q in rest[1:] for c in range(start, end)}
        column.update(ahead)
        more = range(end, end + size if p + 1 < len(part) else end)
        column.update({(q, c): spread(q, c) for q in rest[:2] for c in more})
        mine = (lane >= start) & (lane < end)
        for q in rest:
            part[q] = jnp.where(mine, 0.0, part[q])
        found = jnp.zeros((size, 128), F32)
        for j in range(size):
            at = start + j
            value = column[p, at][j : j + 1, :]
            found = jnp.where(sub == j, value, found)
            inverse = 1.0 / value
            unit = jnp.where(lane[:1] == at, 1.0, part[p][j : j + 1, :])
            pivots = {c: column[p, c][j : j + 1, :] for c in range(at + 1, end + len(more))}
            for q in rest:
                factor = column[q, at] * inverse
                for c in range(at + 1, end + (len(more) if q <= p + 1 else 0)):
                    column[q, c] = column[q, c] - factor * pivots[c]
                if q == p:
                    factor = jnp.where(sub > j, factor, 0.0)
                part[q] = part[q] - factor * unit
        pivot.append(found)
        ahead = {(p + 1, c): column[p + 1, c] for c in more}
    return jnp.concatenate(part, axis=0), jnp.concatenate(pivot, axis=0)


def analyse(members, count, f_ref, mean_ref, obs_ref, out_ref):
    scaled = obs_ref[...]
    full = lax.dot_general(
        scaled, scaled, (((0,), (0,)), ((), ())), precision=HIGHEST, preferred_element_type=F32
    )
    lane, sub = lanes((members, 128)), rows_of((members, 128))
    a, pivots = eliminated(full[:members, :] + jnp.where(lane == sub, members - 1.0, 0.0), members)
    scale = lax.rsqrt(pivots)
    inverse = scale * jnp.where(lane < sub, a, jnp.where(lane == sub, 1.0, 0.0))
    reduced = scale * a[:, members : members + 1]
    weights = jnp.sum(reduced * inverse, axis=0, keepdims=True)
    transform = (jnp.sqrt(members - 1.0) * inverse + weights)[:, :members]
    high = transform.astype(jnp.bfloat16)
    low = (transform - high.astype(F32)).astype(jnp.bfloat16)
    update = jnp.dot(jnp.concatenate([high, high, low], axis=1), f_ref[...], preferred_element_type=F32)
    for r in range(count):
        out_ref[pl.ds(r, members, stride=count), :] = update[:, 128 * r : 128 * (r + 1)] + mean_ref[r : r + 1, :]


def swap(x, axis, offset):
    ny, nx = lax.axis_size("gy"), lax.axis_size("gx")
    partner = {i: i for i in range(ny)}
    for i in range(offset, ny - 1, 2):
        partner[i], partner[i + 1] = i + 1, i
    pairs = []
    for a in range(ny):
        for b in range(nx):
            if partner[a] != a:
                pairs.append((a * nx + b, partner[a] * nx + b))
            elif nx % 2 == 0:
                pairs.append((a * nx + b, a * nx + (b ^ 1)))
    return lax.ppermute(x, ("gy", "gx"), pairs)


def two_power(size):
    return size & (size - 1) == 0


def doubled(x, flip_y, flip_x):
    ny, nx = lax.axis_size("gy"), lax.axis_size("gx")
    pairs = [(a * nx + b, (a ^ flip_y) * nx + (b ^ flip_x)) for a in range(ny) for b in range(nx)]
    return jnp.concatenate([x, lax.ppermute(x, ("gy", "gx"), pairs)], axis=0)


def row_blocks(block):
    size, step = lax.axis_size("gx"), 1
    if not two_power(size):
        return lax.all_gather(block, "gx", tiled=True)
    while step < size:
        block = doubled(block, 0, step | 1)
        step *= 2
    return block


def place_of(tile, size):
    if not two_power(size):
        return tile
    distance = jnp.bitwise_xor(lax.axis_index("gx"), tile)
    place, bit = distance, 2
    while bit < size:
        place = jnp.bitwise_xor(place, (distance // bit) % 2)
        bit *= 2
    return place


def all_rows(packet):
    step = lax.axis_size("gy")
    if not two_power(step):
        return lax.all_gather(packet, "gy", tiled=True)
    while step > 1:
        step //= 2
        packet = doubled(packet, step, 1 - lax.axis_size("gx") % 2)
    return packet


def body(ensemble, flow, obs_cell, obs_value, obs_var):
    members, count, width = ensemble.shape
    n_obs = obs_cell.shape[-1]
    size = lax.axis_size("gx")
    call = functools.partial(pl.pallas_call, compiler_params=PARAMS)

    def shape(*dims):
        return jax.ShapeDtypeStruct(dims + (width,), F32)

    field, tile_flow, obs, rows_even, rows_odd = call(
        functools.partial(load, members, count, n_obs),
        out_shape=[shape(members * count), shape(3, count), shape(24)] + [shape(2 * members + 8)] * 2,
        in_specs=[HBM] * 5,
        out_specs=[VMEM] * 5,
        scratch_shapes=[pltpu.SMEM((n_obs,), jnp.int32)]
        + [pltpu.SMEM((n_obs,), F32)] * 2
        + [pltpu.SemaphoreType.DMA((count + 4,))],
        name="load",
    )(*[
        pltpu.with_memory_space_constraint(x, pltpu.HBM)
        for x in (ensemble, flow, obs_cell.reshape(-1), obs_value.reshape(-1), obs_var.reshape(-1))
    ])
    rows_odd = swap(rows_odd, "gy", 1)
    rows_even = swap(rows_even, "gy", 0)
    tall = pltpu.VMEM((3, EDGE, width), F32)
    block = call(
        functools.partial(observe, members, count, n_obs),
        out_shape=shape(BLOCK),
        in_specs=[VMEM] * 5,
        out_specs=VMEM,
        scratch_shapes=[tall],
        name="observe",
    )(field, tile_flow, obs, rows_odd, rows_even)
    blocks = row_blocks(block)
    packet = call(
        functools.partial(complete, members, n_obs, size),
        out_shape=shape(n_obs * size),
        in_specs=[VMEM],
        out_specs=VMEM,
        name="complete",
    )(blocks)
    anomaly, mean = call(
        functools.partial(forecast, members, count, size),
        out_shape=[jax.ShapeDtypeStruct((3 * members, count * width), jnp.bfloat16), shape(count)],
        in_specs=[VMEM] * 5,
        out_specs=[VMEM] * 2,
        scratch_shapes=[tall],
        cost_estimate=pl.CostEstimate(flops=4 * 10**6, bytes_accessed=6 * 10**5, transcendentals=0),
        name="forecast",
    )(field, tile_flow, rows_odd, rows_even, blocks)
    out = call(
        functools.partial(analyse, members, count),
        out_shape=shape(members * count),
        in_specs=[VMEM] * 3,
        out_specs=VMEM,
        name="analyse",
    )(anomaly, mean, all_rows(packet))
    return out.reshape(ensemble.shape)


def solution(mesh):
    return jax.shard_map(
        body,
        mesh=mesh,
        in_specs=(
            P(None, "gy", "gx"),
            P(None, "gy", "gx"),
            P("gy", "gx", None),
            P("gy", "gx", None),
            P("gy", "gx", None),
        ),
        out_specs=P(None, "gy", "gx"),
        check_vma=False,
    )
```

```python
import functools

import jax
import jax.numpy as jnp
from jax import lax
from jax.experimental import pallas as pl
from jax.experimental.pallas import tpu as pltpu
from jax.sharding import PartitionSpec as P

F32 = jnp.float32
HIGHEST = lax.Precision.HIGHEST
PARAMS = pltpu.CompilerParams(vmem_limit_bytes=24 * 1024 * 1024)
VMEM = pl.BlockSpec(memory_space=pltpu.VMEM)
SMEM = pl.BlockSpec(memory_space=pltpu.SMEM)


def lanes(shape):
    return lax.broadcasted_iota(jnp.int32, shape, len(shape) - 1)


def rows_of(shape):
    return lax.broadcasted_iota(jnp.int32, shape, len(shape) - 2)


def shifted(x, amount):
    return pltpu.roll(x, amount % x.shape[-1], x.ndim - 1)


EDGE = 16
BLOCK = EDGE + 16
MID, OBS = EDGE, EDGE + 8
VALUE, FACTOR, TO_WEST, TO_EAST, WEIGHTS = 64, 65, 66, 67, 72
HBM = pl.BlockSpec(memory_space=pltpu.HBM)
ANY = pl.BlockSpec(memory_space=pl.ANY)


def coefficients(k, u, v):
    return 1.0 - 4.0 * k, k + 0.5 * v, k - 0.5 * v, k + 0.5 * u, k - 0.5 * u


def combine(c, own, north, south, west, east):
    return c[0] * own + c[1] * north + c[2] * south + c[3] * west + c[4] * east


def transposed(x):
    return jnp.concatenate([x, jnp.zeros((128 - x.shape[0], 128), F32)], axis=0).T


def load(members, count, ens_hbm, flow_hbm, even_ref, odd_ref, sems):
    is_even = lax.axis_index("gy") % 2 == 0
    for ref in (even_ref, odd_ref):
        ref[2 * members :, :] = jnp.zeros((8, 128), F32)

    def copies(refs):
        for i, (ref, near, second) in enumerate(zip(refs, (count - 1, 0), (count - 2, 1))):
            yield pltpu.make_async_copy(ens_hbm.at[:, near, :], ref.at[pl.ds(0, members), :], sems.at[3 * i])
            yield pltpu.make_async_copy(ens_hbm.at[:, second, :], ref.at[pl.ds(members, members), :], sems.at[3 * i + 1])
            yield pltpu.make_async_copy(flow_hbm.at[:, near, :], ref.at[pl.ds(2 * members, 3), :], sems.at[3 * i + 2])

    def bring(refs):
        for copy in list(copies(refs)):
            copy.start()
        for copy in list(copies(refs)):
            copy.wait()

    pl.when(is_even)(lambda: bring((even_ref, odd_ref)))
    pl.when(jnp.logical_not(is_even))(lambda: bring((odd_ref, even_ref)))


def halo_rows(even_ref, odd_ref, members):
    at = lax.axis_index("gy")
    is_even = at % 2 == 0
    inside = at > 0, at < lax.axis_size("gy") - 1
    parts = []
    for lo, hi in ((0, members), (members, 2 * members), (2 * members, 2 * members + 3)):
        e, o = even_ref[lo:hi, :], odd_ref[lo:hi, :]
        pair = jnp.where(is_even, o, e), jnp.where(is_even, e, o)
        parts.append([jnp.where(here, x, 0.0) for here, x in zip(inside, pair)])
    return tuple(p[0] for p in parts), tuple(p[1] for p in parts)


def tall_coefficients(scratch, flow_ref, north_flow, south_flow, count):
    for k in range(3):
        scratch[k, 0:count, :] = flow_ref[k]
        scratch[k, count:, :] = jnp.zeros((EDGE - count, 128), F32)
        scratch[k, count : count + 1, :] = south_flow[k : k + 1]
        scratch[k, EDGE - 1 : EDGE, :] = north_flow[k : k + 1]
    return coefficients(*[scratch[k] for k in range(3)])


def tall_field(field_ref, north, south, members, count):
    field = {-2: north[1], -1: north[0], count: south[0], count + 1: south[1]}
    field.update({r: field_ref[r * members : (r + 1) * members, :] for r in range(count)})
    return field


def spread(w, coeffs, lane):
    own, up, down, left, right = coeffs
    to_west, to_east = left * w, right * w
    inside = (
        own * w
        + pltpu.roll(up * w, EDGE - 1, 0)
        + pltpu.roll(down * w, 1, 0)
        + jnp.where(lane == 127, 0.0, shifted(to_west, -1))
        + jnp.where(lane == 0, 0.0, shifted(to_east, 1))
    )
    has_west = lax.axis_index("gx") > 0
    has_east = lax.axis_index("gx") < lax.axis_size("gx") - 1
    return inside, jnp.where(has_west, to_west[:, 0:1], 0.0), jnp.where(has_east, to_east[:, 127:128], 0.0)


def prepare(
    members, count, n_obs, ens_hbm, flow_hbm, cell_hbm, value_hbm, var_hbm, sent_ref,
    field_ref, flow_ref, packed_ref, meta_ref, weight_ref, rest_ref, cell_ref, value_ref, var_ref, tall_ref, sems,
):
    copies = [
        pltpu.make_async_copy(ens_hbm.at[:, r, :], field_ref.at[pl.ds(r * members, members), :], sems.at[r])
        for r in range(count)
    ]
    pairs = ((flow_hbm, flow_ref), (cell_hbm, cell_ref), (value_hbm, value_ref), (var_hbm, var_ref))
    copies += [pltpu.make_async_copy(src, dst, sems.at[count + i]) for i, (src, dst) in enumerate(pairs)]
    for copy in copies:
        copy.start()
    for copy in copies:
        copy.wait()
    lane, sub = lanes((EDGE, 128)), rows_of((EDGE, 128))
    wide = lanes((members, 128))
    nothing = jnp.zeros((3, 128), F32)
    coeffs = tall_coefficients(tall_ref, flow_ref, nothing, nothing, count)
    coeffs = (jnp.where(sub < count, coeffs[0], 0.0),) + coeffs[1:]
    own, up, down, left, right = coeffs
    field = [field_ref[r * members : (r + 1) * members, :] for r in range(count)]
    packed = jnp.zeros((members, 128), F32)
    second = jnp.zeros((members, 128), F32)
    for r, x in enumerate(field):
        packed = jnp.where(wide == r, shifted(x, r), packed)
        packed = jnp.where(wide == EDGE + r, shifted(x, EDGE + r - 127), packed)
        second = jnp.where(wide == r, shifted(x, r - 1), second)
        second = jnp.where(wide == EDGE + r, shifted(x, EDGE + r - 126), second)

    def edge_row(low, high):
        both = jnp.where(lane == sub, low[:, 0:1], jnp.where(lane == sub + EDGE, high[:, 127:128], 0.0))
        return jnp.sum(both, axis=0, keepdims=True)

    middle = (
        edge_row(own, own) * packed
        + edge_row(up, up) * shifted(packed, 1)
        + edge_row(down, down) * shifted(packed, -1)
        + edge_row(right, left) * second
    )
    packed = jnp.where((wide >= 32) & (wide < 40), shifted(middle, 32), packed)
    packed = jnp.where((wide >= 40) & (wide < 48), shifted(middle, 24), packed)
    top_lane, top_sub = lane[:8], sub[:8]
    blocks = []
    for ref, rest in ((value_ref, 0.0), (var_ref, 1.0)):
        block = jnp.full((8, 128), rest, F32)
        for j in range(n_obs):
            block = jnp.where(top_sub == j, ref[j], block)
        blocks.append(block)
    meta = jnp.where(top_lane == VALUE, blocks[0], 0.0)
    meta = jnp.where(top_lane == FACTOR, lax.rsqrt(blocks[1]), meta)
    meta = jnp.where(top_lane == TO_WEST, left[:8, 0:1], meta)
    meta = jnp.where(top_lane == TO_EAST, right[:8, 127:128], meta)
    for j in range(n_obs):
        here = jnp.where((sub < count) & (sub * 128 + lane == cell_ref[j]), 1.0, 0.0)
        first, mid_west, mid_east = spread(here, coeffs, lane)
        w, west, east = spread(first, coeffs, lane)
        weight_ref[j] = first
        rest_ref[j] = w
        total = w[0:1, :] * field[0]
        for r in range(1, count):
            total = total + w[r : r + 1, :] * field[r]
        packed = jnp.where(wide == 48 + j, jnp.sum(total, axis=1, keepdims=True), packed)
        for k, column in ((0, west), (2, east), (4, mid_west), (5, mid_east)):
            meta = jnp.where(top_lane == WEIGHTS + k * n_obs + j, column[:8], meta)
    packed_ref[...] = packed
    meta_ref[0:8, :] = meta
    last = count - 1
    fix = jnp.zeros((8, 128), F32)
    for at, c, r, col in ((32, up, 0, 0), (40, up, 0, 127), (32 + last, down, last, 0), (40 + last, down, last, 127)):
        fix = jnp.where(top_lane == at, c[r : r + 1, col : col + 1], fix)
    meta_ref[8:16, :] = fix


def observe(
    members, count, n_obs, field_ref, flow_ref, packed_ref, meta_ref, weight_ref, rest_ref, odd_ref, even_ref,
    out_ref, tall_ref,
):
    north, south = halo_rows(even_ref, odd_ref, members)
    lane, sub = lanes((EDGE, 128)), rows_of((EDGE, 128))
    wide = lanes((members, 128))
    for k in range(3):
        tall_ref[k] = jnp.zeros((EDGE, 128), F32)
        tall_ref[k, count : count + 1, :] = south[2][k : k + 1]
        tall_ref[k, EDGE - 1 : EDGE, :] = north[2][k : k + 1]
    coeffs = coefficients(*[tall_ref[k] for k in range(3)])
    coeffs = (jnp.where((sub == count) | (sub == EDGE - 1), coeffs[0], 0.0),) + coeffs[1:]
    rows = {-2: north[1], -1: north[0], count: south[0], count + 1: south[1]}
    tile_rows = {r: field_ref[r * members : (r + 1) * members, :] for r in (0, count - 1)}
    packed, meta, fix = packed_ref[...], meta_ref[0:8, :], meta_ref[8:9, :]
    for x, slot, at in ((rows[-1], EDGE - 1, 0), (rows[count], count, count - 1)):
        packed = jnp.where(wide == slot, shifted(x, slot), packed)
        packed = jnp.where(wide == EDGE + slot, shifted(x, EDGE + slot - 127), packed)
        moved = jnp.where(wide == 32 + at, shifted(x, 32 + at), 0.0)
        moved = jnp.where(wide == 40 + at, shifted(x, 40 + at - 127), moved)
        packed = packed + fix * moved
    top_lane = lane[:8]
    for j in range(n_obs):
        w, west, east = spread(weight_ref[j], coeffs, lane)
        all_w = w + rest_ref[j]
        total = sum(all_w[r % EDGE : r % EDGE + 1, :] * x for r, x in rows.items())
        total += sum(w[r : r + 1, :] * x for r, x in tile_rows.items())
        packed = jnp.where(wide == 48 + j, packed + jnp.sum(total, axis=1, keepdims=True), packed)
        for k, column in ((1, west), (3, east)):
            meta = jnp.where(top_lane == WEIGHTS + k * n_obs + j, column[8:], meta)
    turned = jnp.concatenate([packed, jnp.zeros((128 - members, 128), F32)], axis=0).T
    out_ref[0:EDGE, :] = turned[0:EDGE] + shifted(turned[EDGE : 2 * EDGE], 64)
    out_ref[MID : MID + 8, :] = turned[32:40] + shifted(turned[40:48], 64)
    out_ref[OBS : OBS + 8, :] = turned[48:56] + meta


def block_rows(ref, start, tile, size, rows):
    return ref[pl.ds(pl.multiple_of(place_of(tile, size) * BLOCK + start, 8), rows), :]


def side_columns(ref, tile, size):
    west, east = jnp.maximum(tile - 1, 0), jnp.minimum(tile + 1, size - 1)
    own = block_rows(ref, 0, tile, size, EDGE)
    west_x = shifted(block_rows(ref, 0, west, size, EDGE), 64)
    east_x = block_rows(ref, 0, east, size, EDGE)
    west_mid = shifted(block_rows(ref, MID, west, size, 8), 64)
    west_mid += block_rows(ref, OBS, west, size, 8)[:, TO_EAST : TO_EAST + 1] * own[:8]
    east_mid = block_rows(ref, MID, east, size, 8)
    east_mid += block_rows(ref, OBS, east, size, 8)[:, TO_WEST : TO_WEST + 1] * shifted(own[:8], 64)
    return west_x, east_x, west_mid, east_mid


def complete(members, n_obs, size, blocks_ref, out_ref):
    lane = lanes((n_obs, 128))
    for tile in range(size):
        west, east, west_mid, east_mid = side_columns(blocks_ref, jnp.int32(tile), size)
        block = block_rows(blocks_ref, OBS, jnp.int32(tile), size, 8)
        terms = (west[:8], west[8:], east[:8], east[8:], west_mid, east_mid)
        added = []
        for j in range(n_obs):
            at = [WEIGHTS + k * n_obs + j for k in range(len(terms))]
            total = sum(block[:, a : a + 1] * term for a, term in zip(at, terms))
            added.append(jnp.sum(total, axis=0, keepdims=True))
        block = block[:n_obs]
        at = jnp.where(lane < members, block + jnp.concatenate(added, axis=0), 0.0)
        mean = jnp.sum(at, axis=1, keepdims=True) * (1.0 / members)
        raw = jnp.where(lane < members, at - mean, jnp.where(lane == members, block[:, VALUE : VALUE + 1] - mean, 0.0))
        out_ref[n_obs * tile : n_obs * (tile + 1), :] = raw * block[:, FACTOR : FACTOR + 1]


def forecast(members, count, size, field_ref, flow_ref, odd_ref, even_ref, blocks_ref, out_ref, mean_ref, tall_ref):
    north, south = halo_rows(even_ref, odd_ref, members)
    tile = lax.axis_index("gx")
    west, east, west_mid, east_mid = side_columns(blocks_ref, tile, size)
    has_west, has_east = tile > 0, tile < size - 1
    sides = [jnp.where(has_west, west, 0.0), jnp.where(has_east, east, 0.0)]
    sides += [jnp.where(has_west, west_mid, 0.0), jnp.where(has_east, east_mid, 0.0), jnp.zeros((80, 128), F32)]
    sides = jnp.concatenate(sides, axis=0).T[:members]
    field = tall_field(field_ref, north, south, members, count)
    tall = tall_coefficients(tall_ref, flow_ref, north[2], south[2], count)
    lane = lanes((members, 128))

    def step(rows, r, west_at, east_at):
        w = jnp.where(lane == 0, shifted(sides, -west_at), shifted(rows[r], 1))
        e = jnp.where(lane == 127, shifted(sides, 127 - east_at), shifted(rows[r], -1))
        at = r % EDGE
        return combine([c[at : at + 1, :] for c in tall], rows[r], rows[r - 1], rows[r + 1], w, e)

    middle = {r: step(field, r, r % EDGE, EDGE + r % EDGE) for r in range(-1, count + 1)}
    for r in range(count):
        x = step(middle, r, 2 * EDGE + r, 2 * EDGE + 8 + r)
        mean = jnp.sum(x, axis=0, keepdims=True) * (1.0 / members)
        mean_ref[r : r + 1, :] = mean
        x = x - mean
        high = x.astype(jnp.bfloat16)
        at = slice(128 * r, 128 * (r + 1))
        out_ref[0:members, at] = high
        out_ref[members : 2 * members, at] = (x - high.astype(F32)).astype(jnp.bfloat16)
        out_ref[2 * members :, at] = high


def eliminated(a, members):
    size = 8
    lane, sub = lanes((size, 128)), rows_of((size, 128))
    part = [a[size * q : size * (q + 1), :] for q in range(members // size)]
    pivot = []

    def spread(q, c):
        return jnp.broadcast_to(part[q][:, c : c + 1], (size, 128))

    ahead = {(0, c): spread(0, c) for c in range(size)}
    for p in range(len(part)):
        start, end = size * p, size * (p + 1)
        rest = range(p, len(part))
        column = {(q, c): spread(q, c) for q in rest[1:] for c in range(start, end)}
        column.update(ahead)
        more = range(end, end + size if p + 1 < len(part) else end)
        column.update({(q, c): spread(q, c) for q in rest[:2] for c in more})
        mine = (lane >= start) & (lane < end)
        for q in rest:
            part[q] = jnp.where(mine, 0.0, part[q])
        found = jnp.zeros((size, 128), F32)
        for j in range(size):
            at = start + j
            value = column[p, at][j : j + 1, :]
            found = jnp.where(sub == j, value, found)
            inverse = 1.0 / value
            unit = jnp.where(lane[:1] == at, 1.0, part[p][j : j + 1, :])
            pivots = {c: column[p, c][j : j + 1, :] for c in range(at + 1, end + len(more))}
            for q in rest:
                factor = column[q, at] * inverse
                for c in range(at + 1, end + (len(more) if q <= p + 1 else 0)):
                    column[q, c] = column[q, c] - factor * pivots[c]
                if q == p:
                    factor = jnp.where(sub > j, factor, 0.0)
                part[q] = part[q] - factor * unit
        pivot.append(found)
        ahead = {(p + 1, c): column[p + 1, c] for c in more}
    return jnp.concatenate(part, axis=0), jnp.concatenate(pivot, axis=0)


def analyse(members, count, f_ref, mean_ref, obs_ref, out_ref):
    scaled = obs_ref[...]
    full = lax.dot_general(
        scaled, scaled, (((0,), (0,)), ((), ())), precision=HIGHEST, preferred_element_type=F32
    )
    lane, sub = lanes((members, 128)), rows_of((members, 128))
    a, pivots = eliminated(full[:members, :] + jnp.where(lane == sub, members - 1.0, 0.0), members)
    scale = lax.rsqrt(pivots)
    inverse = scale * jnp.where(lane < sub, a, jnp.where(lane == sub, 1.0, 0.0))
    reduced = scale * a[:, members : members + 1]
    weights = jnp.sum(reduced * inverse, axis=0, keepdims=True)
    transform = (jnp.sqrt(members - 1.0) * inverse + weights)[:, :members]
    high = transform.astype(jnp.bfloat16)
    low = (transform - high.astype(F32)).astype(jnp.bfloat16)
    update = jnp.dot(jnp.concatenate([high, high, low], axis=1), f_ref[...], preferred_element_type=F32)
    for r in range(count):
        out_ref[pl.ds(r, members, stride=count), :] = update[:, 128 * r : 128 * (r + 1)] + mean_ref[r : r + 1, :]


def swap(x, axis, offset):
    ny, nx = lax.axis_size("gy"), lax.axis_size("gx")
    partner = {i: i for i in range(ny)}
    for i in range(offset, ny - 1, 2):
        partner[i], partner[i + 1] = i + 1, i
    pairs = []
    for a in range(ny):
        for b in range(nx):
            if partner[a] != a:
                pairs.append((a * nx + b, partner[a] * nx + b))
            elif nx % 2 == 0:
                pairs.append((a * nx + b, a * nx + (b ^ 1)))
    return lax.ppermute(x, ("gy", "gx"), pairs)


def two_power(size):
    return size & (size - 1) == 0


def doubled(x, flip_y, flip_x):
    ny, nx = lax.axis_size("gy"), lax.axis_size("gx")
    pairs = [(a * nx + b, (a ^ flip_y) * nx + (b ^ flip_x)) for a in range(ny) for b in range(nx)]
    return jnp.concatenate([x, lax.ppermute(x, ("gy", "gx"), pairs)], axis=0)


def row_blocks(block):
    size, step = lax.axis_size("gx"), 1
    if not two_power(size):
        return lax.all_gather(block, "gx", tiled=True)
    while step < size:
        block = doubled(block, 0, step | 1)
        step *= 2
    return block


def place_of(tile, size):
    if not two_power(size):
        return tile
    distance = jnp.bitwise_xor(lax.axis_index("gx"), tile)
    place, bit = distance, 2
    while bit < size:
        place = jnp.bitwise_xor(place, (distance // bit) % 2)
        bit *= 2
    return place


def all_rows(packet):
    step = lax.axis_size("gy")
    if not two_power(step):
        return lax.all_gather(packet, "gy", tiled=True)
    while step > 1:
        step //= 2
        packet = doubled(packet, step, 1 - lax.axis_size("gx") % 2)
    return packet


def body(ensemble, flow, obs_cell, obs_value, obs_var):
    members, count, width = ensemble.shape
    n_obs = obs_cell.shape[-1]
    size = lax.axis_size("gx")
    call = functools.partial(pl.pallas_call, compiler_params=PARAMS)

    def shape(*dims):
        return jax.ShapeDtypeStruct(dims + (width,), F32)

    inputs = [
        pltpu.with_memory_space_constraint(x, pltpu.HBM)
        for x in (ensemble, flow, obs_cell.reshape(-1), obs_value.reshape(-1), obs_var.reshape(-1))
    ]
    rows_even, rows_odd = call(
        functools.partial(load, members, count),
        out_shape=[shape(2 * members + 8)] * 2,
        in_specs=[HBM] * 2,
        out_specs=[VMEM] * 2,
        scratch_shapes=[pltpu.SemaphoreType.DMA((6,))],
        name="load",
    )(*inputs[:2])
    tall = pltpu.VMEM((3, EDGE, width), F32)
    field, tile_flow, *ready = call(
        functools.partial(prepare, members, count, n_obs),
        out_shape=[shape(members * count), shape(3, count), shape(members), shape(16)] + [shape(n_obs, EDGE)] * 2,
        in_specs=[HBM] * 5 + [ANY],
        out_specs=[VMEM] * 6,
        scratch_shapes=[pltpu.SMEM((n_obs,), jnp.int32)]
        + [pltpu.SMEM((n_obs,), F32)] * 2
        + [tall, pltpu.SemaphoreType.DMA((count + 4,))],
        cost_estimate=pl.CostEstimate(flops=4 * 10**6, bytes_accessed=6 * 10**5, transcendentals=0),
        name="prepare",
    )(*inputs, rows_even)
    rows_odd = swap(rows_odd, "gy", 1)
    rows_even = swap(rows_even, "gy", 0)
    block = call(
        functools.partial(observe, members, count, n_obs),
        out_shape=shape(BLOCK),
        in_specs=[VMEM] * 8,
        out_specs=VMEM,
        scratch_shapes=[tall],
        name="observe",
    )(field, tile_flow, *ready, rows_odd, rows_even)
    blocks = row_blocks(block)
    packet = call(
        functools.partial(complete, members, n_obs, size),
        out_shape=shape(n_obs * size),
        in_specs=[VMEM],
        out_specs=VMEM,
        name="complete",
    )(blocks)
    anomaly, mean = call(
        functools.partial(forecast, members, count, size),
        out_shape=[jax.ShapeDtypeStruct((3 * members, count * width), jnp.bfloat16), shape(count)],
        in_specs=[VMEM] * 5,
        out_specs=[VMEM] * 2,
        scratch_shapes=[tall],
        cost_estimate=pl.CostEstimate(flops=4 * 10**6, bytes_accessed=6 * 10**5, transcendentals=0),
        name="forecast",
    )(field, tile_flow, rows_odd, rows_even, blocks)
    out = call(
        functools.partial(analyse, members, count),
        out_shape=shape(members * count),
        in_specs=[VMEM] * 3,
        out_specs=VMEM,
        name="analyse",
    )(anomaly, mean, all_rows(packet))
    return out.reshape(ensemble.shape)


def solution(mesh):
    return jax.shard_map(
        body,
        mesh=mesh,
        in_specs=(
            P(None, "gy", "gx"),
            P(None, "gy", "gx"),
            P("gy", "gx", None),
            P("gy", "gx", None),
            P("gy", "gx", None),
        ),
        out_specs=P(None, "gy", "gx"),
        check_vma=False,
    )
```

```python
import functools

import jax
import jax.numpy as jnp
from jax import lax
from jax.experimental import pallas as pl
from jax.experimental.pallas import tpu as pltpu
from jax.sharding import PartitionSpec as P

F32 = jnp.float32
HIGHEST = lax.Precision.HIGHEST
PARAMS = pltpu.CompilerParams(vmem_limit_bytes=24 * 1024 * 1024)
VMEM = pl.BlockSpec(memory_space=pltpu.VMEM)
SMEM = pl.BlockSpec(memory_space=pltpu.SMEM)


def lanes(shape):
    return lax.broadcasted_iota(jnp.int32, shape, len(shape) - 1)


def rows_of(shape):
    return lax.broadcasted_iota(jnp.int32, shape, len(shape) - 2)


def shifted(x, amount):
    return pltpu.roll(x, amount % x.shape[-1], x.ndim - 1)


EDGE = 16
BLOCK = EDGE + 16
MID, OBS = EDGE, EDGE + 8
VALUE, FACTOR, TO_WEST, TO_EAST, WEIGHTS = 64, 65, 66, 67, 72
HBM = pl.BlockSpec(memory_space=pltpu.HBM)
ANY = pl.BlockSpec(memory_space=pl.ANY)
ORDER = (2, 3, 1)


def coefficients(k, u, v):
    return 1.0 - 4.0 * k, k + 0.5 * v, k - 0.5 * v, k + 0.5 * u, k - 0.5 * u


def combine(c, own, north, south, west, east):
    return c[0] * own + c[1] * north + c[2] * south + c[3] * west + c[4] * east


def transposed(x):
    return jnp.concatenate([x, jnp.zeros((128 - x.shape[0], 128), F32)], axis=0).T


def load(members, count, ens_hbm, flow_hbm, even_ref, odd_ref, sems):
    is_even = lax.axis_index("gy") % 2 == 0
    for ref in (even_ref, odd_ref):
        ref[2 * members :, :] = jnp.zeros((8, 128), F32)

    def copies(refs):
        for i, (ref, near, second) in enumerate(zip(refs, (count - 1, 0), (count - 2, 1))):
            yield pltpu.make_async_copy(ens_hbm.at[:, near, :], ref.at[pl.ds(0, members), :], sems.at[3 * i])
            yield pltpu.make_async_copy(ens_hbm.at[:, second, :], ref.at[pl.ds(members, members), :], sems.at[3 * i + 1])
            yield pltpu.make_async_copy(flow_hbm.at[:, near, :], ref.at[pl.ds(2 * members, 3), :], sems.at[3 * i + 2])

    def bring(refs):
        for copy in list(copies(refs)):
            copy.start()
        for copy in list(copies(refs)):
            copy.wait()

    pl.when(is_even)(lambda: bring((even_ref, odd_ref)))
    pl.when(jnp.logical_not(is_even))(lambda: bring((odd_ref, even_ref)))


def halo_rows(even_ref, odd_ref, members):
    at = lax.axis_index("gy")
    is_even = at % 2 == 0
    inside = at > 0, at < lax.axis_size("gy") - 1
    parts = []
    for lo, hi in ((0, members), (members, 2 * members), (2 * members, 2 * members + 3)):
        e, o = even_ref[lo:hi, :], odd_ref[lo:hi, :]
        pair = jnp.where(is_even, o, e), jnp.where(is_even, e, o)
        parts.append([jnp.where(here, x, 0.0) for here, x in zip(inside, pair)])
    return tuple(p[0] for p in parts), tuple(p[1] for p in parts)


def tall_coefficients(scratch, flow_ref, north_flow, south_flow, count):
    for k in range(3):
        scratch[k, 0:count, :] = flow_ref[k]
        scratch[k, count:, :] = jnp.zeros((EDGE - count, 128), F32)
        scratch[k, count : count + 1, :] = south_flow[k : k + 1]
        scratch[k, EDGE - 1 : EDGE, :] = north_flow[k : k + 1]
    return coefficients(*[scratch[k] for k in range(3)])


def tall_field(field_ref, north, south, members, count):
    field = {-2: north[1], -1: north[0], count: south[0], count + 1: south[1]}
    field.update({r: field_ref[r * members : (r + 1) * members, :] for r in range(count)})
    return field


def spread(w, coeffs, lane):
    own, up, down, left, right = coeffs
    to_west, to_east = left * w, right * w
    inside = (
        own * w
        + pltpu.roll(up * w, EDGE - 1, 0)
        + pltpu.roll(down * w, 1, 0)
        + jnp.where(lane == 127, 0.0, shifted(to_west, -1))
        + jnp.where(lane == 0, 0.0, shifted(to_east, 1))
    )
    has_west = lax.axis_index("gx") > 0
    has_east = lax.axis_index("gx") < lax.axis_size("gx") - 1
    return inside, jnp.where(has_west, to_west[:, 0:1], 0.0), jnp.where(has_east, to_east[:, 127:128], 0.0)


def prepare(
    members, count, n_obs, ens_hbm, flow_hbm, cell_hbm, value_hbm, var_hbm, sent_ref,
    field_ref, flow_ref, packed_ref, meta_ref, weight_ref, rest_ref, cell_ref, value_ref, var_ref, tall_ref, sems,
):
    copies = [
        pltpu.make_async_copy(ens_hbm.at[:, r, :], field_ref.at[pl.ds(r * members, members), :], sems.at[r])
        for r in range(count)
    ]
    pairs = ((flow_hbm, flow_ref), (cell_hbm, cell_ref), (value_hbm, value_ref), (var_hbm, var_ref))
    copies += [pltpu.make_async_copy(src, dst, sems.at[count + i]) for i, (src, dst) in enumerate(pairs)]
    for copy in copies:
        copy.start()
    for copy in copies:
        copy.wait()
    lane, sub = lanes((EDGE, 128)), rows_of((EDGE, 128))
    wide = lanes((members, 128))
    nothing = jnp.zeros((3, 128), F32)
    coeffs = tall_coefficients(tall_ref, flow_ref, nothing, nothing, count)
    coeffs = (jnp.where(sub < count, coeffs[0], 0.0),) + coeffs[1:]
    own, up, down, left, right = coeffs
    field = [field_ref[r * members : (r + 1) * members, :] for r in range(count)]
    packed = jnp.zeros((members, 128), F32)
    second = jnp.zeros((members, 128), F32)
    for r, x in enumerate(field):
        packed = jnp.where(wide == r, shifted(x, r), packed)
        packed = jnp.where(wide == EDGE + r, shifted(x, EDGE + r - 127), packed)
        second = jnp.where(wide == r, shifted(x, r - 1), second)
        second = jnp.where(wide == EDGE + r, shifted(x, EDGE + r - 126), second)

    def edge_row(low, high):
        both = jnp.where(lane == sub, low[:, 0:1], jnp.where(lane == sub + EDGE, high[:, 127:128], 0.0))
        return jnp.sum(both, axis=0, keepdims=True)

    middle = (
        edge_row(own, own) * packed
        + edge_row(up, up) * shifted(packed, 1)
        + edge_row(down, down) * shifted(packed, -1)
        + edge_row(right, left) * second
    )
    packed = jnp.where((wide >= 32) & (wide < 40), shifted(middle, 32), packed)
    packed = jnp.where((wide >= 40) & (wide < 48), shifted(middle, 24), packed)
    top_lane, top_sub = lane[:8], sub[:8]
    blocks = []
    for ref, rest in ((value_ref, 0.0), (var_ref, 1.0)):
        block = jnp.full((8, 128), rest, F32)
        for j in range(n_obs):
            block = jnp.where(top_sub == j, ref[j], block)
        blocks.append(block)
    meta = jnp.where(top_lane == VALUE, blocks[0], 0.0)
    meta = jnp.where(top_lane == FACTOR, lax.rsqrt(blocks[1]), meta)
    meta = jnp.where(top_lane == TO_WEST, left[:8, 0:1], meta)
    meta = jnp.where(top_lane == TO_EAST, right[:8, 127:128], meta)
    for j in range(n_obs):
        here = jnp.where((sub < count) & (sub * 128 + lane == cell_ref[j]), 1.0, 0.0)
        first, mid_west, mid_east = spread(here, coeffs, lane)
        w, west, east = spread(first, coeffs, lane)
        weight_ref[j] = first
        rest_ref[j] = w
        total = w[0:1, :] * field[0]
        for r in range(1, count):
            total = total + w[r : r + 1, :] * field[r]
        packed = jnp.where(wide == 48 + j, jnp.sum(total, axis=1, keepdims=True), packed)
        for k, column in ((0, west), (2, east), (4, mid_west), (5, mid_east)):
            meta = jnp.where(top_lane == WEIGHTS + k * n_obs + j, column[:8], meta)
    packed_ref[...] = packed
    meta_ref[0:8, :] = meta
    last = count - 1
    fix = jnp.zeros((8, 128), F32)
    for at, c, r, col in ((32, up, 0, 0), (40, up, 0, 127), (32 + last, down, last, 0), (40 + last, down, last, 127)):
        fix = jnp.where(top_lane == at, c[r : r + 1, col : col + 1], fix)
    meta_ref[8:16, :] = fix


def observe(
    members, count, n_obs, field_ref, flow_ref, packed_ref, meta_ref, weight_ref, rest_ref, odd_ref, even_ref,
    out_ref, tall_ref,
):
    north, south = halo_rows(even_ref, odd_ref, members)
    lane, sub = lanes((EDGE, 128)), rows_of((EDGE, 128))
    wide = lanes((members, 128))
    for k in range(3):
        tall_ref[k] = jnp.zeros((EDGE, 128), F32)
        tall_ref[k, count : count + 1, :] = south[2][k : k + 1]
        tall_ref[k, EDGE - 1 : EDGE, :] = north[2][k : k + 1]
    coeffs = coefficients(*[tall_ref[k] for k in range(3)])
    coeffs = (jnp.where((sub == count) | (sub == EDGE - 1), coeffs[0], 0.0),) + coeffs[1:]
    rows = {-2: north[1], -1: north[0], count: south[0], count + 1: south[1]}
    tile_rows = {r: field_ref[r * members : (r + 1) * members, :] for r in (0, count - 1)}
    packed, meta, fix = packed_ref[...], meta_ref[0:8, :], meta_ref[8:9, :]
    for x, slot, at in ((rows[-1], EDGE - 1, 0), (rows[count], count, count - 1)):
        packed = jnp.where(wide == slot, shifted(x, slot), packed)
        packed = jnp.where(wide == EDGE + slot, shifted(x, EDGE + slot - 127), packed)
        moved = jnp.where(wide == 32 + at, shifted(x, 32 + at), 0.0)
        moved = jnp.where(wide == 40 + at, shifted(x, 40 + at - 127), moved)
        packed = packed + fix * moved
    top_lane = lane[:8]
    for j in range(n_obs):
        w, west, east = spread(weight_ref[j], coeffs, lane)
        all_w = w + rest_ref[j]
        total = sum(all_w[r % EDGE : r % EDGE + 1, :] * x for r, x in rows.items())
        total += sum(w[r : r + 1, :] * x for r, x in tile_rows.items())
        packed = jnp.where(wide == 48 + j, packed + jnp.sum(total, axis=1, keepdims=True), packed)
        for k, column in ((1, west), (3, east)):
            meta = jnp.where(top_lane == WEIGHTS + k * n_obs + j, column[8:], meta)
    turned = jnp.concatenate([packed, jnp.zeros((128 - members, 128), F32)], axis=0).T
    out_ref[0:EDGE, :] = turned[0:EDGE] + shifted(turned[EDGE : 2 * EDGE], 64)
    out_ref[MID : MID + 8, :] = turned[32:40] + shifted(turned[40:48], 64)
    out_ref[OBS : OBS + 8, :] = turned[48:56] + meta


def block_rows(ref, start, tile, size, rows):
    return ref[pl.ds(pl.multiple_of(place_of(tile, size) * BLOCK + start, 8), rows), :]


def side_columns(ref, tile, size):
    west, east = jnp.maximum(tile - 1, 0), jnp.minimum(tile + 1, size - 1)
    own = block_rows(ref, 0, tile, size, EDGE)
    west_x = shifted(block_rows(ref, 0, west, size, EDGE), 64)
    east_x = block_rows(ref, 0, east, size, EDGE)
    west_mid = shifted(block_rows(ref, MID, west, size, 8), 64)
    west_mid += block_rows(ref, OBS, west, size, 8)[:, TO_EAST : TO_EAST + 1] * own[:8]
    east_mid = block_rows(ref, MID, east, size, 8)
    east_mid += block_rows(ref, OBS, east, size, 8)[:, TO_WEST : TO_WEST + 1] * shifted(own[:8], 64)
    return west_x, east_x, west_mid, east_mid


def complete(members, n_obs, size, blocks_ref, out_ref):
    lane = lanes((n_obs, 128))
    for tile in range(size):
        west, east, west_mid, east_mid = side_columns(blocks_ref, jnp.int32(tile), size)
        block = block_rows(blocks_ref, OBS, jnp.int32(tile), size, 8)
        terms = (west[:8], west[8:], east[:8], east[8:], west_mid, east_mid)
        added = []
        for j in range(n_obs):
            at = [WEIGHTS + k * n_obs + j for k in range(len(terms))]
            total = sum(block[:, a : a + 1] * term for a, term in zip(at, terms))
            added.append(jnp.sum(total, axis=0, keepdims=True))
        block = block[:n_obs]
        at = jnp.where(lane < members, block + jnp.concatenate(added, axis=0), 0.0)
        mean = jnp.sum(at, axis=1, keepdims=True) * (1.0 / members)
        raw = jnp.where(lane < members, at - mean, jnp.where(lane == members, block[:, VALUE : VALUE + 1] - mean, 0.0))
        out_ref[n_obs * tile : n_obs * (tile + 1), :] = raw * block[:, FACTOR : FACTOR + 1]


def forecast(members, count, size, field_ref, flow_ref, odd_ref, even_ref, blocks_ref, out_ref, mean_ref, tall_ref):
    north, south = halo_rows(even_ref, odd_ref, members)
    tile = lax.axis_index("gx")
    west, east, west_mid, east_mid = side_columns(blocks_ref, tile, size)
    has_west, has_east = tile > 0, tile < size - 1
    sides = [jnp.where(has_west, west, 0.0), jnp.where(has_east, east, 0.0)]
    sides += [jnp.where(has_west, west_mid, 0.0), jnp.where(has_east, east_mid, 0.0), jnp.zeros((80, 128), F32)]
    sides = jnp.concatenate(sides, axis=0).T[:members]
    field = tall_field(field_ref, north, south, members, count)
    tall = tall_coefficients(tall_ref, flow_ref, north[2], south[2], count)
    lane = lanes((members, 128))

    def step(rows, r, west_at, east_at):
        w = jnp.where(lane == 0, shifted(sides, -west_at), shifted(rows[r], 1))
        e = jnp.where(lane == 127, shifted(sides, 127 - east_at), shifted(rows[r], -1))
        at = r % EDGE
        return combine([c[at : at + 1, :] for c in tall], rows[r], rows[r - 1], rows[r + 1], w, e)

    middle = {r: step(field, r, r % EDGE, EDGE + r % EDGE) for r in range(-1, count + 1)}
    for r in range(count):
        x = step(middle, r, 2 * EDGE + r, 2 * EDGE + 8 + r)
        mean = jnp.sum(x, axis=0, keepdims=True) * (1.0 / members)
        mean_ref[r : r + 1, :] = mean
        x = x - mean
        high = x.astype(jnp.bfloat16)
        at = slice(128 * r, 128 * (r + 1))
        out_ref[0:members, at] = high
        out_ref[members : 2 * members, at] = (x - high.astype(F32)).astype(jnp.bfloat16)
        out_ref[2 * members :, at] = high


def eliminated(a, members):
    size = 8
    lane, sub = lanes((size, 128)), rows_of((size, 128))
    part = [a[size * q : size * (q + 1), :] for q in range(members // size)]
    pivot = []

    def spread(q, c):
        return jnp.broadcast_to(part[q][:, c : c + 1], (size, 128))

    ahead = {(0, c): spread(0, c) for c in range(size)}
    for p in range(len(part)):
        start, end = size * p, size * (p + 1)
        rest = range(p, len(part))
        column = {(q, c): spread(q, c) for q in rest[1:] for c in range(start, end)}
        column.update(ahead)
        more = range(end, end + size if p + 1 < len(part) else end)
        column.update({(q, c): spread(q, c) for q in rest[1:2] for c in more})
        mine = (lane >= start) & (lane < end)
        for q in rest:
            part[q] = jnp.where(mine, 0.0, part[q])
        found = jnp.zeros((size, 128), F32)
        for j in range(size):
            at = start + j
            value = column[p, at][j : j + 1, :]
            found = jnp.where(sub == j, value, found)
            inverse = 1.0 / value
            unit = jnp.where(lane[:1] == at, 1.0, part[p][j : j + 1, :])
            pivots = {c: column[p, c][j : j + 1, :] for c in range(at + 1, end)}
            pivots.update({c: column[p + 1, at][c - end : c - end + 1, :] for c in more})
            for q in rest:
                factor = column[q, at] * inverse
                for c in range(at + 1, end + (len(more) if q == p + 1 else 0)):
                    column[q, c] = column[q, c] - factor * pivots[c]
                if q == p:
                    factor = jnp.where(sub > j, factor, 0.0)
                part[q] = part[q] - factor * unit
        pivot.append(found)
        ahead = {(p + 1, c): column[p + 1, c] for c in more}
    return jnp.concatenate(part, axis=0), jnp.concatenate(pivot, axis=0)


def analyse(members, count, f_ref, mean_ref, *refs):
    out_ref = refs[-1]
    scaled = jnp.concatenate([ref[...] for ref in refs[:-1]], axis=0)
    full = lax.dot_general(
        scaled, scaled, (((0,), (0,)), ((), ())), precision=HIGHEST, preferred_element_type=F32
    )
    lane, sub = lanes((members, 128)), rows_of((members, 128))
    a, pivots = eliminated(full[:members, :] + jnp.where(lane == sub, members - 1.0, 0.0), members)
    scale = lax.rsqrt(pivots)
    inverse = scale * jnp.where(lane < sub, a, jnp.where(lane == sub, 1.0, 0.0))
    reduced = scale * a[:, members : members + 1]
    weights = jnp.sum(reduced * inverse, axis=0, keepdims=True)
    transform = (jnp.sqrt(members - 1.0) * inverse + weights)[:, :members]
    high = transform.astype(jnp.bfloat16)
    low = (transform - high.astype(F32)).astype(jnp.bfloat16)
    update = jnp.dot(jnp.concatenate([high, high, low], axis=1), f_ref[...], preferred_element_type=F32)
    for r in range(count):
        out_ref[pl.ds(r, members, stride=count), :] = update[:, 128 * r : 128 * (r + 1)] + mean_ref[r : r + 1, :]


def swap(x, axis, offset):
    ny, nx = lax.axis_size("gy"), lax.axis_size("gx")
    partner = {i: i for i in range(ny)}
    for i in range(offset, ny - 1, 2):
        partner[i], partner[i + 1] = i + 1, i
    pairs = []
    for a in range(ny):
        for b in range(nx):
            if partner[a] != a:
                pairs.append((a * nx + b, partner[a] * nx + b))
            elif nx % 2 == 0:
                pairs.append((a * nx + b, a * nx + (b ^ 1)))
    return lax.ppermute(x, ("gy", "gx"), pairs)


def two_power(size):
    return size & (size - 1) == 0


def partner(x, flip_y, flip_x):
    ny, nx = lax.axis_size("gy"), lax.axis_size("gx")
    pairs = [(a * nx + b, (a ^ flip_y) * nx + (b ^ flip_x)) for a in range(ny) for b in range(nx)]
    return lax.ppermute(x, ("gy", "gx"), pairs)


def doubled(x, flip_y, flip_x):
    return jnp.concatenate([x, partner(x, flip_y, flip_x)], axis=0)


def row_blocks(block):
    size, step = lax.axis_size("gx"), 1
    if not two_power(size):
        return lax.all_gather(block, "gx", tiled=True)
    while step < size:
        block = doubled(block, 0, step | 1)
        step *= 2
    return block


def place_of(tile, size):
    if not two_power(size):
        return tile
    distance = jnp.bitwise_xor(lax.axis_index("gx"), tile)
    place, bit = distance, 2
    while bit < size:
        place = jnp.bitwise_xor(place, (distance // bit) % 2)
        bit *= 2
    return place


def all_rows(packet):
    size = lax.axis_size("gy")
    if not two_power(size) or size < 4:
        return [lax.all_gather(packet, "gy", tiled=True)]
    flip_x = 1 - lax.axis_size("gx") % 2
    step = size // 2
    while step > 2:
        packet = doubled(packet, step, flip_x)
        step //= 2
    return [packet] + [partner(packet, flip_y, flip_x) for flip_y in ORDER]


def body(ensemble, flow, obs_cell, obs_value, obs_var):
    members, count, width = ensemble.shape
    n_obs = obs_cell.shape[-1]
    size = lax.axis_size("gx")
    call = functools.partial(pl.pallas_call, compiler_params=PARAMS)

    def shape(*dims):
        return jax.ShapeDtypeStruct(dims + (width,), F32)

    inputs = [
        pltpu.with_memory_space_constraint(x, pltpu.HBM)
        for x in (ensemble, flow, obs_cell.reshape(-1), obs_value.reshape(-1), obs_var.reshape(-1))
    ]
    rows_even, rows_odd = call(
        functools.partial(load, members, count),
        out_shape=[shape(2 * members + 8)] * 2,
        in_specs=[HBM] * 2,
        out_specs=[VMEM] * 2,
        scratch_shapes=[pltpu.SemaphoreType.DMA((6,))],
        name="load",
    )(*inputs[:2])
    tall = pltpu.VMEM((3, EDGE, width), F32)
    field, tile_flow, *ready = call(
        functools.partial(prepare, members, count, n_obs),
        out_shape=[shape(members * count), shape(3, count), shape(members), shape(16)] + [shape(n_obs, EDGE)] * 2,
        in_specs=[HBM] * 5 + [ANY],
        out_specs=[VMEM] * 6,
        scratch_shapes=[pltpu.SMEM((n_obs,), jnp.int32)]
        + [pltpu.SMEM((n_obs,), F32)] * 2
        + [tall, pltpu.SemaphoreType.DMA((count + 4,))],
        cost_estimate=pl.CostEstimate(flops=4 * 10**6, bytes_accessed=6 * 10**5, transcendentals=0),
        name="prepare",
    )(*inputs, rows_even)
    rows_odd = swap(rows_odd, "gy", 1)
    rows_even = swap(rows_even, "gy", 0)
    block = call(
        functools.partial(observe, members, count, n_obs),
        out_shape=shape(BLOCK),
        in_specs=[VMEM] * 8,
        out_specs=VMEM,
        scratch_shapes=[tall],
        name="observe",
    )(field, tile_flow, *ready, rows_odd, rows_even)
    blocks = row_blocks(block)
    packet = call(
        functools.partial(complete, members, n_obs, size),
        out_shape=shape(n_obs * size),
        in_specs=[VMEM],
        out_specs=VMEM,
        name="complete",
    )(blocks)
    anomaly, mean = call(
        functools.partial(forecast, members, count, size),
        out_shape=[jax.ShapeDtypeStruct((3 * members, count * width), jnp.bfloat16), shape(count)],
        in_specs=[VMEM] * 5,
        out_specs=[VMEM] * 2,
        scratch_shapes=[tall],
        cost_estimate=pl.CostEstimate(flops=4 * 10**6, bytes_accessed=6 * 10**5, transcendentals=0),
        name="forecast",
    )(field, tile_flow, rows_odd, rows_even, blocks)
    packets = all_rows(packet)
    out = call(
        functools.partial(analyse, members, count),
        out_shape=shape(members * count),
        in_specs=[VMEM] * (2 + len(packets)),
        out_specs=VMEM,
        name="analyse",
    )(anomaly, mean, *packets)
    return out.reshape(ensemble.shape)


def solution(mesh):
    return jax.shard_map(
        body,
        mesh=mesh,
        in_specs=(
            P(None, "gy", "gx"),
            P(None, "gy", "gx"),
            P("gy", "gx", None),
            P("gy", "gx", None),
            P("gy", "gx", None),
        ),
        out_specs=P(None, "gy", "gx"),
        check_vma=False,
    )
```

```python
import functools

import jax
import jax.numpy as jnp
from jax import lax
from jax.experimental import pallas as pl
from jax.experimental.pallas import tpu as pltpu
from jax.sharding import PartitionSpec as P

F32 = jnp.float32
HIGHEST = lax.Precision.HIGHEST
PARAMS = pltpu.CompilerParams(vmem_limit_bytes=24 * 1024 * 1024)
VMEM = pl.BlockSpec(memory_space=pltpu.VMEM)
SMEM = pl.BlockSpec(memory_space=pltpu.SMEM)


def lanes(shape):
    return lax.broadcasted_iota(jnp.int32, shape, len(shape) - 1)


def rows_of(shape):
    return lax.broadcasted_iota(jnp.int32, shape, len(shape) - 2)


def shifted(x, amount):
    return pltpu.roll(x, amount % x.shape[-1], x.ndim - 1)


EDGE = 16
BLOCK = EDGE + 16
MID, OBS = EDGE, EDGE + 8
VALUE, FACTOR, TO_WEST, TO_EAST, WEIGHTS = 64, 65, 66, 67, 72
HBM = pl.BlockSpec(memory_space=pltpu.HBM)
ANY = pl.BlockSpec(memory_space=pl.ANY)
ORDER = (2, 3, 1)


def coefficients(k, u, v):
    return 1.0 - 4.0 * k, k + 0.5 * v, k - 0.5 * v, k + 0.5 * u, k - 0.5 * u


def combine(c, own, north, south, west, east):
    return c[0] * own + c[1] * north + c[2] * south + c[3] * west + c[4] * east


def transposed(x):
    return jnp.concatenate([x, jnp.zeros((128 - x.shape[0], 128), F32)], axis=0).T


def load(members, count, ens_hbm, flow_hbm, even_ref, odd_ref, sems):
    is_even = lax.axis_index("gy") % 2 == 0
    for ref in (even_ref, odd_ref):
        ref[2 * members :, :] = jnp.zeros((8, 128), F32)

    def copies(refs):
        for i, (ref, near, second) in enumerate(zip(refs, (count - 1, 0), (count - 2, 1))):
            yield pltpu.make_async_copy(ens_hbm.at[:, near, :], ref.at[pl.ds(0, members), :], sems.at[3 * i])
            yield pltpu.make_async_copy(ens_hbm.at[:, second, :], ref.at[pl.ds(members, members), :], sems.at[3 * i + 1])
            yield pltpu.make_async_copy(flow_hbm.at[:, near, :], ref.at[pl.ds(2 * members, 3), :], sems.at[3 * i + 2])

    def bring(refs):
        for copy in list(copies(refs)):
            copy.start()
        for copy in list(copies(refs)):
            copy.wait()

    pl.when(is_even)(lambda: bring((even_ref, odd_ref)))
    pl.when(jnp.logical_not(is_even))(lambda: bring((odd_ref, even_ref)))


def halo_rows(even_ref, odd_ref, members):
    at = lax.axis_index("gy")
    is_even = at % 2 == 0
    inside = at > 0, at < lax.axis_size("gy") - 1
    parts = []
    for lo, hi in ((0, members), (members, 2 * members), (2 * members, 2 * members + 3)):
        e, o = even_ref[lo:hi, :], odd_ref[lo:hi, :]
        pair = jnp.where(is_even, o, e), jnp.where(is_even, e, o)
        parts.append([jnp.where(here, x, 0.0) for here, x in zip(inside, pair)])
    return tuple(p[0] for p in parts), tuple(p[1] for p in parts)


def tall_coefficients(scratch, flow_ref, north_flow, south_flow, count):
    for k in range(3):
        scratch[k, 0:count, :] = flow_ref[k]
        scratch[k, count:, :] = jnp.zeros((EDGE - count, 128), F32)
        scratch[k, count : count + 1, :] = south_flow[k : k + 1]
        scratch[k, EDGE - 1 : EDGE, :] = north_flow[k : k + 1]
    return coefficients(*[scratch[k] for k in range(3)])


def tall_field(field_ref, north, south, members, count):
    field = {-2: north[1], -1: north[0], count: south[0], count + 1: south[1]}
    field.update({r: field_ref[r * members : (r + 1) * members, :] for r in range(count)})
    return field


def spread(w, coeffs, lane):
    own, up, down, left, right = coeffs
    to_west, to_east = left * w, right * w
    inside = (
        own * w
        + pltpu.roll(up * w, EDGE - 1, 0)
        + pltpu.roll(down * w, 1, 0)
        + jnp.where(lane == 127, 0.0, shifted(to_west, -1))
        + jnp.where(lane == 0, 0.0, shifted(to_east, 1))
    )
    has_west = lax.axis_index("gx") > 0
    has_east = lax.axis_index("gx") < lax.axis_size("gx") - 1
    return inside, jnp.where(has_west, to_west[:, 0:1], 0.0), jnp.where(has_east, to_east[:, 127:128], 0.0)


def prepare(
    members, count, n_obs, ens_hbm, flow_hbm, cell_hbm, value_hbm, var_hbm, sent_ref,
    field_ref, flow_ref, packed_ref, meta_ref, weight_ref, rest_ref, cell_ref, value_ref, var_ref, tall_ref, sems,
):
    copies = [
        pltpu.make_async_copy(ens_hbm.at[:, r, :], field_ref.at[pl.ds(r * members, members), :], sems.at[r])
        for r in range(count)
    ]
    pairs = ((flow_hbm, flow_ref), (cell_hbm, cell_ref), (value_hbm, value_ref), (var_hbm, var_ref))
    copies += [pltpu.make_async_copy(src, dst, sems.at[count + i]) for i, (src, dst) in enumerate(pairs)]
    for copy in copies:
        copy.start()
    for copy in copies:
        copy.wait()
    lane, sub = lanes((EDGE, 128)), rows_of((EDGE, 128))
    wide = lanes((members, 128))
    nothing = jnp.zeros((3, 128), F32)
    coeffs = tall_coefficients(tall_ref, flow_ref, nothing, nothing, count)
    coeffs = (jnp.where(sub < count, coeffs[0], 0.0),) + coeffs[1:]
    own, up, down, left, right = coeffs
    field = [field_ref[r * members : (r + 1) * members, :] for r in range(count)]
    packed = jnp.zeros((members, 128), F32)
    second = jnp.zeros((members, 128), F32)
    for r, x in enumerate(field):
        packed = jnp.where(wide == r, shifted(x, r), packed)
        packed = jnp.where(wide == EDGE + r, shifted(x, EDGE + r - 127), packed)
        second = jnp.where(wide == r, shifted(x, r - 1), second)
        second = jnp.where(wide == EDGE + r, shifted(x, EDGE + r - 126), second)

    def edge_row(low, high):
        both = jnp.where(lane == sub, low[:, 0:1], jnp.where(lane == sub + EDGE, high[:, 127:128], 0.0))
        return jnp.sum(both, axis=0, keepdims=True)

    middle = (
        edge_row(own, own) * packed
        + edge_row(up, up) * shifted(packed, 1)
        + edge_row(down, down) * shifted(packed, -1)
        + edge_row(right, left) * second
    )
    packed = jnp.where((wide >= 32) & (wide < 40), shifted(middle, 32), packed)
    packed = jnp.where((wide >= 40) & (wide < 48), shifted(middle, 24), packed)
    top_lane, top_sub = lane[:8], sub[:8]
    blocks = []
    for ref, rest in ((value_ref, 0.0), (var_ref, 1.0)):
        block = jnp.full((8, 128), rest, F32)
        for j in range(n_obs):
            block = jnp.where(top_sub == j, ref[j], block)
        blocks.append(block)
    meta = jnp.where(top_lane == VALUE, blocks[0], 0.0)
    meta = jnp.where(top_lane == FACTOR, lax.rsqrt(blocks[1]), meta)
    meta = jnp.where(top_lane == TO_WEST, left[:8, 0:1], meta)
    meta = jnp.where(top_lane == TO_EAST, right[:8, 127:128], meta)
    for j in range(n_obs):
        here = jnp.where((sub < count) & (sub * 128 + lane == cell_ref[j]), 1.0, 0.0)
        first, mid_west, mid_east = spread(here, coeffs, lane)
        w, west, east = spread(first, coeffs, lane)
        weight_ref[j] = first
        rest_ref[j] = w
        total = w[0:1, :] * field[0]
        for r in range(1, count):
            total = total + w[r : r + 1, :] * field[r]
        packed = jnp.where(wide == 48 + j, jnp.sum(total, axis=1, keepdims=True), packed)
        for k, column in ((0, west), (2, east), (4, mid_west), (5, mid_east)):
            meta = jnp.where(top_lane == WEIGHTS + k * n_obs + j, column[:8], meta)
    packed_ref[...] = packed
    meta_ref[0:8, :] = meta
    last = count - 1
    fix = jnp.zeros((8, 128), F32)
    for at, c, r, col in ((32, up, 0, 0), (40, up, 0, 127), (32 + last, down, last, 0), (40 + last, down, last, 127)):
        fix = jnp.where(top_lane == at, c[r : r + 1, col : col + 1], fix)
    meta_ref[8:16, :] = fix


def observe(
    members, count, n_obs, field_ref, flow_ref, packed_ref, meta_ref, weight_ref, rest_ref, odd_ref, even_ref,
    out_ref, tall_ref,
):
    north, south = halo_rows(even_ref, odd_ref, members)
    lane, sub = lanes((EDGE, 128)), rows_of((EDGE, 128))
    wide = lanes((members, 128))
    for k in range(3):
        tall_ref[k] = jnp.zeros((EDGE, 128), F32)
        tall_ref[k, count : count + 1, :] = south[2][k : k + 1]
        tall_ref[k, EDGE - 1 : EDGE, :] = north[2][k : k + 1]
    coeffs = coefficients(*[tall_ref[k] for k in range(3)])
    coeffs = (jnp.where((sub == count) | (sub == EDGE - 1), coeffs[0], 0.0),) + coeffs[1:]
    rows = {-2: north[1], -1: north[0], count: south[0], count + 1: south[1]}
    tile_rows = {r: field_ref[r * members : (r + 1) * members, :] for r in (0, count - 1)}
    packed, meta, fix = packed_ref[...], meta_ref[0:8, :], meta_ref[8:9, :]
    for x, slot, at in ((rows[-1], EDGE - 1, 0), (rows[count], count, count - 1)):
        packed = jnp.where(wide == slot, shifted(x, slot), packed)
        packed = jnp.where(wide == EDGE + slot, shifted(x, EDGE + slot - 127), packed)
        moved = jnp.where(wide == 32 + at, shifted(x, 32 + at), 0.0)
        moved = jnp.where(wide == 40 + at, shifted(x, 40 + at - 127), moved)
        packed = packed + fix * moved
    top_lane = lane[:8]
    for j in range(n_obs):
        w, west, east = spread(weight_ref[j], coeffs, lane)
        all_w = w + rest_ref[j]
        total = sum(all_w[r % EDGE : r % EDGE + 1, :] * x for r, x in rows.items())
        total += sum(w[r : r + 1, :] * x for r, x in tile_rows.items())
        packed = jnp.where(wide == 48 + j, packed + jnp.sum(total, axis=1, keepdims=True), packed)
        for k, column in ((1, west), (3, east)):
            meta = jnp.where(top_lane == WEIGHTS + k * n_obs + j, column[8:], meta)
    turned = jnp.concatenate([packed, jnp.zeros((128 - members, 128), F32)], axis=0).T
    out_ref[0:EDGE, :] = turned[0:EDGE] + shifted(turned[EDGE : 2 * EDGE], 64)
    out_ref[MID : MID + 8, :] = turned[32:40] + shifted(turned[40:48], 64)
    out_ref[OBS : OBS + 8, :] = turned[48:56] + meta


def block_rows(ref, start, tile, size, rows):
    return ref[pl.ds(pl.multiple_of(place_of(tile, size) * BLOCK + start, 8), rows), :]


def side_columns(ref, tile, size):
    west, east = jnp.maximum(tile - 1, 0), jnp.minimum(tile + 1, size - 1)
    own = block_rows(ref, 0, tile, size, EDGE)
    west_x = shifted(block_rows(ref, 0, west, size, EDGE), 64)
    east_x = block_rows(ref, 0, east, size, EDGE)
    west_mid = shifted(block_rows(ref, MID, west, size, 8), 64)
    west_mid += block_rows(ref, OBS, west, size, 8)[:, TO_EAST : TO_EAST + 1] * own[:8]
    east_mid = block_rows(ref, MID, east, size, 8)
    east_mid += block_rows(ref, OBS, east, size, 8)[:, TO_WEST : TO_WEST + 1] * shifted(own[:8], 64)
    return west_x, east_x, west_mid, east_mid


def complete(members, n_obs, size, blocks_ref, out_ref):
    lane = lanes((n_obs, 128))
    for tile in range(size):
        west, east, west_mid, east_mid = side_columns(blocks_ref, jnp.int32(tile), size)
        block = block_rows(blocks_ref, OBS, jnp.int32(tile), size, 8)
        terms = (west[:8], west[8:], east[:8], east[8:], west_mid, east_mid)
        added = []
        for j in range(n_obs):
            at = [WEIGHTS + k * n_obs + j for k in range(len(terms))]
            total = sum(block[:, a : a + 1] * term for a, term in zip(at, terms))
            added.append(jnp.sum(total, axis=0, keepdims=True))
        block = block[:n_obs]
        at = jnp.where(lane < members, block + jnp.concatenate(added, axis=0), 0.0)
        mean = jnp.sum(at, axis=1, keepdims=True) * (1.0 / members)
        raw = jnp.where(lane < members, at - mean, jnp.where(lane == members, block[:, VALUE : VALUE + 1] - mean, 0.0))
        out_ref[n_obs * tile : n_obs * (tile + 1), :] = raw * block[:, FACTOR : FACTOR + 1]


def forecast(members, count, size, field_ref, flow_ref, odd_ref, even_ref, blocks_ref, out_ref, mean_ref, tall_ref):
    north, south = halo_rows(even_ref, odd_ref, members)
    tile = lax.axis_index("gx")
    west, east, west_mid, east_mid = side_columns(blocks_ref, tile, size)
    has_west, has_east = tile > 0, tile < size - 1
    sides = [jnp.where(has_west, west, 0.0), jnp.where(has_east, east, 0.0)]
    sides += [jnp.where(has_west, west_mid, 0.0), jnp.where(has_east, east_mid, 0.0), jnp.zeros((80, 128), F32)]
    sides = jnp.concatenate(sides, axis=0).T[:members]
    field = tall_field(field_ref, north, south, members, count)
    tall = tall_coefficients(tall_ref, flow_ref, north[2], south[2], count)
    lane = lanes((members, 128))

    def step(rows, r, west_at, east_at):
        w = jnp.where(lane == 0, shifted(sides, -west_at), shifted(rows[r], 1))
        e = jnp.where(lane == 127, shifted(sides, 127 - east_at), shifted(rows[r], -1))
        at = r % EDGE
        return combine([c[at : at + 1, :] for c in tall], rows[r], rows[r - 1], rows[r + 1], w, e)

    middle = {r: step(field, r, r % EDGE, EDGE + r % EDGE) for r in range(-1, count + 1)}
    for r in range(count):
        x = step(middle, r, 2 * EDGE + r, 2 * EDGE + 8 + r)
        mean = jnp.sum(x, axis=0, keepdims=True) * (1.0 / members)
        mean_ref[r : r + 1, :] = mean
        x = x - mean
        high = x.astype(jnp.bfloat16)
        at = slice(128 * r, 128 * (r + 1))
        out_ref[0:members, at] = high
        out_ref[members : 2 * members, at] = (x - high.astype(F32)).astype(jnp.bfloat16)
        out_ref[2 * members :, at] = high


def eliminated(a, members):
    size = 8
    lane, sub = lanes((size, 128)), rows_of((size, 128))
    part = [a[size * q : size * (q + 1), :] for q in range(members // size)]
    pivot = []

    def spread(q, c):
        return jnp.broadcast_to(part[q][:, c : c + 1], (size, 128))

    ahead = {(0, c): spread(0, c) for c in range(size)}
    for p in range(len(part)):
        start, end = size * p, size * (p + 1)
        rest = range(p, len(part))
        column = {(q, c): spread(q, c) for q in rest[1:] for c in range(start, end)}
        column.update(ahead)
        more = range(end, end + size if p + 1 < len(part) else end)
        column.update({(q, c): spread(q, c) for q in rest[1:2] for c in more})
        mine = (lane >= start) & (lane < end)
        for q in rest:
            part[q] = jnp.where(mine, 0.0, part[q])
        found = jnp.zeros((size, 128), F32)
        for j in range(size):
            at = start + j
            value = column[p, at][j : j + 1, :]
            found = jnp.where(sub == j, value, found)
            inverse = 1.0 / value
            unit = jnp.where(lane[:1] == at, 1.0, part[p][j : j + 1, :])
            pivots = {c: column[p, c][j : j + 1, :] for c in range(at + 1, end)}
            pivots.update({c: column[p + 1, at][c - end : c - end + 1, :] for c in more})
            for q in rest:
                factor = column[q, at] * inverse
                for c in range(at + 1, end + (len(more) if q == p + 1 else 0)):
                    column[q, c] = column[q, c] - factor * pivots[c]
                if q == p:
                    factor = jnp.where(sub > j, factor, 0.0)
                part[q] = part[q] - factor * unit
        pivot.append(found)
        ahead = {(p + 1, c): column[p + 1, c] for c in more}
    return jnp.concatenate(part, axis=0), jnp.concatenate(pivot, axis=0)


def analyse(members, count, f_ref, mean_ref, *refs):
    out_ref = refs[-1]
    scaled = jnp.concatenate([ref[...] for ref in refs[:-1]], axis=0)
    full = lax.dot_general(
        scaled, scaled, (((0,), (0,)), ((), ())), precision=HIGHEST, preferred_element_type=F32
    )
    lane, sub = lanes((members, 128)), rows_of((members, 128))
    a, pivots = eliminated(full[:members, :] + jnp.where(lane == sub, members - 1.0, 0.0), members)
    scale = lax.rsqrt(pivots)
    inverse = scale * jnp.where(lane < sub, a, jnp.where(lane == sub, 1.0, 0.0))
    reduced = scale * a[:, members : members + 1]
    weights = jnp.sum(reduced * inverse, axis=0, keepdims=True)
    transform = (jnp.sqrt(members - 1.0) * inverse + weights)[:, :members]
    high = transform.astype(jnp.bfloat16)
    low = (transform - high.astype(F32)).astype(jnp.bfloat16)
    update = jnp.dot(jnp.concatenate([high, high, low], axis=1), f_ref[...], preferred_element_type=F32)
    for r in range(count):
        out_ref[pl.ds(r, members, stride=count), :] = update[:, 128 * r : 128 * (r + 1)] + mean_ref[r : r + 1, :]


def swap(x, axis, offset):
    ny, nx = lax.axis_size("gy"), lax.axis_size("gx")
    partner = {i: i for i in range(ny)}
    for i in range(offset, ny - 1, 2):
        partner[i], partner[i + 1] = i + 1, i
    pairs = []
    for a in range(ny):
        for b in range(nx):
            if partner[a] != a:
                pairs.append((a * nx + b, partner[a] * nx + b))
            elif nx % 2 == 0:
                pairs.append((a * nx + b, a * nx + (b ^ 1)))
    return lax.ppermute(x, ("gy", "gx"), pairs)


def two_power(size):
    return size & (size - 1) == 0


def partner(x, flip_y, flip_x):
    ny, nx = lax.axis_size("gy"), lax.axis_size("gx")
    pairs = [(a * nx + b, (a ^ flip_y) * nx + (b ^ flip_x)) for a in range(ny) for b in range(nx)]
    return lax.ppermute(x, ("gy", "gx"), pairs)


def stack(x_ref, other_ref, *refs):
    out_ref = refs[-1]
    out_ref[: x_ref.shape[0], :] = x_ref[...]
    out_ref[x_ref.shape[0] :, :] = other_ref[...]


def doubled(x, flip_y, flip_x, *before):
    other = partner(x, flip_y, flip_x)
    if not before:
        return jnp.concatenate([x, other], axis=0)
    return pl.pallas_call(
        stack,
        out_shape=jax.ShapeDtypeStruct((2 * x.shape[0], x.shape[1]), x.dtype),
        in_specs=[VMEM] * 2 + [ANY] * len(before),
        out_specs=VMEM,
        compiler_params=PARAMS,
        name="stack",
    )(x, other, *before)


def row_blocks(block):
    size, step = lax.axis_size("gx"), 1
    if not two_power(size):
        return lax.all_gather(block, "gx", tiled=True)
    while step < size:
        block = doubled(block, 0, step | 1)
        step *= 2
    return block


def place_of(tile, size):
    if not two_power(size):
        return tile
    distance = jnp.bitwise_xor(lax.axis_index("gx"), tile)
    place, bit = distance, 2
    while bit < size:
        place = jnp.bitwise_xor(place, (distance // bit) % 2)
        bit *= 2
    return place


def all_rows(packet, beside):
    size = lax.axis_size("gy")
    if not two_power(size) or size < 4:
        return [lax.all_gather(packet, "gy", tiled=True)]
    flip_x = 1 - lax.axis_size("gx") % 2
    step = size // 2
    while step > 2:
        packet = doubled(packet, step, flip_x, *([beside] if 2 * step == size else []))
        step //= 2
    return [packet] + [partner(packet, flip_y, flip_x) for flip_y in ORDER]


def body(ensemble, flow, obs_cell, obs_value, obs_var):
    members, count, width = ensemble.shape
    n_obs = obs_cell.shape[-1]
    size = lax.axis_size("gx")
    call = functools.partial(pl.pallas_call, compiler_params=PARAMS)

    def shape(*dims):
        return jax.ShapeDtypeStruct(dims + (width,), F32)

    inputs = [
        pltpu.with_memory_space_constraint(x, pltpu.HBM)
        for x in (ensemble, flow, obs_cell.reshape(-1), obs_value.reshape(-1), obs_var.reshape(-1))
    ]
    rows_even, rows_odd = call(
        functools.partial(load, members, count),
        out_shape=[shape(2 * members + 8)] * 2,
        in_specs=[HBM] * 2,
        out_specs=[VMEM] * 2,
        scratch_shapes=[pltpu.SemaphoreType.DMA((6,))],
        name="load",
    )(*inputs[:2])
    tall = pltpu.VMEM((3, EDGE, width), F32)
    field, tile_flow, *ready = call(
        functools.partial(prepare, members, count, n_obs),
        out_shape=[shape(members * count), shape(3, count), shape(members), shape(16)] + [shape(n_obs, EDGE)] * 2,
        in_specs=[HBM] * 5 + [ANY],
        out_specs=[VMEM] * 6,
        scratch_shapes=[pltpu.SMEM((n_obs,), jnp.int32)]
        + [pltpu.SMEM((n_obs,), F32)] * 2
        + [tall, pltpu.SemaphoreType.DMA((count + 4,))],
        cost_estimate=pl.CostEstimate(flops=4 * 10**6, bytes_accessed=6 * 10**5, transcendentals=0),
        name="prepare",
    )(*inputs, rows_even)
    rows_odd = swap(rows_odd, "gy", 1)
    rows_even = swap(rows_even, "gy", 0)
    block = call(
        functools.partial(observe, members, count, n_obs),
        out_shape=shape(BLOCK),
        in_specs=[VMEM] * 8,
        out_specs=VMEM,
        scratch_shapes=[tall],
        name="observe",
    )(field, tile_flow, *ready, rows_odd, rows_even)
    blocks = row_blocks(block)
    packet = call(
        functools.partial(complete, members, n_obs, size),
        out_shape=shape(n_obs * size),
        in_specs=[VMEM],
        out_specs=VMEM,
        name="complete",
    )(blocks)
    anomaly, mean = call(
        functools.partial(forecast, members, count, size),
        out_shape=[jax.ShapeDtypeStruct((3 * members, count * width), jnp.bfloat16), shape(count)],
        in_specs=[VMEM] * 5,
        out_specs=[VMEM] * 2,
        scratch_shapes=[tall],
        cost_estimate=pl.CostEstimate(flops=4 * 10**6, bytes_accessed=6 * 10**5, transcendentals=0),
        name="forecast",
    )(field, tile_flow, rows_odd, rows_even, blocks)
    packets = all_rows(packet, anomaly)
    out = call(
        functools.partial(analyse, members, count),
        out_shape=shape(members * count),
        in_specs=[VMEM] * (2 + len(packets)),
        out_specs=VMEM,
        name="analyse",
    )(anomaly, mean, *packets)
    return out.reshape(ensemble.shape)


def solution(mesh):
    return jax.shard_map(
        body,
        mesh=mesh,
        in_specs=(
            P(None, "gy", "gx"),
            P(None, "gy", "gx"),
            P("gy", "gx", None),
            P("gy", "gx", None),
            P("gy", "gx", None),
        ),
        out_specs=P(None, "gy", "gx"),
        check_vma=False,
    )
```

```python
import functools

import jax
import jax.numpy as jnp
from jax import lax
from jax.experimental import pallas as pl
from jax.experimental.pallas import tpu as pltpu
from jax.sharding import PartitionSpec as P

F32 = jnp.float32
HIGHEST = lax.Precision.HIGHEST
PARAMS = pltpu.CompilerParams(vmem_limit_bytes=24 * 1024 * 1024)
VMEM = pl.BlockSpec(memory_space=pltpu.VMEM)
SMEM = pl.BlockSpec(memory_space=pltpu.SMEM)


def lanes(shape):
    return lax.broadcasted_iota(jnp.int32, shape, len(shape) - 1)


def rows_of(shape):
    return lax.broadcasted_iota(jnp.int32, shape, len(shape) - 2)


def shifted(x, amount):
    return pltpu.roll(x, amount % x.shape[-1], x.ndim - 1)


EDGE = 16
BLOCK = EDGE + 16
MID, OBS = EDGE, EDGE + 8
VALUE, FACTOR, TO_WEST, TO_EAST, WEIGHTS = 64, 65, 66, 67, 72
HBM = pl.BlockSpec(memory_space=pltpu.HBM)
ANY = pl.BlockSpec(memory_space=pl.ANY)
ORDER = (2, 3, 1)


def coefficients(k, u, v):
    return 1.0 - 4.0 * k, k + 0.5 * v, k - 0.5 * v, k + 0.5 * u, k - 0.5 * u


def combine(c, own, north, south, west, east):
    return c[0] * own + c[1] * north + c[2] * south + c[3] * west + c[4] * east


def transposed(x):
    return jnp.concatenate([x, jnp.zeros((128 - x.shape[0], 128), F32)], axis=0).T


def load(members, count, ens_hbm, flow_hbm, even_ref, odd_ref, sems):
    is_even = lax.axis_index("gy") % 2 == 0
    for ref in (even_ref, odd_ref):
        ref[2 * members :, :] = jnp.zeros((8, 128), F32)

    def copies(refs):
        for i, (ref, near, second) in enumerate(zip(refs, (count - 1, 0), (count - 2, 1))):
            yield pltpu.make_async_copy(ens_hbm.at[:, near, :], ref.at[pl.ds(0, members), :], sems.at[3 * i])
            yield pltpu.make_async_copy(ens_hbm.at[:, second, :], ref.at[pl.ds(members, members), :], sems.at[3 * i + 1])
            yield pltpu.make_async_copy(flow_hbm.at[:, near, :], ref.at[pl.ds(2 * members, 3), :], sems.at[3 * i + 2])

    def bring(refs):
        for copy in list(copies(refs)):
            copy.start()
        for copy in list(copies(refs)):
            copy.wait()

    pl.when(is_even)(lambda: bring((even_ref, odd_ref)))
    pl.when(jnp.logical_not(is_even))(lambda: bring((odd_ref, even_ref)))


def halo_rows(even_ref, odd_ref, members):
    at = lax.axis_index("gy")
    is_even = at % 2 == 0
    inside = at > 0, at < lax.axis_size("gy") - 1
    parts = []
    for lo, hi in ((0, members), (members, 2 * members), (2 * members, 2 * members + 3)):
        e, o = even_ref[lo:hi, :], odd_ref[lo:hi, :]
        pair = jnp.where(is_even, o, e), jnp.where(is_even, e, o)
        parts.append([jnp.where(here, x, 0.0) for here, x in zip(inside, pair)])
    return tuple(p[0] for p in parts), tuple(p[1] for p in parts)


def tall_coefficients(scratch, flow_ref, north_flow, south_flow, count):
    for k in range(3):
        scratch[k, 0:count, :] = flow_ref[k]
        scratch[k, count:, :] = jnp.zeros((EDGE - count, 128), F32)
        scratch[k, count : count + 1, :] = south_flow[k : k + 1]
        scratch[k, EDGE - 1 : EDGE, :] = north_flow[k : k + 1]
    return coefficients(*[scratch[k] for k in range(3)])


def tall_field(field_ref, north, south, members, count):
    field = {-2: north[1], -1: north[0], count: south[0], count + 1: south[1]}
    field.update({r: field_ref[r * members : (r + 1) * members, :] for r in range(count)})
    return field


def spread(w, coeffs, lane):
    own, up, down, left, right = coeffs
    to_west, to_east = left * w, right * w
    inside = (
        own * w
        + pltpu.roll(up * w, EDGE - 1, 0)
        + pltpu.roll(down * w, 1, 0)
        + jnp.where(lane == 127, 0.0, shifted(to_west, -1))
        + jnp.where(lane == 0, 0.0, shifted(to_east, 1))
    )
    has_west = lax.axis_index("gx") > 0
    has_east = lax.axis_index("gx") < lax.axis_size("gx") - 1
    return inside, jnp.where(has_west, to_west[:, 0:1], 0.0), jnp.where(has_east, to_east[:, 127:128], 0.0)


def prepare(
    members, count, n_obs, ens_hbm, flow_hbm, cell_hbm, value_hbm, var_hbm, sent_ref,
    field_ref, flow_ref, packed_ref, meta_ref, weight_ref, rest_ref, cell_ref, value_ref, var_ref, tall_ref, sems,
):
    copies = [
        pltpu.make_async_copy(ens_hbm.at[:, r, :], field_ref.at[pl.ds(r * members, members), :], sems.at[r])
        for r in range(count)
    ]
    pairs = ((flow_hbm, flow_ref), (cell_hbm, cell_ref), (value_hbm, value_ref), (var_hbm, var_ref))
    copies += [pltpu.make_async_copy(src, dst, sems.at[count + i]) for i, (src, dst) in enumerate(pairs)]
    for copy in copies:
        copy.start()
    for copy in copies:
        copy.wait()
    lane, sub = lanes((EDGE, 128)), rows_of((EDGE, 128))
    wide = lanes((members, 128))
    nothing = jnp.zeros((3, 128), F32)
    coeffs = tall_coefficients(tall_ref, flow_ref, nothing, nothing, count)
    coeffs = (jnp.where(sub < count, coeffs[0], 0.0),) + coeffs[1:]
    own, up, down, left, right = coeffs
    field = [field_ref[r * members : (r + 1) * members, :] for r in range(count)]
    packed = jnp.zeros((members, 128), F32)
    second = jnp.zeros((members, 128), F32)
    for r, x in enumerate(field):
        packed = jnp.where(wide == r, shifted(x, r), packed)
        packed = jnp.where(wide == EDGE + r, shifted(x, EDGE + r - 127), packed)
        second = jnp.where(wide == r, shifted(x, r - 1), second)
        second = jnp.where(wide == EDGE + r, shifted(x, EDGE + r - 126), second)

    def edge_row(low, high):
        both = jnp.where(lane == sub, low[:, 0:1], jnp.where(lane == sub + EDGE, high[:, 127:128], 0.0))
        return jnp.sum(both, axis=0, keepdims=True)

    middle = (
        edge_row(own, own) * packed
        + edge_row(up, up) * shifted(packed, 1)
        + edge_row(down, down) * shifted(packed, -1)
        + edge_row(right, left) * second
    )
    packed = jnp.where((wide >= 32) & (wide < 40), shifted(middle, 32), packed)
    packed = jnp.where((wide >= 40) & (wide < 48), shifted(middle, 24), packed)
    top_lane, top_sub = lane[:8], sub[:8]
    blocks = []
    for ref, rest in ((value_ref, 0.0), (var_ref, 1.0)):
        block = jnp.full((8, 128), rest, F32)
        for j in range(n_obs):
            block = jnp.where(top_sub == j, ref[j], block)
        blocks.append(block)
    meta = jnp.where(top_lane == VALUE, blocks[0], 0.0)
    meta = jnp.where(top_lane == FACTOR, lax.rsqrt(blocks[1]), meta)
    meta = jnp.where(top_lane == TO_WEST, left[:8, 0:1], meta)
    meta = jnp.where(top_lane == TO_EAST, right[:8, 127:128], meta)
    for j in range(n_obs):
        here = jnp.where((sub < count) & (sub * 128 + lane == cell_ref[j]), 1.0, 0.0)
        first, mid_west, mid_east = spread(here, coeffs, lane)
        w, west, east = spread(first, coeffs, lane)
        weight_ref[j] = first
        rest_ref[j] = w
        total = w[0:1, :] * field[0]
        for r in range(1, count):
            total = total + w[r : r + 1, :] * field[r]
        packed = jnp.where(wide == 48 + j, jnp.sum(total, axis=1, keepdims=True), packed)
        for k, column in ((0, west), (2, east), (4, mid_west), (5, mid_east)):
            meta = jnp.where(top_lane == WEIGHTS + k * n_obs + j, column[:8], meta)
    packed_ref[...] = packed
    meta_ref[0:8, :] = meta
    last = count - 1
    fix = jnp.zeros((8, 128), F32)
    for at, c, r, col in ((32, up, 0, 0), (40, up, 0, 127), (32 + last, down, last, 0), (40 + last, down, last, 127)):
        fix = jnp.where(top_lane == at, c[r : r + 1, col : col + 1], fix)
    meta_ref[8:16, :] = fix


def observe(
    members, count, n_obs, field_ref, flow_ref, packed_ref, meta_ref, weight_ref, rest_ref, odd_ref, even_ref,
    out_ref, tall_ref,
):
    north, south = halo_rows(even_ref, odd_ref, members)
    lane, sub = lanes((EDGE, 128)), rows_of((EDGE, 128))
    wide = lanes((members, 128))
    for k in range(3):
        tall_ref[k] = jnp.zeros((EDGE, 128), F32)
        tall_ref[k, count : count + 1, :] = south[2][k : k + 1]
        tall_ref[k, EDGE - 1 : EDGE, :] = north[2][k : k + 1]
    coeffs = coefficients(*[tall_ref[k] for k in range(3)])
    coeffs = (jnp.where((sub == count) | (sub == EDGE - 1), coeffs[0], 0.0),) + coeffs[1:]
    rows = {-2: north[1], -1: north[0], count: south[0], count + 1: south[1]}
    tile_rows = {r: field_ref[r * members : (r + 1) * members, :] for r in (0, count - 1)}
    packed, meta, fix = packed_ref[...], meta_ref[0:8, :], meta_ref[8:9, :]
    for x, slot, at in ((rows[-1], EDGE - 1, 0), (rows[count], count, count - 1)):
        packed = jnp.where(wide == slot, shifted(x, slot), packed)
        packed = jnp.where(wide == EDGE + slot, shifted(x, EDGE + slot - 127), packed)
        moved = jnp.where(wide == 32 + at, shifted(x, 32 + at), 0.0)
        moved = jnp.where(wide == 40 + at, shifted(x, 40 + at - 127), moved)
        packed = packed + fix * moved
    top_lane = lane[:8]
    for j in range(n_obs):
        w, west, east = spread(weight_ref[j], coeffs, lane)
        all_w = w + rest_ref[j]
        total = sum(all_w[r % EDGE : r % EDGE + 1, :] * x for r, x in rows.items())
        total += sum(w[r : r + 1, :] * x for r, x in tile_rows.items())
        packed = jnp.where(wide == 48 + j, packed + jnp.sum(total, axis=1, keepdims=True), packed)
        for k, column in ((1, west), (3, east)):
            meta = jnp.where(top_lane == WEIGHTS + k * n_obs + j, column[8:], meta)
    turned = jnp.concatenate([packed, jnp.zeros((128 - members, 128), F32)], axis=0).T
    out_ref[0:EDGE, :] = turned[0:EDGE] + shifted(turned[EDGE : 2 * EDGE], 64)
    out_ref[MID : MID + 8, :] = turned[32:40] + shifted(turned[40:48], 64)
    out_ref[OBS : OBS + 8, :] = turned[48:56] + meta


def block_rows(ref, start, tile, size, rows):
    return ref[pl.ds(pl.multiple_of(place_of(tile, size) * BLOCK + start, 8), rows), :]


def side_columns(ref, tile, size):
    west, east = jnp.maximum(tile - 1, 0), jnp.minimum(tile + 1, size - 1)
    own = block_rows(ref, 0, tile, size, EDGE)
    west_x = shifted(block_rows(ref, 0, west, size, EDGE), 64)
    east_x = block_rows(ref, 0, east, size, EDGE)
    west_mid = shifted(block_rows(ref, MID, west, size, 8), 64)
    west_mid += block_rows(ref, OBS, west, size, 8)[:, TO_EAST : TO_EAST + 1] * own[:8]
    east_mid = block_rows(ref, MID, east, size, 8)
    east_mid += block_rows(ref, OBS, east, size, 8)[:, TO_WEST : TO_WEST + 1] * shifted(own[:8], 64)
    return west_x, east_x, west_mid, east_mid


def complete(members, n_obs, size, blocks_ref, out_ref):
    lane = lanes((n_obs, 128))
    for tile in range(size):
        west, east, west_mid, east_mid = side_columns(blocks_ref, jnp.int32(tile), size)
        block = block_rows(blocks_ref, OBS, jnp.int32(tile), size, 8)
        terms = (west[:8], west[8:], east[:8], east[8:], west_mid, east_mid)
        added = []
        for j in range(n_obs):
            at = [WEIGHTS + k * n_obs + j for k in range(len(terms))]
            total = sum(block[:, a : a + 1] * term for a, term in zip(at, terms))
            added.append(jnp.sum(total, axis=0, keepdims=True))
        block = block[:n_obs]
        at = jnp.where(lane < members, block + jnp.concatenate(added, axis=0), 0.0)
        mean = jnp.sum(at, axis=1, keepdims=True) * (1.0 / members)
        raw = jnp.where(lane < members, at - mean, jnp.where(lane == members, block[:, VALUE : VALUE + 1] - mean, 0.0))
        out_ref[n_obs * tile : n_obs * (tile + 1), :] = raw * block[:, FACTOR : FACTOR + 1]


def forecast(members, count, size, field_ref, flow_ref, odd_ref, even_ref, blocks_ref, out_ref, mean_ref, tall_ref):
    north, south = halo_rows(even_ref, odd_ref, members)
    tile = lax.axis_index("gx")
    west, east, west_mid, east_mid = side_columns(blocks_ref, tile, size)
    has_west, has_east = tile > 0, tile < size - 1
    sides = [jnp.where(has_west, west, 0.0), jnp.where(has_east, east, 0.0)]
    sides += [jnp.where(has_west, west_mid, 0.0), jnp.where(has_east, east_mid, 0.0), jnp.zeros((80, 128), F32)]
    sides = jnp.concatenate(sides, axis=0).T[:members]
    field = tall_field(field_ref, north, south, members, count)
    tall = tall_coefficients(tall_ref, flow_ref, north[2], south[2], count)
    lane = lanes((members, 128))

    def step(rows, r, west_at, east_at):
        w = jnp.where(lane == 0, shifted(sides, -west_at), shifted(rows[r], 1))
        e = jnp.where(lane == 127, shifted(sides, 127 - east_at), shifted(rows[r], -1))
        at = r % EDGE
        return combine([c[at : at + 1, :] for c in tall], rows[r], rows[r - 1], rows[r + 1], w, e)

    middle = {r: step(field, r, r % EDGE, EDGE + r % EDGE) for r in range(-1, count + 1)}
    for r in range(count):
        x = step(middle, r, 2 * EDGE + r, 2 * EDGE + 8 + r)
        mean = jnp.sum(x, axis=0, keepdims=True) * (1.0 / members)
        mean_ref[r : r + 1, :] = mean
        x = x - mean
        high = x.astype(jnp.bfloat16)
        at = slice(128 * r, 128 * (r + 1))
        out_ref[0:members, at] = high
        out_ref[members : 2 * members, at] = (x - high.astype(F32)).astype(jnp.bfloat16)
        out_ref[2 * members :, at] = high


def eliminated(a, members):
    size = 8
    lane, sub = lanes((size, 128)), rows_of((size, 128))
    part = [a[size * q : size * (q + 1), :] for q in range(members // size)]
    pivot = []

    def spread(q, c):
        return jnp.broadcast_to(part[q][:, c : c + 1], (size, 128))

    ahead = {(0, c): spread(0, c) for c in range(size)}
    for p in range(len(part)):
        start, end = size * p, size * (p + 1)
        rest = range(p, len(part))
        column = {(q, c): spread(q, c) for q in rest[1:] for c in range(start, end)}
        column.update(ahead)
        more = range(end, end + size if p + 1 < len(part) else end)
        column.update({(q, c): spread(q, c) for q in rest[1:2] for c in more})
        mine = (lane >= start) & (lane < end)
        for q in rest:
            part[q] = jnp.where(mine, 0.0, part[q])
        found = jnp.zeros((size, 128), F32)
        for j in range(size):
            at = start + j
            value = column[p, at][j : j + 1, :]
            found = jnp.where(sub == j, value, found)
            inverse = 1.0 / value
            unit = jnp.where(lane[:1] == at, 1.0, part[p][j : j + 1, :])
            pivots = {c: column[p, c][j : j + 1, :] for c in range(at + 1, end)}
            pivots.update({c: column[p + 1, at][c - end : c - end + 1, :] for c in more})
            for q in rest:
                factor = column[q, at] * inverse
                for c in range(at + 1, end + (len(more) if q == p + 1 else 0)):
                    column[q, c] = column[q, c] - factor * pivots[c]
                if q == p:
                    factor = jnp.where(sub > j, factor, 0.0)
                part[q] = part[q] - factor * unit
        pivot.append(found)
        ahead = {(p + 1, c): column[p + 1, c] for c in more}
    return jnp.concatenate(part, axis=0), jnp.concatenate(pivot, axis=0)


def analyse(members, count, f_ref, mean_ref, *refs):
    out_ref = refs[-1]
    scaled = jnp.concatenate([ref[...] for ref in refs[:-1]], axis=0)
    full = lax.dot_general(
        scaled, scaled, (((0,), (0,)), ((), ())), precision=HIGHEST, preferred_element_type=F32
    )
    lane, sub = lanes((members, 128)), rows_of((members, 128))
    a, pivots = eliminated(full[:members, :] + jnp.where(lane == sub, members - 1.0, 0.0), members)
    scale = lax.rsqrt(pivots)
    inverse = scale * jnp.where(lane < sub, a, jnp.where(lane == sub, 1.0, 0.0))
    reduced = scale * a[:, members : members + 1]
    weights = jnp.sum(reduced * inverse, axis=0, keepdims=True)
    transform = (jnp.sqrt(members - 1.0) * inverse + weights)[:, :members]
    high = transform.astype(jnp.bfloat16)
    low = (transform - high.astype(F32)).astype(jnp.bfloat16)
    update = jnp.dot(jnp.concatenate([high, high, low], axis=1), f_ref[...], preferred_element_type=F32)
    for r in range(count):
        out_ref[pl.ds(r, members, stride=count), :] = update[:, 128 * r : 128 * (r + 1)] + mean_ref[r : r + 1, :]


def swap(x, axis, offset):
    ny, nx = lax.axis_size("gy"), lax.axis_size("gx")
    partner = {i: i for i in range(ny)}
    for i in range(offset, ny - 1, 2):
        partner[i], partner[i + 1] = i + 1, i
    pairs = []
    for a in range(ny):
        for b in range(nx):
            if partner[a] != a:
                pairs.append((a * nx + b, partner[a] * nx + b))
            elif nx % 2 == 0:
                pairs.append((a * nx + b, a * nx + (b ^ 1)))
    return lax.ppermute(x, ("gy", "gx"), pairs)


def two_power(size):
    return size & (size - 1) == 0


def partner(x, flip_y, flip_x):
    ny, nx = lax.axis_size("gy"), lax.axis_size("gx")
    pairs = [(a * nx + b, (a ^ flip_y) * nx + (b ^ flip_x)) for a in range(ny) for b in range(nx)]
    return lax.ppermute(x, ("gy", "gx"), pairs)


def doubled(x, flip_y, flip_x):
    return jnp.concatenate([x, partner(x, flip_y, flip_x)], axis=0)


def row_blocks(block):
    size, step = lax.axis_size("gx"), 4
    if not two_power(size) or size < 4:
        return lax.all_gather(block, "gx", tiled=True)
    block = jnp.concatenate([block] + [partner(block, 0, flip) for flip in (1, 3, 2)], axis=0)
    while step < size:
        block = doubled(block, 0, step | 1)
        step *= 2
    return block


def place_of(tile, size):
    if not two_power(size) or size < 4:
        return tile
    distance = jnp.bitwise_xor(lax.axis_index("gx"), tile)
    place, bit = distance, 2
    while bit < size:
        place = jnp.bitwise_xor(place, (distance // bit) % 2)
        bit *= 2
    return place


def all_rows(packet):
    size = lax.axis_size("gy")
    if not two_power(size) or size < 4:
        return [lax.all_gather(packet, "gy", tiled=True)]
    flip_x = 1 - lax.axis_size("gx") % 2
    step = size // 2
    while step > 2:
        packet = doubled(packet, step, flip_x)
        step //= 2
    return [packet] + [partner(packet, flip_y, flip_x) for flip_y in ORDER]


def body(ensemble, flow, obs_cell, obs_value, obs_var):
    members, count, width = ensemble.shape
    n_obs = obs_cell.shape[-1]
    size = lax.axis_size("gx")
    call = functools.partial(pl.pallas_call, compiler_params=PARAMS)

    def shape(*dims):
        return jax.ShapeDtypeStruct(dims + (width,), F32)

    inputs = [
        pltpu.with_memory_space_constraint(x, pltpu.HBM)
        for x in (ensemble, flow, obs_cell.reshape(-1), obs_value.reshape(-1), obs_var.reshape(-1))
    ]
    rows_even, rows_odd = call(
        functools.partial(load, members, count),
        out_shape=[shape(2 * members + 8)] * 2,
        in_specs=[HBM] * 2,
        out_specs=[VMEM] * 2,
        scratch_shapes=[pltpu.SemaphoreType.DMA((6,))],
        name="load",
    )(*inputs[:2])
    tall = pltpu.VMEM((3, EDGE, width), F32)
    field, tile_flow, *ready = call(
        functools.partial(prepare, members, count, n_obs),
        out_shape=[shape(members * count), shape(3, count), shape(members), shape(16)] + [shape(n_obs, EDGE)] * 2,
        in_specs=[HBM] * 5 + [ANY],
        out_specs=[VMEM] * 6,
        scratch_shapes=[pltpu.SMEM((n_obs,), jnp.int32)]
        + [pltpu.SMEM((n_obs,), F32)] * 2
        + [tall, pltpu.SemaphoreType.DMA((count + 4,))],
        cost_estimate=pl.CostEstimate(flops=4 * 10**6, bytes_accessed=6 * 10**5, transcendentals=0),
        name="prepare",
    )(*inputs, rows_even)
    rows_odd = swap(rows_odd, "gy", 1)
    rows_even = swap(rows_even, "gy", 0)
    block = call(
        functools.partial(observe, members, count, n_obs),
        out_shape=shape(BLOCK),
        in_specs=[VMEM] * 8,
        out_specs=VMEM,
        scratch_shapes=[tall],
        name="observe",
    )(field, tile_flow, *ready, rows_odd, rows_even)
    blocks = row_blocks(block)
    packet = call(
        functools.partial(complete, members, n_obs, size),
        out_shape=shape(n_obs * size),
        in_specs=[VMEM],
        out_specs=VMEM,
        name="complete",
    )(blocks)
    anomaly, mean = call(
        functools.partial(forecast, members, count, size),
        out_shape=[jax.ShapeDtypeStruct((3 * members, count * width), jnp.bfloat16), shape(count)],
        in_specs=[VMEM] * 5,
        out_specs=[VMEM] * 2,
        scratch_shapes=[tall],
        cost_estimate=pl.CostEstimate(flops=4 * 10**6, bytes_accessed=6 * 10**5, transcendentals=0),
        name="forecast",
    )(field, tile_flow, rows_odd, rows_even, blocks)
    packets = all_rows(packet)
    out = call(
        functools.partial(analyse, members, count),
        out_shape=shape(members * count),
        in_specs=[VMEM] * (2 + len(packets)),
        out_specs=VMEM,
        name="analyse",
    )(anomaly, mean, *packets)
    return out.reshape(ensemble.shape)


def solution(mesh):
    return jax.shard_map(
        body,
        mesh=mesh,
        in_specs=(
            P(None, "gy", "gx"),
            P(None, "gy", "gx"),
            P("gy", "gx", None),
            P("gy", "gx", None),
            P("gy", "gx", None),
        ),
        out_specs=P(None, "gy", "gx"),
        check_vma=False,
    )
```

```python
import functools

import jax
import jax.numpy as jnp
from jax import lax
from jax.experimental import pallas as pl
from jax.experimental.pallas import tpu as pltpu
from jax.sharding import PartitionSpec as P

F32 = jnp.float32
PARAMS = pltpu.CompilerParams(vmem_limit_bytes=24 * 1024 * 1024)
VMEM = pl.BlockSpec(memory_space=pltpu.VMEM)
SMEM = pl.BlockSpec(memory_space=pltpu.SMEM)


def lanes(shape):
    return lax.broadcasted_iota(jnp.int32, shape, len(shape) - 1)


def rows_of(shape):
    return lax.broadcasted_iota(jnp.int32, shape, len(shape) - 2)


def shifted(x, amount):
    return pltpu.roll(x, amount % x.shape[-1], x.ndim - 1)


EDGE = 16
BLOCK = EDGE + 16
MID, OBS = EDGE, EDGE + 8
VALUE, FACTOR, TO_WEST, TO_EAST, WEIGHTS = 64, 65, 66, 67, 72
HBM = pl.BlockSpec(memory_space=pltpu.HBM)
ANY = pl.BlockSpec(memory_space=pl.ANY)
ORDER = (2, 3, 1)


def coefficients(k, u, v):
    return 1.0 - 4.0 * k, k + 0.5 * v, k - 0.5 * v, k + 0.5 * u, k - 0.5 * u


def combine(c, own, north, south, west, east):
    return c[0] * own + c[1] * north + c[2] * south + c[3] * west + c[4] * east


def transposed(x):
    return jnp.concatenate([x, jnp.zeros((128 - x.shape[0], 128), F32)], axis=0).T


def load(members, count, ens_hbm, flow_hbm, even_ref, odd_ref, sems):
    is_even = lax.axis_index("gy") % 2 == 0
    for ref in (even_ref, odd_ref):
        ref[2 * members :, :] = jnp.zeros((8, 128), F32)

    def copies(refs):
        for i, (ref, near, second) in enumerate(zip(refs, (count - 1, 0), (count - 2, 1))):
            yield pltpu.make_async_copy(ens_hbm.at[:, near, :], ref.at[pl.ds(0, members), :], sems.at[3 * i])
            yield pltpu.make_async_copy(ens_hbm.at[:, second, :], ref.at[pl.ds(members, members), :], sems.at[3 * i + 1])
            yield pltpu.make_async_copy(flow_hbm.at[:, near, :], ref.at[pl.ds(2 * members, 3), :], sems.at[3 * i + 2])

    def bring(refs):
        for copy in list(copies(refs)):
            copy.start()
        for copy in list(copies(refs)):
            copy.wait()

    pl.when(is_even)(lambda: bring((even_ref, odd_ref)))
    pl.when(jnp.logical_not(is_even))(lambda: bring((odd_ref, even_ref)))


def halo_rows(even_ref, odd_ref, members):
    at = lax.axis_index("gy")
    is_even = at % 2 == 0
    inside = at > 0, at < lax.axis_size("gy") - 1
    parts = []
    for lo, hi in ((0, members), (members, 2 * members), (2 * members, 2 * members + 3)):
        e, o = even_ref[lo:hi, :], odd_ref[lo:hi, :]
        pair = jnp.where(is_even, o, e), jnp.where(is_even, e, o)
        parts.append([jnp.where(here, x, 0.0) for here, x in zip(inside, pair)])
    return tuple(p[0] for p in parts), tuple(p[1] for p in parts)


def tall_coefficients(scratch, flow_ref, north_flow, south_flow, count):
    for k in range(3):
        scratch[k, 0:count, :] = flow_ref[k]
        scratch[k, count:, :] = jnp.zeros((EDGE - count, 128), F32)
        scratch[k, count : count + 1, :] = south_flow[k : k + 1]
        scratch[k, EDGE - 1 : EDGE, :] = north_flow[k : k + 1]
    return coefficients(*[scratch[k] for k in range(3)])


def tall_field(field_ref, north, south, members, count):
    field = {-2: north[1], -1: north[0], count: south[0], count + 1: south[1]}
    field.update({r: field_ref[r * members : (r + 1) * members, :] for r in range(count)})
    return field


def spread(w, coeffs, lane):
    own, up, down, left, right = coeffs
    to_west, to_east = left * w, right * w
    inside = (
        own * w
        + pltpu.roll(up * w, EDGE - 1, 0)
        + pltpu.roll(down * w, 1, 0)
        + jnp.where(lane == 127, 0.0, shifted(to_west, -1))
        + jnp.where(lane == 0, 0.0, shifted(to_east, 1))
    )
    has_west = lax.axis_index("gx") > 0
    has_east = lax.axis_index("gx") < lax.axis_size("gx") - 1
    return inside, jnp.where(has_west, to_west[:, 0:1], 0.0), jnp.where(has_east, to_east[:, 127:128], 0.0)


def prepare(
    members, count, n_obs, ens_hbm, flow_hbm, cell_hbm, value_hbm, var_hbm, sent_ref,
    field_ref, flow_ref, packed_ref, meta_ref, weight_ref, rest_ref, cell_ref, value_ref, var_ref, tall_ref, sems,
):
    copies = [
        pltpu.make_async_copy(ens_hbm.at[:, r, :], field_ref.at[pl.ds(r * members, members), :], sems.at[r])
        for r in range(count)
    ]
    pairs = ((flow_hbm, flow_ref), (cell_hbm, cell_ref), (value_hbm, value_ref), (var_hbm, var_ref))
    copies += [pltpu.make_async_copy(src, dst, sems.at[count + i]) for i, (src, dst) in enumerate(pairs)]
    for copy in copies:
        copy.start()
    for copy in copies:
        copy.wait()
    lane, sub = lanes((EDGE, 128)), rows_of((EDGE, 128))
    wide = lanes((members, 128))
    nothing = jnp.zeros((3, 128), F32)
    coeffs = tall_coefficients(tall_ref, flow_ref, nothing, nothing, count)
    coeffs = (jnp.where(sub < count, coeffs[0], 0.0),) + coeffs[1:]
    own, up, down, left, right = coeffs
    field = [field_ref[r * members : (r + 1) * members, :] for r in range(count)]
    packed = jnp.zeros((members, 128), F32)
    second = jnp.zeros((members, 128), F32)
    for r, x in enumerate(field):
        packed = jnp.where(wide == r, shifted(x, r), packed)
        packed = jnp.where(wide == EDGE + r, shifted(x, EDGE + r - 127), packed)
        second = jnp.where(wide == r, shifted(x, r - 1), second)
        second = jnp.where(wide == EDGE + r, shifted(x, EDGE + r - 126), second)

    def edge_row(low, high):
        both = jnp.where(lane == sub, low[:, 0:1], jnp.where(lane == sub + EDGE, high[:, 127:128], 0.0))
        return jnp.sum(both, axis=0, keepdims=True)

    middle = (
        edge_row(own, own) * packed
        + edge_row(up, up) * shifted(packed, 1)
        + edge_row(down, down) * shifted(packed, -1)
        + edge_row(right, left) * second
    )
    packed = jnp.where((wide >= 32) & (wide < 40), shifted(middle, 32), packed)
    packed = jnp.where((wide >= 40) & (wide < 48), shifted(middle, 24), packed)
    top_lane, top_sub = lane[:8], sub[:8]
    blocks = []
    for ref, rest in ((value_ref, 0.0), (var_ref, 1.0)):
        block = jnp.full((8, 128), rest, F32)
        for j in range(n_obs):
            block = jnp.where(top_sub == j, ref[j], block)
        blocks.append(block)
    meta = jnp.where(top_lane == VALUE, blocks[0], 0.0)
    meta = jnp.where(top_lane == FACTOR, lax.rsqrt(blocks[1]), meta)
    meta = jnp.where(top_lane == TO_WEST, left[:8, 0:1], meta)
    meta = jnp.where(top_lane == TO_EAST, right[:8, 127:128], meta)
    for j in range(n_obs):
        here = jnp.where((sub < count) & (sub * 128 + lane == cell_ref[j]), 1.0, 0.0)
        first, mid_west, mid_east = spread(here, coeffs, lane)
        w, west, east = spread(first, coeffs, lane)
        weight_ref[j] = first
        rest_ref[j] = w
        total = w[0:1, :] * field[0]
        for r in range(1, count):
            total = total + w[r : r + 1, :] * field[r]
        packed = jnp.where(wide == 48 + j, jnp.sum(total, axis=1, keepdims=True), packed)
        for k, column in ((0, west), (2, east), (4, mid_west), (5, mid_east)):
            meta = jnp.where(top_lane == WEIGHTS + k * n_obs + j, column[:8], meta)
    packed_ref[...] = packed
    meta_ref[0:8, :] = meta
    last = count - 1
    fix = jnp.zeros((8, 128), F32)
    for at, c, r, col in ((32, up, 0, 0), (40, up, 0, 127), (32 + last, down, last, 0), (40 + last, down, last, 127)):
        fix = jnp.where(top_lane == at, c[r : r + 1, col : col + 1], fix)
    meta_ref[8:16, :] = fix


def observe(
    members, count, n_obs, field_ref, flow_ref, packed_ref, meta_ref, weight_ref, rest_ref, odd_ref, even_ref,
    out_ref, tall_ref,
):
    north, south = halo_rows(even_ref, odd_ref, members)
    lane, sub = lanes((EDGE, 128)), rows_of((EDGE, 128))
    wide = lanes((members, 128))
    for k in range(3):
        tall_ref[k] = jnp.zeros((EDGE, 128), F32)
        tall_ref[k, count : count + 1, :] = south[2][k : k + 1]
        tall_ref[k, EDGE - 1 : EDGE, :] = north[2][k : k + 1]
    coeffs = coefficients(*[tall_ref[k] for k in range(3)])
    coeffs = (jnp.where((sub == count) | (sub == EDGE - 1), coeffs[0], 0.0),) + coeffs[1:]
    rows = {-2: north[1], -1: north[0], count: south[0], count + 1: south[1]}
    tile_rows = {r: field_ref[r * members : (r + 1) * members, :] for r in (0, count - 1)}
    packed, meta, fix = packed_ref[...], meta_ref[0:8, :], meta_ref[8:9, :]
    for x, slot, at in ((rows[-1], EDGE - 1, 0), (rows[count], count, count - 1)):
        packed = jnp.where(wide == slot, shifted(x, slot), packed)
        packed = jnp.where(wide == EDGE + slot, shifted(x, EDGE + slot - 127), packed)
        moved = jnp.where(wide == 32 + at, shifted(x, 32 + at), 0.0)
        moved = jnp.where(wide == 40 + at, shifted(x, 40 + at - 127), moved)
        packed = packed + fix * moved
    top_lane = lane[:8]
    for j in range(n_obs):
        w, west, east = spread(weight_ref[j], coeffs, lane)
        all_w = w + rest_ref[j]
        total = sum(all_w[r % EDGE : r % EDGE + 1, :] * x for r, x in rows.items())
        total += sum(w[r : r + 1, :] * x for r, x in tile_rows.items())
        packed = jnp.where(wide == 48 + j, packed + jnp.sum(total, axis=1, keepdims=True), packed)
        for k, column in ((1, west), (3, east)):
            meta = jnp.where(top_lane == WEIGHTS + k * n_obs + j, column[8:], meta)
    turned = jnp.concatenate([packed, jnp.zeros((128 - members, 128), F32)], axis=0).T
    out_ref[0:EDGE, :] = turned[0:EDGE] + shifted(turned[EDGE : 2 * EDGE], 64)
    out_ref[MID : MID + 8, :] = turned[32:40] + shifted(turned[40:48], 64)
    out_ref[OBS : OBS + 8, :] = turned[48:56] + meta


def block_rows(ref, start, tile, size, rows):
    return ref[pl.ds(pl.multiple_of(place_of(tile, size) * BLOCK + start, 8), rows), :]


def side_columns(ref, tile, size):
    west, east = jnp.maximum(tile - 1, 0), jnp.minimum(tile + 1, size - 1)
    own = block_rows(ref, 0, tile, size, EDGE)
    west_x = shifted(block_rows(ref, 0, west, size, EDGE), 64)
    east_x = block_rows(ref, 0, east, size, EDGE)
    west_mid = shifted(block_rows(ref, MID, west, size, 8), 64)
    west_mid += block_rows(ref, OBS, west, size, 8)[:, TO_EAST : TO_EAST + 1] * own[:8]
    east_mid = block_rows(ref, MID, east, size, 8)
    east_mid += block_rows(ref, OBS, east, size, 8)[:, TO_WEST : TO_WEST + 1] * shifted(own[:8], 64)
    return west_x, east_x, west_mid, east_mid


def complete(members, n_obs, size, blocks_ref, out_ref):
    lane = lanes((n_obs, 128))
    for tile in range(size):
        west, east, west_mid, east_mid = side_columns(blocks_ref, jnp.int32(tile), size)
        block = block_rows(blocks_ref, OBS, jnp.int32(tile), size, 8)
        terms = (west[:8], west[8:], east[:8], east[8:], west_mid, east_mid)
        added = []
        for j in range(n_obs):
            at = [WEIGHTS + k * n_obs + j for k in range(len(terms))]
            total = sum(block[:, a : a + 1] * term for a, term in zip(at, terms))
            added.append(jnp.sum(total, axis=0, keepdims=True))
        block = block[:n_obs]
        at = jnp.where(lane < members, block + jnp.concatenate(added, axis=0), 0.0)
        mean = jnp.sum(at, axis=1, keepdims=True) * (1.0 / members)
        raw = jnp.where(lane < members, at - mean, jnp.where(lane == members, block[:, VALUE : VALUE + 1] - mean, 0.0))
        out_ref[n_obs * tile : n_obs * (tile + 1), :] = raw * block[:, FACTOR : FACTOR + 1]


def forecast(members, count, size, field_ref, flow_ref, odd_ref, even_ref, blocks_ref, out_ref, mean_ref, tall_ref):
    north, south = halo_rows(even_ref, odd_ref, members)
    tile = lax.axis_index("gx")
    west, east, west_mid, east_mid = side_columns(blocks_ref, tile, size)
    has_west, has_east = tile > 0, tile < size - 1
    sides = [jnp.where(has_west, west, 0.0), jnp.where(has_east, east, 0.0)]
    sides += [jnp.where(has_west, west_mid, 0.0), jnp.where(has_east, east_mid, 0.0), jnp.zeros((80, 128), F32)]
    sides = jnp.concatenate(sides, axis=0).T[:members]
    field = tall_field(field_ref, north, south, members, count)
    tall = tall_coefficients(tall_ref, flow_ref, north[2], south[2], count)
    lane = lanes((members, 128))

    def step(rows, r, west_at, east_at):
        w = jnp.where(lane == 0, shifted(sides, -west_at), shifted(rows[r], 1))
        e = jnp.where(lane == 127, shifted(sides, 127 - east_at), shifted(rows[r], -1))
        at = r % EDGE
        return combine([c[at : at + 1, :] for c in tall], rows[r], rows[r - 1], rows[r + 1], w, e)

    middle = {r: step(field, r, r % EDGE, EDGE + r % EDGE) for r in range(-1, count + 1)}
    for r in range(count):
        x = step(middle, r, 2 * EDGE + r, 2 * EDGE + 8 + r)
        mean = jnp.sum(x, axis=0, keepdims=True) * (1.0 / members)
        mean_ref[r : r + 1, :] = mean
        x = x - mean
        high = x.astype(jnp.bfloat16)
        at = slice(128 * r, 128 * (r + 1))
        out_ref[0:members, at] = high
        out_ref[members : 2 * members, at] = (x - high.astype(F32)).astype(jnp.bfloat16)
        out_ref[2 * members :, at] = high


def eliminated(a, members, column_ref):
    size = 8
    lane, sub = lanes((size, 128)), rows_of((size, 128))
    part = [a[size * q : size * (q + 1), :] for q in range(members // size)]
    pivot = []

    def spread(q, c):
        return jnp.broadcast_to(part[q][:, c : c + 1], (size, 128))

    ahead = {(0, c): spread(0, c) for c in range(size)}
    for p in range(len(part)):
        start, end = size * p, size * (p + 1)
        rest = range(p, len(part))
        column = {(q, c): spread(q, c) for q in rest[1:] for c in range(start, end)}
        column.update(ahead)
        more = range(end, end + size if p + 1 < len(part) else end)
        column.update({(q, c): spread(q, c) for q in rest[1:2] for c in more})
        mine = (lane >= start) & (lane < end)
        for q in rest:
            part[q] = jnp.where(mine, 0.0, part[q])
        found = jnp.zeros((size, 128), F32)
        for j in range(size):
            at = start + j
            value = column[p, at][j : j + 1, :]
            found = jnp.where(sub == j, value, found)
            inverse = 1.0 / value
            unit = jnp.where(lane[:1] == at, 1.0, part[p][j : j + 1, :])
            pivots = {c: column[p, c][j : j + 1, :] for c in range(at + 1, end)}
            if more:
                column_ref[at] = column[p + 1, at]
            pivots.update({c: column_ref[at, c - end : c - end + 1, :] for c in more})
            for q in rest:
                factor = column[q, at] * inverse
                for c in range(at + 1, end + (len(more) if q == p + 1 else 0)):
                    column[q, c] = column[q, c] - factor * pivots[c]
                if q == p:
                    factor = jnp.where(sub > j, factor, 0.0)
                part[q] = part[q] - factor * unit
        pivot.append(found)
        ahead = {(p + 1, c): column[p + 1, c] for c in more}
    return jnp.concatenate(part, axis=0), jnp.concatenate(pivot, axis=0)


def thirds(x):
    first = x.astype(jnp.bfloat16)
    rest = x - first.astype(F32)
    second = rest.astype(jnp.bfloat16)
    return first, second, (rest - second.astype(F32)).astype(jnp.bfloat16)


def product(lefts, rights):
    left, right = jnp.concatenate(lefts, axis=1), jnp.concatenate(rights, axis=0)
    return jnp.dot(left, right, preferred_element_type=F32)


def analyse(members, count, f_ref, mean_ref, *refs):
    out_ref, column_ref = refs[-2:]
    scaled = jnp.concatenate([ref[...] for ref in refs[:-2]], axis=0)
    a1, a2, a3 = thirds(scaled)
    t1, t2, t3 = thirds(scaled.T[:members])
    full = product([t1, t2], [a1, a1]) + (product([t1, t2], [a2, a2]) + product([t1, t3], [a3, a1]))
    lane, sub = lanes((members, 128)), rows_of((members, 128))
    a, pivots = eliminated(full + jnp.where(lane == sub, members - 1.0, 0.0), members, column_ref)
    scale = lax.rsqrt(pivots)
    inverse = scale * jnp.where(lane < sub, a, jnp.where(lane == sub, 1.0, 0.0))
    reduced = scale * a[:, members : members + 1]
    weights = jnp.sum(reduced * inverse, axis=0, keepdims=True)
    transform = (jnp.sqrt(members - 1.0) * inverse + weights)[:, :members]
    high = transform.astype(jnp.bfloat16)
    low = (transform - high.astype(F32)).astype(jnp.bfloat16)
    update = product([high, high, low], [f_ref[...]])
    for r in range(count):
        out_ref[pl.ds(r, members, stride=count), :] = update[:, 128 * r : 128 * (r + 1)] + mean_ref[r : r + 1, :]


def swap(x, axis, offset):
    ny, nx = lax.axis_size("gy"), lax.axis_size("gx")
    partner = {i: i for i in range(ny)}
    for i in range(offset, ny - 1, 2):
        partner[i], partner[i + 1] = i + 1, i
    pairs = []
    for a in range(ny):
        for b in range(nx):
            if partner[a] != a:
                pairs.append((a * nx + b, partner[a] * nx + b))
            elif nx % 2 == 0:
                pairs.append((a * nx + b, a * nx + (b ^ 1)))
    return lax.ppermute(x, ("gy", "gx"), pairs)


def two_power(size):
    return size & (size - 1) == 0


def partner(x, flip_y, flip_x):
    ny, nx = lax.axis_size("gy"), lax.axis_size("gx")
    pairs = [(a * nx + b, (a ^ flip_y) * nx + (b ^ flip_x)) for a in range(ny) for b in range(nx)]
    return lax.ppermute(x, ("gy", "gx"), pairs)


def doubled(x, flip_y, flip_x):
    return jnp.concatenate([x, partner(x, flip_y, flip_x)], axis=0)


def row_blocks(block):
    size, step = lax.axis_size("gx"), 1
    if not two_power(size):
        return lax.all_gather(block, "gx", tiled=True)
    while step < size:
        block = doubled(block, 0, step | 1)
        step *= 2
    return block


def place_of(tile, size):
    if not two_power(size):
        return tile
    distance = jnp.bitwise_xor(lax.axis_index("gx"), tile)
    place, bit = distance, 2
    while bit < size:
        place = jnp.bitwise_xor(place, (distance // bit) % 2)
        bit *= 2
    return place


def all_rows(packet):
    size = lax.axis_size("gy")
    if not two_power(size) or size < 4:
        return [lax.all_gather(packet, "gy", tiled=True)]
    flip_x = 1 - lax.axis_size("gx") % 2
    step = size // 2
    while step > 2:
        packet = doubled(packet, step, flip_x)
        step //= 2
    return [packet] + [partner(packet, flip_y, flip_x) for flip_y in ORDER]


def body(ensemble, flow, obs_cell, obs_value, obs_var):
    members, count, width = ensemble.shape
    n_obs = obs_cell.shape[-1]
    size = lax.axis_size("gx")
    call = functools.partial(pl.pallas_call, compiler_params=PARAMS)

    def shape(*dims):
        return jax.ShapeDtypeStruct(dims + (width,), F32)

    inputs = [
        pltpu.with_memory_space_constraint(x, pltpu.HBM)
        for x in (ensemble, flow, obs_cell.reshape(-1), obs_value.reshape(-1), obs_var.reshape(-1))
    ]
    rows_even, rows_odd = call(
        functools.partial(load, members, count),
        out_shape=[shape(2 * members + 8)] * 2,
        in_specs=[HBM] * 2,
        out_specs=[VMEM] * 2,
        scratch_shapes=[pltpu.SemaphoreType.DMA((6,))],
        name="load",
    )(*inputs[:2])
    tall = pltpu.VMEM((3, EDGE, width), F32)
    field, tile_flow, *ready = call(
        functools.partial(prepare, members, count, n_obs),
        out_shape=[shape(members * count), shape(3, count), shape(members), shape(16)] + [shape(n_obs, EDGE)] * 2,
        in_specs=[HBM] * 5 + [ANY],
        out_specs=[VMEM] * 6,
        scratch_shapes=[pltpu.SMEM((n_obs,), jnp.int32)]
        + [pltpu.SMEM((n_obs,), F32)] * 2
        + [tall, pltpu.SemaphoreType.DMA((count + 4,))],
        cost_estimate=pl.CostEstimate(flops=4 * 10**6, bytes_accessed=6 * 10**5, transcendentals=0),
        name="prepare",
    )(*inputs, rows_even)
    rows_odd = swap(rows_odd, "gy", 1)
    rows_even = swap(rows_even, "gy", 0)
    block = call(
        functools.partial(observe, members, count, n_obs),
        out_shape=shape(BLOCK),
        in_specs=[VMEM] * 8,
        out_specs=VMEM,
        scratch_shapes=[tall],
        name="observe",
    )(field, tile_flow, *ready, rows_odd, rows_even)
    blocks = row_blocks(block)
    packet = call(
        functools.partial(complete, members, n_obs, size),
        out_shape=shape(n_obs * size),
        in_specs=[VMEM],
        out_specs=VMEM,
        name="complete",
    )(blocks)
    anomaly, mean = call(
        functools.partial(forecast, members, count, size),
        out_shape=[jax.ShapeDtypeStruct((3 * members, count * width), jnp.bfloat16), shape(count)],
        in_specs=[VMEM] * 5,
        out_specs=[VMEM] * 2,
        scratch_shapes=[tall],
        cost_estimate=pl.CostEstimate(flops=4 * 10**6, bytes_accessed=6 * 10**5, transcendentals=0),
        name="forecast",
    )(field, tile_flow, rows_odd, rows_even, blocks)
    packets = all_rows(packet)
    out = call(
        functools.partial(analyse, members, count),
        out_shape=shape(members * count),
        in_specs=[VMEM] * (2 + len(packets)),
        out_specs=VMEM,
        scratch_shapes=[pltpu.VMEM((members, 8, width), F32)],
        name="analyse",
    )(anomaly, mean, *packets)
    return out.reshape(ensemble.shape)


def solution(mesh):
    return jax.shard_map(
        body,
        mesh=mesh,
        in_specs=(
            P(None, "gy", "gx"),
            P(None, "gy", "gx"),
            P("gy", "gx", None),
            P("gy", "gx", None),
            P("gy", "gx", None),
        ),
        out_specs=P(None, "gy", "gx"),
        check_vma=False,
    )
```

```python
import functools

import jax
import jax.numpy as jnp
from jax import lax
from jax.experimental import pallas as pl
from jax.experimental.pallas import tpu as pltpu
from jax.sharding import PartitionSpec as P

F32 = jnp.float32
PARAMS = pltpu.CompilerParams(vmem_limit_bytes=24 * 1024 * 1024)
VMEM = pl.BlockSpec(memory_space=pltpu.VMEM)
SMEM = pl.BlockSpec(memory_space=pltpu.SMEM)


def lanes(shape):
    return lax.broadcasted_iota(jnp.int32, shape, len(shape) - 1)


def rows_of(shape):
    return lax.broadcasted_iota(jnp.int32, shape, len(shape) - 2)


def shifted(x, amount):
    return pltpu.roll(x, amount % x.shape[-1], x.ndim - 1)


EDGE = 16
BLOCK = EDGE + 16
MID, OBS = EDGE, EDGE + 8
VALUE, FACTOR, TO_WEST, TO_EAST, WEIGHTS = 64, 65, 66, 67, 72
HBM = pl.BlockSpec(memory_space=pltpu.HBM)
ANY = pl.BlockSpec(memory_space=pl.ANY)


def coefficients(k, u, v):
    return 1.0 - 4.0 * k, k + 0.5 * v, k - 0.5 * v, k + 0.5 * u, k - 0.5 * u


def combine(c, own, north, south, west, east):
    return c[0] * own + c[1] * north + c[2] * south + c[3] * west + c[4] * east


def transposed(x):
    return jnp.concatenate([x, jnp.zeros((128 - x.shape[0], 128), F32)], axis=0).T


def load(members, count, ens_hbm, flow_hbm, even_ref, odd_ref, sems):
    is_even = lax.axis_index("gy") % 2 == 0
    for ref in (even_ref, odd_ref):
        ref[2 * members :, :] = jnp.zeros((8, 128), F32)

    def copies(refs):
        for i, (ref, near, second) in enumerate(zip(refs, (count - 1, 0), (count - 2, 1))):
            yield pltpu.make_async_copy(ens_hbm.at[:, near, :], ref.at[pl.ds(0, members), :], sems.at[3 * i])
            yield pltpu.make_async_copy(ens_hbm.at[:, second, :], ref.at[pl.ds(members, members), :], sems.at[3 * i + 1])
            yield pltpu.make_async_copy(flow_hbm.at[:, near, :], ref.at[pl.ds(2 * members, 3), :], sems.at[3 * i + 2])

    def bring(refs):
        for copy in list(copies(refs)):
            copy.start()
        for copy in list(copies(refs)):
            copy.wait()

    pl.when(is_even)(lambda: bring((even_ref, odd_ref)))
    pl.when(jnp.logical_not(is_even))(lambda: bring((odd_ref, even_ref)))


def halo_rows(even_ref, odd_ref, members):
    at = lax.axis_index("gy")
    is_even = at % 2 == 0
    inside = at > 0, at < lax.axis_size("gy") - 1
    parts = []
    for lo, hi in ((0, members), (members, 2 * members), (2 * members, 2 * members + 3)):
        e, o = even_ref[lo:hi, :], odd_ref[lo:hi, :]
        pair = jnp.where(is_even, o, e), jnp.where(is_even, e, o)
        parts.append([jnp.where(here, x, 0.0) for here, x in zip(inside, pair)])
    return tuple(p[0] for p in parts), tuple(p[1] for p in parts)


def tall_coefficients(scratch, flow_ref, north_flow, south_flow, count):
    for k in range(3):
        scratch[k, 0:count, :] = flow_ref[k]
        scratch[k, count:, :] = jnp.zeros((EDGE - count, 128), F32)
        scratch[k, count : count + 1, :] = south_flow[k : k + 1]
        scratch[k, EDGE - 1 : EDGE, :] = north_flow[k : k + 1]
    return coefficients(*[scratch[k] for k in range(3)])


def tall_field(field_ref, north, south, members, count):
    field = {-2: north[1], -1: north[0], count: south[0], count + 1: south[1]}
    field.update({r: field_ref[r * members : (r + 1) * members, :] for r in range(count)})
    return field


def spread(w, coeffs, lane):
    own, up, down, left, right = coeffs
    to_west, to_east = left * w, right * w
    inside = (
        own * w
        + pltpu.roll(up * w, EDGE - 1, 0)
        + pltpu.roll(down * w, 1, 0)
        + jnp.where(lane == 127, 0.0, shifted(to_west, -1))
        + jnp.where(lane == 0, 0.0, shifted(to_east, 1))
    )
    has_west = lax.axis_index("gx") > 0
    has_east = lax.axis_index("gx") < lax.axis_size("gx") - 1
    return inside, jnp.where(has_west, to_west[:, 0:1], 0.0), jnp.where(has_east, to_east[:, 127:128], 0.0)


def prepare(
    members, count, n_obs, ens_hbm, flow_hbm, cell_hbm, value_hbm, var_hbm, sent_ref,
    field_ref, flow_ref, packed_ref, meta_ref, weight_ref, rest_ref, cell_ref, value_ref, var_ref, tall_ref, sems,
):
    copies = [
        pltpu.make_async_copy(ens_hbm.at[:, r, :], field_ref.at[pl.ds(r * members, members), :], sems.at[r])
        for r in range(count)
    ]
    pairs = ((flow_hbm, flow_ref), (cell_hbm, cell_ref), (value_hbm, value_ref), (var_hbm, var_ref))
    copies += [pltpu.make_async_copy(src, dst, sems.at[count + i]) for i, (src, dst) in enumerate(pairs)]
    for copy in copies:
        copy.start()
    for copy in copies:
        copy.wait()
    lane, sub = lanes((EDGE, 128)), rows_of((EDGE, 128))
    wide = lanes((members, 128))
    nothing = jnp.zeros((3, 128), F32)
    coeffs = tall_coefficients(tall_ref, flow_ref, nothing, nothing, count)
    coeffs = (jnp.where(sub < count, coeffs[0], 0.0),) + coeffs[1:]
    own, up, down, left, right = coeffs
    field = [field_ref[r * members : (r + 1) * members, :] for r in range(count)]
    packed = jnp.zeros((members, 128), F32)
    second = jnp.zeros((members, 128), F32)
    for r, x in enumerate(field):
        packed = jnp.where(wide == r, shifted(x, r), packed)
        packed = jnp.where(wide == EDGE + r, shifted(x, EDGE + r - 127), packed)
        second = jnp.where(wide == r, shifted(x, r - 1), second)
        second = jnp.where(wide == EDGE + r, shifted(x, EDGE + r - 126), second)

    def edge_row(low, high):
        both = jnp.where(lane == sub, low[:, 0:1], jnp.where(lane == sub + EDGE, high[:, 127:128], 0.0))
        return jnp.sum(both, axis=0, keepdims=True)

    middle = (
        edge_row(own, own) * packed
        + edge_row(up, up) * shifted(packed, 1)
        + edge_row(down, down) * shifted(packed, -1)
        + edge_row(right, left) * second
    )
    packed = jnp.where((wide >= 32) & (wide < 40), shifted(middle, 32), packed)
    packed = jnp.where((wide >= 40) & (wide < 48), shifted(middle, 24), packed)
    top_lane, top_sub = lane[:8], sub[:8]
    blocks = []
    for ref, rest in ((value_ref, 0.0), (var_ref, 1.0)):
        block = jnp.full((8, 128), rest, F32)
        for j in range(n_obs):
            block = jnp.where(top_sub == j, ref[j], block)
        blocks.append(block)
    meta = jnp.where(top_lane == VALUE, blocks[0], 0.0)
    meta = jnp.where(top_lane == FACTOR, lax.rsqrt(blocks[1]), meta)
    meta = jnp.where(top_lane == TO_WEST, left[:8, 0:1], meta)
    meta = jnp.where(top_lane == TO_EAST, right[:8, 127:128], meta)
    for j in range(n_obs):
        here = jnp.where((sub < count) & (sub * 128 + lane == cell_ref[j]), 1.0, 0.0)
        first, mid_west, mid_east = spread(here, coeffs, lane)
        w, west, east = spread(first, coeffs, lane)
        weight_ref[j] = first
        rest_ref[j] = w
        total = w[0:1, :] * field[0]
        for r in range(1, count):
            total = total + w[r : r + 1, :] * field[r]
        packed = jnp.where(wide == 48 + j, jnp.sum(total, axis=1, keepdims=True), packed)
        for k, column in ((0, west), (2, east), (4, mid_west), (5, mid_east)):
            meta = jnp.where(top_lane == WEIGHTS + k * n_obs + j, column[:8], meta)
    packed_ref[...] = packed
    meta_ref[0:8, :] = meta
    last = count - 1
    fix = jnp.zeros((8, 128), F32)
    for at, c, r, col in ((32, up, 0, 0), (40, up, 0, 127), (32 + last, down, last, 0), (40 + last, down, last, 127)):
        fix = jnp.where(top_lane == at, c[r : r + 1, col : col + 1], fix)
    meta_ref[8:16, :] = fix


def observe(
    members, count, n_obs, field_ref, flow_ref, packed_ref, meta_ref, weight_ref, rest_ref, odd_ref, even_ref,
    out_ref, tall_ref,
):
    north, south = halo_rows(even_ref, odd_ref, members)
    lane, sub = lanes((EDGE, 128)), rows_of((EDGE, 128))
    wide = lanes((members, 128))
    for k in range(3):
        tall_ref[k] = jnp.zeros((EDGE, 128), F32)
        tall_ref[k, count : count + 1, :] = south[2][k : k + 1]
        tall_ref[k, EDGE - 1 : EDGE, :] = north[2][k : k + 1]
    coeffs = coefficients(*[tall_ref[k] for k in range(3)])
    coeffs = (jnp.where((sub == count) | (sub == EDGE - 1), coeffs[0], 0.0),) + coeffs[1:]
    rows = {-2: north[1], -1: north[0], count: south[0], count + 1: south[1]}
    tile_rows = {r: field_ref[r * members : (r + 1) * members, :] for r in (0, count - 1)}
    packed, meta, fix = packed_ref[...], meta_ref[0:8, :], meta_ref[8:9, :]
    for x, slot, at in ((rows[-1], EDGE - 1, 0), (rows[count], count, count - 1)):
        packed = jnp.where(wide == slot, shifted(x, slot), packed)
        packed = jnp.where(wide == EDGE + slot, shifted(x, EDGE + slot - 127), packed)
        moved = jnp.where(wide == 32 + at, shifted(x, 32 + at), 0.0)
        moved = jnp.where(wide == 40 + at, shifted(x, 40 + at - 127), moved)
        packed = packed + fix * moved
    top_lane = lane[:8]
    for j in range(n_obs):
        w, west, east = spread(weight_ref[j], coeffs, lane)
        all_w = w + rest_ref[j]
        total = sum(all_w[r % EDGE : r % EDGE + 1, :] * x for r, x in rows.items())
        total += sum(w[r : r + 1, :] * x for r, x in tile_rows.items())
        packed = jnp.where(wide == 48 + j, packed + jnp.sum(total, axis=1, keepdims=True), packed)
        for k, column in ((1, west), (3, east)):
            meta = jnp.where(top_lane == WEIGHTS + k * n_obs + j, column[8:], meta)
    turned = jnp.concatenate([packed, jnp.zeros((128 - members, 128), F32)], axis=0).T
    out_ref[0:EDGE, :] = turned[0:EDGE] + shifted(turned[EDGE : 2 * EDGE], 64)
    out_ref[MID : MID + 8, :] = turned[32:40] + shifted(turned[40:48], 64)
    out_ref[OBS : OBS + 8, :] = turned[48:56] + meta


def block_rows(ref, start, tile, size, rows):
    return ref[pl.ds(pl.multiple_of(place_of(tile, size) * BLOCK + start, 8), rows), :]


def side_columns(ref, tile, size):
    west, east = jnp.maximum(tile - 1, 0), jnp.minimum(tile + 1, size - 1)
    own = block_rows(ref, 0, tile, size, EDGE)
    west_x = shifted(block_rows(ref, 0, west, size, EDGE), 64)
    east_x = block_rows(ref, 0, east, size, EDGE)
    west_mid = shifted(block_rows(ref, MID, west, size, 8), 64)
    west_mid += block_rows(ref, OBS, west, size, 8)[:, TO_EAST : TO_EAST + 1] * own[:8]
    east_mid = block_rows(ref, MID, east, size, 8)
    east_mid += block_rows(ref, OBS, east, size, 8)[:, TO_WEST : TO_WEST + 1] * shifted(own[:8], 64)
    return west_x, east_x, west_mid, east_mid


def complete(members, n_obs, size, blocks_ref, out_ref):
    lane = lanes((n_obs, 128))
    for tile in range(size):
        west, east, west_mid, east_mid = side_columns(blocks_ref, jnp.int32(tile), size)
        block = block_rows(blocks_ref, OBS, jnp.int32(tile), size, 8)
        terms = (west[:8], west[8:], east[:8], east[8:], west_mid, east_mid)
        added = []
        for j in range(n_obs):
            at = [WEIGHTS + k * n_obs + j for k in range(len(terms))]
            total = sum(block[:, a : a + 1] * term for a, term in zip(at, terms))
            added.append(jnp.sum(total, axis=0, keepdims=True))
        block = block[:n_obs]
        at = jnp.where(lane < members, block + jnp.concatenate(added, axis=0), 0.0)
        mean = jnp.sum(at, axis=1, keepdims=True) * (1.0 / members)
        raw = jnp.where(lane < members, at - mean, jnp.where(lane == members, block[:, VALUE : VALUE + 1] - mean, 0.0))
        out_ref[n_obs * tile : n_obs * (tile + 1), :] = raw * block[:, FACTOR : FACTOR + 1]


def forecast(members, count, size, field_ref, flow_ref, odd_ref, even_ref, blocks_ref, out_ref, mean_ref, tall_ref):
    north, south = halo_rows(even_ref, odd_ref, members)
    tile = lax.axis_index("gx")
    west, east, west_mid, east_mid = side_columns(blocks_ref, tile, size)
    has_west, has_east = tile > 0, tile < size - 1
    sides = [jnp.where(has_west, west, 0.0), jnp.where(has_east, east, 0.0)]
    sides += [jnp.where(has_west, west_mid, 0.0), jnp.where(has_east, east_mid, 0.0), jnp.zeros((80, 128), F32)]
    sides = jnp.concatenate(sides, axis=0).T[:members]
    field = tall_field(field_ref, north, south, members, count)
    tall = tall_coefficients(tall_ref, flow_ref, north[2], south[2], count)
    lane = lanes((members, 128))

    def step(rows, r, west_at, east_at):
        w = jnp.where(lane == 0, shifted(sides, -west_at), shifted(rows[r], 1))
        e = jnp.where(lane == 127, shifted(sides, 127 - east_at), shifted(rows[r], -1))
        at = r % EDGE
        return combine([c[at : at + 1, :] for c in tall], rows[r], rows[r - 1], rows[r + 1], w, e)

    middle = {r: step(field, r, r % EDGE, EDGE + r % EDGE) for r in range(-1, count + 1)}
    for r in range(count):
        x = step(middle, r, 2 * EDGE + r, 2 * EDGE + 8 + r)
        mean = jnp.sum(x, axis=0, keepdims=True) * (1.0 / members)
        mean_ref[r : r + 1, :] = mean
        x = x - mean
        high = x.astype(jnp.bfloat16)
        at = slice(128 * r, 128 * (r + 1))
        out_ref[0:members, at] = high
        out_ref[members : 2 * members, at] = (x - high.astype(F32)).astype(jnp.bfloat16)
        out_ref[2 * members :, at] = high


def eliminated(a, members, column_ref):
    size = 8
    lane, sub = lanes((size, 128)), rows_of((size, 128))
    part = [a[size * q : size * (q + 1), :] for q in range(members // size)]
    pivot = []

    def spread(q, c):
        return jnp.broadcast_to(part[q][:, c : c + 1], (size, 128))

    ahead = {(0, c): spread(0, c) for c in range(size)}
    for p in range(len(part)):
        start, end = size * p, size * (p + 1)
        rest = range(p, len(part))
        column = {(q, c): spread(q, c) for q in rest[1:] for c in range(start, end)}
        column.update(ahead)
        more = range(end, end + size if p + 1 < len(part) else end)
        column.update({(q, c): spread(q, c) for q in rest[1:2] for c in more})
        mine = (lane >= start) & (lane < end)
        for q in rest:
            part[q] = jnp.where(mine, 0.0, part[q])
        found = jnp.zeros((size, 128), F32)
        for j in range(size):
            at = start + j
            value = column[p, at][j : j + 1, :]
            found = jnp.where(sub == j, value, found)
            inverse = 1.0 / value
            unit = jnp.where(lane[:1] == at, 1.0, part[p][j : j + 1, :])
            pivots = {c: column[p, c][j : j + 1, :] for c in range(at + 1, end)}
            if more:
                column_ref[at] = column[p + 1, at]
            pivots.update({c: column_ref[at, c - end : c - end + 1, :] for c in more})
            for q in rest:
                factor = column[q, at] * inverse
                for c in range(at + 1, end + (len(more) if q == p + 1 else 0)):
                    column[q, c] = column[q, c] - factor * pivots[c]
                if q == p:
                    factor = jnp.where(sub > j, factor, 0.0)
                part[q] = part[q] - factor * unit
        pivot.append(found)
        ahead = {(p + 1, c): column[p + 1, c] for c in more}
    return jnp.concatenate(part, axis=0), jnp.concatenate(pivot, axis=0)


def thirds(x):
    first = x.astype(jnp.bfloat16)
    rest = x - first.astype(F32)
    second = rest.astype(jnp.bfloat16)
    return first, second, (rest - second.astype(F32)).astype(jnp.bfloat16)


def product(lefts, rights):
    left, right = jnp.concatenate(lefts, axis=1), jnp.concatenate(rights, axis=0)
    return jnp.dot(left, right, preferred_element_type=F32)


def analyse(members, count, f_ref, mean_ref, *refs):
    out_ref, column_ref = refs[-2:]
    scaled = jnp.concatenate([ref[...] for ref in refs[:-2]], axis=0)
    a1, a2, a3 = thirds(scaled)
    t1, t2, t3 = thirds(scaled.T[:members])
    full = product([t1, t2], [a1, a1]) + (product([t1, t2], [a2, a2]) + product([t1, t3], [a3, a1]))
    lane, sub = lanes((members, 128)), rows_of((members, 128))
    a, pivots = eliminated(full + jnp.where(lane == sub, members - 1.0, 0.0), members, column_ref)
    scale = lax.rsqrt(pivots)
    inverse = scale * jnp.where(lane < sub, a, jnp.where(lane == sub, 1.0, 0.0))
    reduced = scale * a[:, members : members + 1]
    weights = jnp.sum(reduced * inverse, axis=0, keepdims=True)
    transform = (jnp.sqrt(members - 1.0) * inverse + weights)[:, :members]
    high = transform.astype(jnp.bfloat16)
    low = (transform - high.astype(F32)).astype(jnp.bfloat16)
    update = product([high, high, low], [f_ref[...]])
    for r in range(count):
        out_ref[pl.ds(r, members, stride=count), :] = update[:, 128 * r : 128 * (r + 1)] + mean_ref[r : r + 1, :]


def swap(x, axis, offset):
    ny, nx = lax.axis_size("gy"), lax.axis_size("gx")
    partner = {i: i for i in range(ny)}
    for i in range(offset, ny - 1, 2):
        partner[i], partner[i + 1] = i + 1, i
    pairs = []
    for a in range(ny):
        for b in range(nx):
            if partner[a] != a:
                pairs.append((a * nx + b, partner[a] * nx + b))
            elif nx % 2 == 0:
                pairs.append((a * nx + b, a * nx + (b ^ 1)))
    return lax.ppermute(x, ("gy", "gx"), pairs)


def two_power(size):
    return size & (size - 1) == 0


def partner(x, flip_y, flip_x):
    ny, nx = lax.axis_size("gy"), lax.axis_size("gx")
    pairs = [(a * nx + b, (a ^ flip_y) * nx + (b ^ flip_x)) for a in range(ny) for b in range(nx)]
    return lax.ppermute(x, ("gy", "gx"), pairs)


def doubled(x, flip_y, flip_x):
    return jnp.concatenate([x, partner(x, flip_y, flip_x)], axis=0)


def row_blocks(block):
    size, step = lax.axis_size("gx"), 1
    if not two_power(size):
        return lax.all_gather(block, "gx", tiled=True)
    while step < size:
        block = doubled(block, 0, step | 1)
        step *= 2
    return block


def place_of(tile, size):
    if not two_power(size):
        return tile
    distance = jnp.bitwise_xor(lax.axis_index("gx"), tile)
    place, bit = distance, 2
    while bit < size:
        place = jnp.bitwise_xor(place, (distance // bit) % 2)
        bit *= 2
    return place


def all_rows(packet):
    ny, nx = lax.axis_size("gy"), lax.axis_size("gx")
    if not two_power(ny) or ny < 4 or nx % 2:
        return [lax.all_gather(packet, "gy", tiled=True)]
    step = ny // 2
    while step > 2:
        packet = doubled(packet, step, 1)
        step //= 2
    pairs = [(a * nx + b, (a ^ (2 - b % 2)) * nx + (b ^ 1)) for a in range(ny) for b in range(nx)]
    near = lax.ppermute(packet, ("gy", "gx"), pairs)
    return [packet, near, partner(packet, 3, 1), partner(near, 0, 1)]


def body(ensemble, flow, obs_cell, obs_value, obs_var):
    members, count, width = ensemble.shape
    n_obs = obs_cell.shape[-1]
    size = lax.axis_size("gx")
    call = functools.partial(pl.pallas_call, compiler_params=PARAMS)

    def shape(*dims):
        return jax.ShapeDtypeStruct(dims + (width,), F32)

    inputs = [
        pltpu.with_memory_space_constraint(x, pltpu.HBM)
        for x in (ensemble, flow, obs_cell.reshape(-1), obs_value.reshape(-1), obs_var.reshape(-1))
    ]
    rows_even, rows_odd = call(
        functools.partial(load, members, count),
        out_shape=[shape(2 * members + 8)] * 2,
        in_specs=[HBM] * 2,
        out_specs=[VMEM] * 2,
        scratch_shapes=[pltpu.SemaphoreType.DMA((6,))],
        name="load",
    )(*inputs[:2])
    tall = pltpu.VMEM((3, EDGE, width), F32)
    field, tile_flow, *ready = call(
        functools.partial(prepare, members, count, n_obs),
        out_shape=[shape(members * count), shape(3, count), shape(members), shape(16)] + [shape(n_obs, EDGE)] * 2,
        in_specs=[HBM] * 5 + [ANY],
        out_specs=[VMEM] * 6,
        scratch_shapes=[pltpu.SMEM((n_obs,), jnp.int32)]
        + [pltpu.SMEM((n_obs,), F32)] * 2
        + [tall, pltpu.SemaphoreType.DMA((count + 4,))],
        cost_estimate=pl.CostEstimate(flops=4 * 10**6, bytes_accessed=6 * 10**5, transcendentals=0),
        name="prepare",
    )(*inputs, rows_even)
    rows_odd = swap(rows_odd, "gy", 1)
    rows_even = swap(rows_even, "gy", 0)
    block = call(
        functools.partial(observe, members, count, n_obs),
        out_shape=shape(BLOCK),
        in_specs=[VMEM] * 8,
        out_specs=VMEM,
        scratch_shapes=[tall],
        name="observe",
    )(field, tile_flow, *ready, rows_odd, rows_even)
    blocks = row_blocks(block)
    packet = call(
        functools.partial(complete, members, n_obs, size),
        out_shape=shape(n_obs * size),
        in_specs=[VMEM],
        out_specs=VMEM,
        name="complete",
    )(blocks)
    anomaly, mean = call(
        functools.partial(forecast, members, count, size),
        out_shape=[jax.ShapeDtypeStruct((3 * members, count * width), jnp.bfloat16), shape(count)],
        in_specs=[VMEM] * 5,
        out_specs=[VMEM] * 2,
        scratch_shapes=[tall],
        cost_estimate=pl.CostEstimate(flops=4 * 10**6, bytes_accessed=6 * 10**5, transcendentals=0),
        name="forecast",
    )(field, tile_flow, rows_odd, rows_even, blocks)
    packets = all_rows(packet)
    out = call(
        functools.partial(analyse, members, count),
        out_shape=shape(members * count),
        in_specs=[VMEM] * (2 + len(packets)),
        out_specs=VMEM,
        scratch_shapes=[pltpu.VMEM((members, 8, width), F32)],
        name="analyse",
    )(anomaly, mean, *packets)
    return out.reshape(ensemble.shape)


def solution(mesh):
    return jax.shard_map(
        body,
        mesh=mesh,
        in_specs=(
            P(None, "gy", "gx"),
            P(None, "gy", "gx"),
            P("gy", "gx", None),
            P("gy", "gx", None),
            P("gy", "gx", None),
        ),
        out_specs=P(None, "gy", "gx"),
        check_vma=False,
    )
```

```python
import functools

import jax
import jax.numpy as jnp
from jax import lax
from jax.experimental import pallas as pl
from jax.experimental.pallas import tpu as pltpu
from jax.sharding import PartitionSpec as P

F32 = jnp.float32
PARAMS = pltpu.CompilerParams(vmem_limit_bytes=24 * 1024 * 1024)
VMEM = pl.BlockSpec(memory_space=pltpu.VMEM)
SMEM = pl.BlockSpec(memory_space=pltpu.SMEM)


def lanes(shape):
    return lax.broadcasted_iota(jnp.int32, shape, len(shape) - 1)


def rows_of(shape):
    return lax.broadcasted_iota(jnp.int32, shape, len(shape) - 2)


def shifted(x, amount):
    return pltpu.roll(x, amount % x.shape[-1], x.ndim - 1)


EDGE = 16
BLOCK = EDGE + 16
MID, OBS = EDGE, EDGE + 8
VALUE, FACTOR, TO_WEST, TO_EAST, WEIGHTS = 64, 65, 66, 67, 72
HBM = pl.BlockSpec(memory_space=pltpu.HBM)
ANY = pl.BlockSpec(memory_space=pl.ANY)


def coefficients(k, u, v):
    return 1.0 - 4.0 * k, k + 0.5 * v, k - 0.5 * v, k + 0.5 * u, k - 0.5 * u


def combine(c, own, north, south, west, east):
    return c[0] * own + c[1] * north + c[2] * south + c[3] * west + c[4] * east


def transposed(x):
    return jnp.concatenate([x, jnp.zeros((128 - x.shape[0], 128), F32)], axis=0).T


def load(members, count, ens_hbm, flow_hbm, even_ref, odd_ref, sems):
    is_even = lax.axis_index("gy") % 2 == 0
    for ref in (even_ref, odd_ref):
        ref[2 * members :, :] = jnp.zeros((8, 128), F32)

    def copies(refs):
        for i, (ref, near, second) in enumerate(zip(refs, (count - 1, 0), (count - 2, 1))):
            yield pltpu.make_async_copy(ens_hbm.at[:, near, :], ref.at[pl.ds(0, members), :], sems.at[3 * i])
            yield pltpu.make_async_copy(ens_hbm.at[:, second, :], ref.at[pl.ds(members, members), :], sems.at[3 * i + 1])
            yield pltpu.make_async_copy(flow_hbm.at[:, near, :], ref.at[pl.ds(2 * members, 3), :], sems.at[3 * i + 2])

    def bring(refs):
        for copy in list(copies(refs)):
            copy.start()
        for copy in list(copies(refs)):
            copy.wait()

    pl.when(is_even)(lambda: bring((even_ref, odd_ref)))
    pl.when(jnp.logical_not(is_even))(lambda: bring((odd_ref, even_ref)))


def halo_rows(even_ref, odd_ref, members):
    at = lax.axis_index("gy")
    is_even = at % 2 == 0
    inside = at > 0, at < lax.axis_size("gy") - 1
    parts = []
    for lo, hi in ((0, members), (members, 2 * members), (2 * members, 2 * members + 3)):
        e, o = even_ref[lo:hi, :], odd_ref[lo:hi, :]
        pair = jnp.where(is_even, o, e), jnp.where(is_even, e, o)
        parts.append([jnp.where(here, x, 0.0) for here, x in zip(inside, pair)])
    return tuple(p[0] for p in parts), tuple(p[1] for p in parts)


def tall_coefficients(scratch, flow_ref, north_flow, south_flow, count):
    for k in range(3):
        scratch[k, 0:count, :] = flow_ref[k]
        scratch[k, count:, :] = jnp.zeros((EDGE - count, 128), F32)
        scratch[k, count : count + 1, :] = south_flow[k : k + 1]
        scratch[k, EDGE - 1 : EDGE, :] = north_flow[k : k + 1]
    return coefficients(*[scratch[k] for k in range(3)])


def tall_field(field_ref, north, south, members, count):
    field = {-2: north[1], -1: north[0], count: south[0], count + 1: south[1]}
    field.update({r: field_ref[r * members : (r + 1) * members, :] for r in range(count)})
    return field


def spread(w, coeffs, lane):
    own, up, down, left, right = coeffs
    to_west, to_east = left * w, right * w
    inside = (
        own * w
        + pltpu.roll(up * w, EDGE - 1, 0)
        + pltpu.roll(down * w, 1, 0)
        + jnp.where(lane == 127, 0.0, shifted(to_west, -1))
        + jnp.where(lane == 0, 0.0, shifted(to_east, 1))
    )
    has_west = lax.axis_index("gx") > 0
    has_east = lax.axis_index("gx") < lax.axis_size("gx") - 1
    return inside, jnp.where(has_west, to_west[:, 0:1], 0.0), jnp.where(has_east, to_east[:, 127:128], 0.0)


def prepare(
    members, count, n_obs, ens_hbm, flow_hbm, cell_hbm, value_hbm, var_hbm, sent_ref,
    field_ref, flow_ref, packed_ref, meta_ref, weight_ref, rest_ref, cell_ref, value_ref, var_ref, tall_ref, sems,
):
    copies = [
        pltpu.make_async_copy(ens_hbm.at[:, r, :], field_ref.at[pl.ds(r * members, members), :], sems.at[r])
        for r in range(count)
    ]
    pairs = ((flow_hbm, flow_ref), (cell_hbm, cell_ref), (value_hbm, value_ref), (var_hbm, var_ref))
    copies += [pltpu.make_async_copy(src, dst, sems.at[count + i]) for i, (src, dst) in enumerate(pairs)]
    for copy in copies:
        copy.start()
    for copy in copies:
        copy.wait()
    lane, sub = lanes((EDGE, 128)), rows_of((EDGE, 128))
    wide = lanes((members, 128))
    nothing = jnp.zeros((3, 128), F32)
    coeffs = tall_coefficients(tall_ref, flow_ref, nothing, nothing, count)
    coeffs = (jnp.where(sub < count, coeffs[0], 0.0),) + coeffs[1:]
    own, up, down, left, right = coeffs
    field = [field_ref[r * members : (r + 1) * members, :] for r in range(count)]
    packed = jnp.zeros((members, 128), F32)
    second = jnp.zeros((members, 128), F32)
    for r, x in enumerate(field):
        packed = jnp.where(wide == r, shifted(x, r), packed)
        packed = jnp.where(wide == EDGE + r, shifted(x, EDGE + r - 127), packed)
        second = jnp.where(wide == r, shifted(x, r - 1), second)
        second = jnp.where(wide == EDGE + r, shifted(x, EDGE + r - 126), second)

    def edge_row(low, high):
        both = jnp.where(lane == sub, low[:, 0:1], jnp.where(lane == sub + EDGE, high[:, 127:128], 0.0))
        return jnp.sum(both, axis=0, keepdims=True)

    middle = (
        edge_row(own, own) * packed
        + edge_row(up, up) * shifted(packed, 1)
        + edge_row(down, down) * shifted(packed, -1)
        + edge_row(right, left) * second
    )
    packed = jnp.where((wide >= 32) & (wide < 40), shifted(middle, 32), packed)
    packed = jnp.where((wide >= 40) & (wide < 48), shifted(middle, 24), packed)
    top_lane, top_sub = lane[:8], sub[:8]
    blocks = []
    for ref, rest in ((value_ref, 0.0), (var_ref, 1.0)):
        block = jnp.full((8, 128), rest, F32)
        for j in range(n_obs):
            block = jnp.where(top_sub == j, ref[j], block)
        blocks.append(block)
    meta = jnp.where(top_lane == VALUE, blocks[0], 0.0)
    meta = jnp.where(top_lane == FACTOR, lax.rsqrt(blocks[1]), meta)
    meta = jnp.where(top_lane == TO_WEST, left[:8, 0:1], meta)
    meta = jnp.where(top_lane == TO_EAST, right[:8, 127:128], meta)
    for j in range(n_obs):
        here = jnp.where((sub < count) & (sub * 128 + lane == cell_ref[j]), 1.0, 0.0)
        first, mid_west, mid_east = spread(here, coeffs, lane)
        w, west, east = spread(first, coeffs, lane)
        weight_ref[j] = first
        rest_ref[j] = w
        total = w[0:1, :] * field[0]
        for r in range(1, count):
            total = total + w[r : r + 1, :] * field[r]
        packed = jnp.where(wide == 48 + j, jnp.sum(total, axis=1, keepdims=True), packed)
        for k, column in ((0, west), (2, east), (4, mid_west), (5, mid_east)):
            meta = jnp.where(top_lane == WEIGHTS + k * n_obs + j, column[:8], meta)
    packed_ref[...] = packed
    meta_ref[0:8, :] = meta
    last = count - 1
    fix = jnp.zeros((8, 128), F32)
    for at, c, r, col in ((32, up, 0, 0), (40, up, 0, 127), (32 + last, down, last, 0), (40 + last, down, last, 127)):
        fix = jnp.where(top_lane == at, c[r : r + 1, col : col + 1], fix)
    meta_ref[8:16, :] = fix


def observe(
    members, count, n_obs, field_ref, flow_ref, packed_ref, meta_ref, weight_ref, rest_ref, odd_ref, even_ref,
    out_ref, tall_ref,
):
    north, south = halo_rows(even_ref, odd_ref, members)
    lane, sub = lanes((EDGE, 128)), rows_of((EDGE, 128))
    wide = lanes((members, 128))
    for k in range(3):
        tall_ref[k] = jnp.zeros((EDGE, 128), F32)
        tall_ref[k, count : count + 1, :] = south[2][k : k + 1]
        tall_ref[k, EDGE - 1 : EDGE, :] = north[2][k : k + 1]
    coeffs = coefficients(*[tall_ref[k] for k in range(3)])
    coeffs = (jnp.where((sub == count) | (sub == EDGE - 1), coeffs[0], 0.0),) + coeffs[1:]
    rows = {-2: north[1], -1: north[0], count: south[0], count + 1: south[1]}
    tile_rows = {r: field_ref[r * members : (r + 1) * members, :] for r in (0, count - 1)}
    packed, meta, fix = packed_ref[...], meta_ref[0:8, :], meta_ref[8:9, :]
    for x, slot, at in ((rows[-1], EDGE - 1, 0), (rows[count], count, count - 1)):
        packed = jnp.where(wide == slot, shifted(x, slot), packed)
        packed = jnp.where(wide == EDGE + slot, shifted(x, EDGE + slot - 127), packed)
        moved = jnp.where(wide == 32 + at, shifted(x, 32 + at), 0.0)
        moved = jnp.where(wide == 40 + at, shifted(x, 40 + at - 127), moved)
        packed = packed + fix * moved
    top_lane = lane[:8]
    for j in range(n_obs):
        w, west, east = spread(weight_ref[j], coeffs, lane)
        all_w = w + rest_ref[j]
        total = sum(all_w[r % EDGE : r % EDGE + 1, :] * x for r, x in rows.items())
        total += sum(w[r : r + 1, :] * x for r, x in tile_rows.items())
        packed = jnp.where(wide == 48 + j, packed + jnp.sum(total, axis=1, keepdims=True), packed)
        for k, column in ((1, west), (3, east)):
            meta = jnp.where(top_lane == WEIGHTS + k * n_obs + j, column[8:], meta)
    turned = jnp.concatenate([packed, jnp.zeros((128 - members, 128), F32)], axis=0).T
    out_ref[0:EDGE, :] = turned[0:EDGE] + shifted(turned[EDGE : 2 * EDGE], 64)
    out_ref[MID : MID + 8, :] = turned[32:40] + shifted(turned[40:48], 64)
    out_ref[OBS : OBS + 8, :] = turned[48:56] + meta


def block_rows(ref, start, tile, size, rows):
    return ref[pl.ds(pl.multiple_of(place_of(tile, size) * BLOCK + start, 8), rows), :]


def side_columns(ref, tile, size):
    west, east = jnp.maximum(tile - 1, 0), jnp.minimum(tile + 1, size - 1)
    own = block_rows(ref, 0, tile, size, EDGE)
    west_x = shifted(block_rows(ref, 0, west, size, EDGE), 64)
    east_x = block_rows(ref, 0, east, size, EDGE)
    west_mid = shifted(block_rows(ref, MID, west, size, 8), 64)
    west_mid += block_rows(ref, OBS, west, size, 8)[:, TO_EAST : TO_EAST + 1] * own[:8]
    east_mid = block_rows(ref, MID, east, size, 8)
    east_mid += block_rows(ref, OBS, east, size, 8)[:, TO_WEST : TO_WEST + 1] * shifted(own[:8], 64)
    return west_x, east_x, west_mid, east_mid


def complete(members, n_obs, size, blocks_ref, out_ref):
    rows = n_obs * size
    lane, sub = lanes((rows, 128)), rows_of((rows, 128))
    at = own = jnp.zeros((rows, 128), F32)
    for tile in range(size):
        west, east, west_mid, east_mid = side_columns(blocks_ref, jnp.int32(tile), size)
        block = block_rows(blocks_ref, OBS, jnp.int32(tile), size, 8)
        terms = (west[:8], west[8:], east[:8], east[8:], west_mid, east_mid)
        for j in range(n_obs):
            places = [WEIGHTS + k * n_obs + j for k in range(len(terms))]
            total = sum(block[:, a : a + 1] * term for a, term in zip(places, terms))
            row = jnp.sum(total, axis=0, keepdims=True) + block[j : j + 1, :]
            here = sub == n_obs * tile + j
            at = jnp.where(here, row, at)
            own = jnp.where(here, block[j : j + 1, :], own)
    at = jnp.where(lane < members, at, 0.0)
    mean = jnp.sum(at, axis=1, keepdims=True) * (1.0 / members)
    raw = jnp.where(lane < members, at - mean, jnp.where(lane == members, own[:, VALUE : VALUE + 1] - mean, 0.0))
    out_ref[...] = raw * own[:, FACTOR : FACTOR + 1]


def forecast(members, count, size, field_ref, flow_ref, odd_ref, even_ref, blocks_ref, out_ref, mean_ref, tall_ref):
    north, south = halo_rows(even_ref, odd_ref, members)
    tile = lax.axis_index("gx")
    west, east, west_mid, east_mid = side_columns(blocks_ref, tile, size)
    has_west, has_east = tile > 0, tile < size - 1
    sides = [jnp.where(has_west, west, 0.0), jnp.where(has_east, east, 0.0)]
    sides += [jnp.where(has_west, west_mid, 0.0), jnp.where(has_east, east_mid, 0.0), jnp.zeros((80, 128), F32)]
    sides = jnp.concatenate(sides, axis=0).T[:members]
    field = tall_field(field_ref, north, south, members, count)
    tall = tall_coefficients(tall_ref, flow_ref, north[2], south[2], count)
    lane = lanes((members, 128))

    def step(rows, r, west_at, east_at):
        w = jnp.where(lane == 0, shifted(sides, -west_at), shifted(rows[r], 1))
        e = jnp.where(lane == 127, shifted(sides, 127 - east_at), shifted(rows[r], -1))
        at = r % EDGE
        return combine([c[at : at + 1, :] for c in tall], rows[r], rows[r - 1], rows[r + 1], w, e)

    middle = {r: step(field, r, r % EDGE, EDGE + r % EDGE) for r in range(-1, count + 1)}
    for r in range(count):
        x = step(middle, r, 2 * EDGE + r, 2 * EDGE + 8 + r)
        mean = jnp.sum(x, axis=0, keepdims=True) * (1.0 / members)
        mean_ref[r : r + 1, :] = mean
        x = x - mean
        high = x.astype(jnp.bfloat16)
        at = slice(128 * r, 128 * (r + 1))
        out_ref[0:members, at] = high
        out_ref[members : 2 * members, at] = (x - high.astype(F32)).astype(jnp.bfloat16)
        out_ref[2 * members :, at] = high


def eliminated(a, members, column_ref):
    size = 8
    lane, sub = lanes((size, 128)), rows_of((size, 128))
    part = [a[size * q : size * (q + 1), :] for q in range(members // size)]
    pivot = []

    def spread(q, c):
        return jnp.broadcast_to(part[q][:, c : c + 1], (size, 128))

    ahead = {(0, c): spread(0, c) for c in range(size)}
    for p in range(len(part)):
        start, end = size * p, size * (p + 1)
        rest = range(p, len(part))
        column = {(q, c): spread(q, c) for q in rest[1:] for c in range(start, end)}
        column.update(ahead)
        more = range(end, end + size if p + 1 < len(part) else end)
        column.update({(q, c): spread(q, c) for q in rest[1:2] for c in more})
        mine = (lane >= start) & (lane < end)
        for q in rest:
            part[q] = jnp.where(mine, 0.0, part[q])
        found = jnp.zeros((size, 128), F32)
        for j in range(size):
            at = start + j
            value = column[p, at][j : j + 1, :]
            found = jnp.where(sub == j, value, found)
            inverse = 1.0 / value
            unit = jnp.where(lane[:1] == at, 1.0, part[p][j : j + 1, :])
            pivots = {c: column[p, c][j : j + 1, :] for c in range(at + 1, end)}
            if more:
                column_ref[at] = column[p + 1, at]
            pivots.update({c: column_ref[at, c - end : c - end + 1, :] for c in more})
            for q in rest:
                factor = column[q, at] * inverse
                for c in range(at + 1, end + (len(more) if q == p + 1 else 0)):
                    column[q, c] = column[q, c] - factor * pivots[c]
                if q == p:
                    factor = jnp.where(sub > j, factor, 0.0)
                part[q] = part[q] - factor * unit
        pivot.append(found)
        ahead = {(p + 1, c): column[p + 1, c] for c in more}
    return jnp.concatenate(part, axis=0), jnp.concatenate(pivot, axis=0)


def thirds(x):
    first = x.astype(jnp.bfloat16)
    rest = x - first.astype(F32)
    second = rest.astype(jnp.bfloat16)
    return first, second, (rest - second.astype(F32)).astype(jnp.bfloat16)


def product(lefts, rights):
    left, right = jnp.concatenate(lefts, axis=1), jnp.concatenate(rights, axis=0)
    return jnp.dot(left, right, preferred_element_type=F32)


def analyse(members, count, f_ref, mean_ref, *refs):
    out_ref, column_ref = refs[-2:]
    scaled = jnp.concatenate([ref[...] for ref in refs[:-2]], axis=0)
    a1, a2, a3 = thirds(scaled)
    t1, t2, t3 = thirds(scaled.T[:members])
    full = product([t1, t2], [a1, a1]) + (product([t1, t2], [a2, a2]) + product([t1, t3], [a3, a1]))
    lane, sub = lanes((members, 128)), rows_of((members, 128))
    a, pivots = eliminated(full + jnp.where(lane == sub, members - 1.0, 0.0), members, column_ref)
    scale = lax.rsqrt(pivots)
    inverse = scale * jnp.where(lane < sub, a, jnp.where(lane == sub, 1.0, 0.0))
    reduced = scale * a[:, members : members + 1]
    weights = jnp.sum(reduced * inverse, axis=0, keepdims=True)
    transform = (jnp.sqrt(members - 1.0) * inverse + weights)[:, :members]
    high = transform.astype(jnp.bfloat16)
    low = (transform - high.astype(F32)).astype(jnp.bfloat16)
    update = product([high, high, low], [f_ref[...]])
    for r in range(count):
        out_ref[pl.ds(r, members, stride=count), :] = update[:, 128 * r : 128 * (r + 1)] + mean_ref[r : r + 1, :]


def swap(x, axis, offset):
    ny, nx = lax.axis_size("gy"), lax.axis_size("gx")
    partner = {i: i for i in range(ny)}
    for i in range(offset, ny - 1, 2):
        partner[i], partner[i + 1] = i + 1, i
    pairs = []
    for a in range(ny):
        for b in range(nx):
            if partner[a] != a:
                pairs.append((a * nx + b, partner[a] * nx + b))
            elif nx % 2 == 0:
                pairs.append((a * nx + b, a * nx + (b ^ 1)))
    return lax.ppermute(x, ("gy", "gx"), pairs)


def two_power(size):
    return size & (size - 1) == 0


def partner(x, flip_y, flip_x):
    ny, nx = lax.axis_size("gy"), lax.axis_size("gx")
    pairs = [(a * nx + b, (a ^ flip_y) * nx + (b ^ flip_x)) for a in range(ny) for b in range(nx)]
    return lax.ppermute(x, ("gy", "gx"), pairs)


def doubled(x, flip_y, flip_x):
    return jnp.concatenate([x, partner(x, flip_y, flip_x)], axis=0)


def row_blocks(block):
    size = step = lax.axis_size("gx")
    if not two_power(size):
        return lax.all_gather(block, "gx", tiled=True)
    while step > 2:
        step //= 2
        block = doubled(block, 0, step | 1)
    return doubled(block, 0, 1) if size > 1 else block


def place_of(tile, size):
    if not two_power(size) or size == 1:
        return tile
    distance = jnp.bitwise_xor(lax.axis_index("gx"), tile)
    place, last, value, bit = 0, distance % 2, 1, size // 2
    while bit > 1:
        chosen = (distance // bit) % 2
        place, last = place + chosen * value, jnp.bitwise_xor(last, chosen)
        value, bit = 2 * value, bit // 2
    return place + last * value


def all_rows(packet):
    ny, nx = lax.axis_size("gy"), lax.axis_size("gx")
    if not two_power(ny) or ny < 4 or nx % 2:
        return [lax.all_gather(packet, "gy", tiled=True)]
    step = ny // 2
    while step > 2:
        packet = doubled(packet, step, 1)
        step //= 2
    pairs = [(a * nx + b, (a ^ (2 - b % 2)) * nx + (b ^ 1)) for a in range(ny) for b in range(nx)]
    near = lax.ppermute(packet, ("gy", "gx"), pairs)
    return [packet, near, partner(packet, 3, 1), partner(near, 0, 1)]


def body(ensemble, flow, obs_cell, obs_value, obs_var):
    members, count, width = ensemble.shape
    n_obs = obs_cell.shape[-1]
    size = lax.axis_size("gx")
    call = functools.partial(pl.pallas_call, compiler_params=PARAMS)

    def shape(*dims):
        return jax.ShapeDtypeStruct(dims + (width,), F32)

    inputs = [
        pltpu.with_memory_space_constraint(x, pltpu.HBM)
        for x in (ensemble, flow, obs_cell.reshape(-1), obs_value.reshape(-1), obs_var.reshape(-1))
    ]
    rows_even, rows_odd = call(
        functools.partial(load, members, count),
        out_shape=[shape(2 * members + 8)] * 2,
        in_specs=[HBM] * 2,
        out_specs=[VMEM] * 2,
        scratch_shapes=[pltpu.SemaphoreType.DMA((6,))],
        name="load",
    )(*inputs[:2])
    tall = pltpu.VMEM((3, EDGE, width), F32)
    field, tile_flow, *ready = call(
        functools.partial(prepare, members, count, n_obs),
        out_shape=[shape(members * count), shape(3, count), shape(members), shape(16)] + [shape(n_obs, EDGE)] * 2,
        in_specs=[HBM] * 5 + [ANY],
        out_specs=[VMEM] * 6,
        scratch_shapes=[pltpu.SMEM((n_obs,), jnp.int32)]
        + [pltpu.SMEM((n_obs,), F32)] * 2
        + [tall, pltpu.SemaphoreType.DMA((count + 4,))],
        cost_estimate=pl.CostEstimate(flops=4 * 10**6, bytes_accessed=6 * 10**5, transcendentals=0),
        name="prepare",
    )(*inputs, rows_even)
    rows_odd = swap(rows_odd, "gy", 1)
    rows_even = swap(rows_even, "gy", 0)
    block = call(
        functools.partial(observe, members, count, n_obs),
        out_shape=shape(BLOCK),
        in_specs=[VMEM] * 8,
        out_specs=VMEM,
        scratch_shapes=[tall],
        name="observe",
    )(field, tile_flow, *ready, rows_odd, rows_even)
    blocks = row_blocks(block)
    packet = call(
        functools.partial(complete, members, n_obs, size),
        out_shape=shape(n_obs * size),
        in_specs=[VMEM],
        out_specs=VMEM,
        name="complete",
    )(blocks)
    anomaly, mean = call(
        functools.partial(forecast, members, count, size),
        out_shape=[jax.ShapeDtypeStruct((3 * members, count * width), jnp.bfloat16), shape(count)],
        in_specs=[VMEM] * 5,
        out_specs=[VMEM] * 2,
        scratch_shapes=[tall],
        cost_estimate=pl.CostEstimate(flops=4 * 10**6, bytes_accessed=6 * 10**5, transcendentals=0),
        name="forecast",
    )(field, tile_flow, rows_odd, rows_even, blocks)
    packets = all_rows(packet)
    out = call(
        functools.partial(analyse, members, count),
        out_shape=shape(members * count),
        in_specs=[VMEM] * (2 + len(packets)),
        out_specs=VMEM,
        scratch_shapes=[pltpu.VMEM((members, 8, width), F32)],
        name="analyse",
    )(anomaly, mean, *packets)
    return out.reshape(ensemble.shape)


def solution(mesh):
    return jax.shard_map(
        body,
        mesh=mesh,
        in_specs=(
            P(None, "gy", "gx"),
            P(None, "gy", "gx"),
            P("gy", "gx", None),
            P("gy", "gx", None),
            P("gy", "gx", None),
        ),
        out_specs=P(None, "gy", "gx"),
        check_vma=False,
    )
```

```python
import functools

import jax
import jax.numpy as jnp
from jax import lax
from jax.experimental import pallas as pl
from jax.experimental.pallas import tpu as pltpu
from jax.sharding import PartitionSpec as P

F32 = jnp.float32
PARAMS = pltpu.CompilerParams(vmem_limit_bytes=24 * 1024 * 1024)
VMEM = pl.BlockSpec(memory_space=pltpu.VMEM)
SMEM = pl.BlockSpec(memory_space=pltpu.SMEM)


def lanes(shape):
    return lax.broadcasted_iota(jnp.int32, shape, len(shape) - 1)


def rows_of(shape):
    return lax.broadcasted_iota(jnp.int32, shape, len(shape) - 2)


def shifted(x, amount):
    return pltpu.roll(x, amount % x.shape[-1], x.ndim - 1)


EDGE = 16
BLOCK = EDGE + 16
MID, OBS = EDGE, EDGE + 8
VALUE, FACTOR, TO_WEST, TO_EAST, WEIGHTS = 64, 65, 66, 67, 72
HBM = pl.BlockSpec(memory_space=pltpu.HBM)
ANY = pl.BlockSpec(memory_space=pl.ANY)


def coefficients(k, u, v):
    return 1.0 - 4.0 * k, k + 0.5 * v, k - 0.5 * v, k + 0.5 * u, k - 0.5 * u


def combine(c, own, north, south, west, east):
    return c[0] * own + c[1] * north + c[2] * south + c[3] * west + c[4] * east


def transposed(x):
    return jnp.concatenate([x, jnp.zeros((128 - x.shape[0], 128), F32)], axis=0).T


def load(members, count, ens_hbm, flow_hbm, even_ref, odd_ref, sems):
    is_even = lax.axis_index("gy") % 2 == 0
    for ref in (even_ref, odd_ref):
        ref[2 * members :, :] = jnp.zeros((8, 128), F32)

    def copies(refs):
        for i, (ref, near, second) in enumerate(zip(refs, (count - 1, 0), (count - 2, 1))):
            yield pltpu.make_async_copy(ens_hbm.at[:, near, :], ref.at[pl.ds(0, members), :], sems.at[3 * i])
            yield pltpu.make_async_copy(ens_hbm.at[:, second, :], ref.at[pl.ds(members, members), :], sems.at[3 * i + 1])
            yield pltpu.make_async_copy(flow_hbm.at[:, near, :], ref.at[pl.ds(2 * members, 3), :], sems.at[3 * i + 2])

    def bring(refs):
        for copy in list(copies(refs)):
            copy.start()
        for copy in list(copies(refs)):
            copy.wait()

    pl.when(is_even)(lambda: bring((even_ref, odd_ref)))
    pl.when(jnp.logical_not(is_even))(lambda: bring((odd_ref, even_ref)))


def halo_rows(even_ref, odd_ref, members):
    at = lax.axis_index("gy")
    is_even = at % 2 == 0
    inside = at > 0, at < lax.axis_size("gy") - 1
    parts = []
    for lo, hi in ((0, members), (members, 2 * members), (2 * members, 2 * members + 3)):
        e, o = even_ref[lo:hi, :], odd_ref[lo:hi, :]
        pair = jnp.where(is_even, o, e), jnp.where(is_even, e, o)
        parts.append([jnp.where(here, x, 0.0) for here, x in zip(inside, pair)])
    return tuple(p[0] for p in parts), tuple(p[1] for p in parts)


def tall_coefficients(scratch, flow_ref, north_flow, south_flow, count):
    for k in range(3):
        scratch[k, 0:count, :] = flow_ref[k]
        scratch[k, count:, :] = jnp.zeros((EDGE - count, 128), F32)
        scratch[k, count : count + 1, :] = south_flow[k : k + 1]
        scratch[k, EDGE - 1 : EDGE, :] = north_flow[k : k + 1]
    return coefficients(*[scratch[k] for k in range(3)])


def tall_field(field_ref, north, south, members, count):
    field = {-2: north[1], -1: north[0], count: south[0], count + 1: south[1]}
    field.update({r: field_ref[r * members : (r + 1) * members, :] for r in range(count)})
    return field


def spread(w, coeffs, lane):
    own, up, down, left, right = coeffs
    to_west, to_east = left * w, right * w
    inside = (
        own * w
        + pltpu.roll(up * w, EDGE - 1, 0)
        + pltpu.roll(down * w, 1, 0)
        + jnp.where(lane == 127, 0.0, shifted(to_west, -1))
        + jnp.where(lane == 0, 0.0, shifted(to_east, 1))
    )
    has_west = lax.axis_index("gx") > 0
    has_east = lax.axis_index("gx") < lax.axis_size("gx") - 1
    return inside, jnp.where(has_west, to_west[:, 0:1], 0.0), jnp.where(has_east, to_east[:, 127:128], 0.0)


def prepare(
    members, count, n_obs, ens_hbm, flow_hbm, cell_hbm, value_hbm, var_hbm, sent_ref,
    field_ref, flow_ref, packed_ref, meta_ref, weight_ref, rest_ref, cell_ref, value_ref, var_ref, tall_ref, sems,
):
    copies = [
        pltpu.make_async_copy(ens_hbm.at[:, r, :], field_ref.at[pl.ds(r * members, members), :], sems.at[r])
        for r in range(count)
    ]
    pairs = ((flow_hbm, flow_ref), (cell_hbm, cell_ref), (value_hbm, value_ref), (var_hbm, var_ref))
    copies += [pltpu.make_async_copy(src, dst, sems.at[count + i]) for i, (src, dst) in enumerate(pairs)]
    for copy in copies:
        copy.start()
    for copy in copies:
        copy.wait()
    lane, sub = lanes((EDGE, 128)), rows_of((EDGE, 128))
    wide = lanes((members, 128))
    nothing = jnp.zeros((3, 128), F32)
    coeffs = tall_coefficients(tall_ref, flow_ref, nothing, nothing, count)
    coeffs = (jnp.where(sub < count, coeffs[0], 0.0),) + coeffs[1:]
    own, up, down, left, right = coeffs
    field = [field_ref[r * members : (r + 1) * members, :] for r in range(count)]
    packed = jnp.zeros((members, 128), F32)
    second = jnp.zeros((members, 128), F32)
    for r, x in enumerate(field):
        packed = jnp.where(wide == r, shifted(x, r), packed)
        packed = jnp.where(wide == EDGE + r, shifted(x, EDGE + r - 127), packed)
        second = jnp.where(wide == r, shifted(x, r - 1), second)
        second = jnp.where(wide == EDGE + r, shifted(x, EDGE + r - 126), second)

    def edge_row(low, high):
        both = jnp.where(lane == sub, low[:, 0:1], jnp.where(lane == sub + EDGE, high[:, 127:128], 0.0))
        return jnp.sum(both, axis=0, keepdims=True)

    middle = (
        edge_row(own, own) * packed
        + edge_row(up, up) * shifted(packed, 1)
        + edge_row(down, down) * shifted(packed, -1)
        + edge_row(right, left) * second
    )
    packed = jnp.where((wide >= 32) & (wide < 40), shifted(middle, 32), packed)
    packed = jnp.where((wide >= 40) & (wide < 48), shifted(middle, 24), packed)
    top_lane, top_sub = lane[:8], sub[:8]
    blocks = []
    for ref, rest in ((value_ref, 0.0), (var_ref, 1.0)):
        block = jnp.full((8, 128), rest, F32)
        for j in range(n_obs):
            block = jnp.where(top_sub == j, ref[j], block)
        blocks.append(block)
    meta = jnp.where(top_lane == VALUE, blocks[0], 0.0)
    meta = jnp.where(top_lane == FACTOR, lax.rsqrt(blocks[1]), meta)
    meta = jnp.where(top_lane == TO_WEST, left[:8, 0:1], meta)
    meta = jnp.where(top_lane == TO_EAST, right[:8, 127:128], meta)
    for j in range(n_obs):
        here = jnp.where((sub < count) & (sub * 128 + lane == cell_ref[j]), 1.0, 0.0)
        first, mid_west, mid_east = spread(here, coeffs, lane)
        w, west, east = spread(first, coeffs, lane)
        weight_ref[j] = first
        rest_ref[j] = w
        total = w[0:1, :] * field[0]
        for r in range(1, count):
            total = total + w[r : r + 1, :] * field[r]
        packed = jnp.where(wide == 48 + j, jnp.sum(total, axis=1, keepdims=True), packed)
        for k, column in ((0, west), (2, east), (4, mid_west), (5, mid_east)):
            meta = jnp.where(top_lane == WEIGHTS + k * n_obs + j, column[:8], meta)
    packed_ref[...] = packed
    meta_ref[0:8, :] = meta
    last = count - 1
    fix = jnp.zeros((8, 128), F32)
    for at, c, r, col in ((32, up, 0, 0), (40, up, 0, 127), (32 + last, down, last, 0), (40 + last, down, last, 127)):
        fix = jnp.where(top_lane == at, c[r : r + 1, col : col + 1], fix)
    meta_ref[8:16, :] = fix


def observe(
    members, count, n_obs, field_ref, flow_ref, packed_ref, meta_ref, weight_ref, rest_ref, odd_ref, even_ref,
    out_ref, tall_ref,
):
    north, south = halo_rows(even_ref, odd_ref, members)
    lane, sub = lanes((EDGE, 128)), rows_of((EDGE, 128))
    wide = lanes((members, 128))
    for k in range(3):
        tall_ref[k] = jnp.zeros((EDGE, 128), F32)
        tall_ref[k, count : count + 1, :] = south[2][k : k + 1]
        tall_ref[k, EDGE - 1 : EDGE, :] = north[2][k : k + 1]
    coeffs = coefficients(*[tall_ref[k] for k in range(3)])
    coeffs = (jnp.where((sub == count) | (sub == EDGE - 1), coeffs[0], 0.0),) + coeffs[1:]
    rows = {-2: north[1], -1: north[0], count: south[0], count + 1: south[1]}
    tile_rows = {r: field_ref[r * members : (r + 1) * members, :] for r in (0, count - 1)}
    packed, meta, fix = packed_ref[...], meta_ref[0:8, :], meta_ref[8:9, :]
    for x, slot, at in ((rows[-1], EDGE - 1, 0), (rows[count], count, count - 1)):
        packed = jnp.where(wide == slot, shifted(x, slot), packed)
        packed = jnp.where(wide == EDGE + slot, shifted(x, EDGE + slot - 127), packed)
        moved = jnp.where(wide == 32 + at, shifted(x, 32 + at), 0.0)
        moved = jnp.where(wide == 40 + at, shifted(x, 40 + at - 127), moved)
        packed = packed + fix * moved
    top_lane = lane[:8]
    for j in range(n_obs):
        w, west, east = spread(weight_ref[j], coeffs, lane)
        all_w = w + rest_ref[j]
        total = sum(all_w[r % EDGE : r % EDGE + 1, :] * x for r, x in rows.items())
        total += sum(w[r : r + 1, :] * x for r, x in tile_rows.items())
        packed = jnp.where(wide == 48 + j, packed + jnp.sum(total, axis=1, keepdims=True), packed)
        for k, column in ((1, west), (3, east)):
            meta = jnp.where(top_lane == WEIGHTS + k * n_obs + j, column[8:], meta)
    turned = jnp.concatenate([packed, jnp.zeros((128 - members, 128), F32)], axis=0).T
    out_ref[0:EDGE, :] = turned[0:EDGE] + shifted(turned[EDGE : 2 * EDGE], 64)
    out_ref[MID : MID + 8, :] = turned[32:40] + shifted(turned[40:48], 64)
    out_ref[OBS : OBS + 8, :] = turned[48:56] + meta


def block_rows(ref, start, tile, size, rows):
    return ref[pl.ds(pl.multiple_of(place_of(tile, size) * BLOCK + start, 8), rows), :]


def side_columns(ref, tile, size):
    west, east = jnp.maximum(tile - 1, 0), jnp.minimum(tile + 1, size - 1)
    own = block_rows(ref, 0, tile, size, EDGE)
    west_x = shifted(block_rows(ref, 0, west, size, EDGE), 64)
    east_x = block_rows(ref, 0, east, size, EDGE)
    west_mid = shifted(block_rows(ref, MID, west, size, 8), 64)
    west_mid += block_rows(ref, OBS, west, size, 8)[:, TO_EAST : TO_EAST + 1] * own[:8]
    east_mid = block_rows(ref, MID, east, size, 8)
    east_mid += block_rows(ref, OBS, east, size, 8)[:, TO_WEST : TO_WEST + 1] * shifted(own[:8], 64)
    return west_x, east_x, west_mid, east_mid


def complete(members, n_obs, size, blocks_ref, out_ref):
    rows = n_obs * size
    lane, sub = lanes((rows, 128)), rows_of((rows, 128))
    at = own = jnp.zeros((rows, 128), F32)
    for tile in range(size):
        west, east, west_mid, east_mid = side_columns(blocks_ref, jnp.int32(tile), size)
        block = block_rows(blocks_ref, OBS, jnp.int32(tile), size, 8)
        terms = []
        if tile > 0:
            terms += [(0, west[:8]), (1, west[8:]), (4, west_mid)]
        if tile < size - 1:
            terms += [(2, east[:8]), (3, east[8:]), (5, east_mid)]
        for j in range(n_obs):
            total = jnp.zeros((8, 128), F32)
            for k, term in terms:
                place = WEIGHTS + k * n_obs + j
                total = total + block[:, place : place + 1] * term
            row = jnp.sum(total, axis=0, keepdims=True) + block[j : j + 1, :]
            here = sub == n_obs * tile + j
            at = jnp.where(here, row, at)
            own = jnp.where(here, block[j : j + 1, :], own)
    at = jnp.where(lane < members, at, 0.0)
    mean = jnp.sum(at, axis=1, keepdims=True) * (1.0 / members)
    raw = jnp.where(lane < members, at - mean, jnp.where(lane == members, own[:, VALUE : VALUE + 1] - mean, 0.0))
    out_ref[...] = raw * own[:, FACTOR : FACTOR + 1]


def forecast(members, count, size, field_ref, flow_ref, odd_ref, even_ref, blocks_ref, out_ref, mean_ref, tall_ref):
    north, south = halo_rows(even_ref, odd_ref, members)
    tile = lax.axis_index("gx")
    west, east, west_mid, east_mid = side_columns(blocks_ref, tile, size)
    has_west, has_east = tile > 0, tile < size - 1
    sides = [jnp.where(has_west, west, 0.0), jnp.where(has_east, east, 0.0)]
    sides += [jnp.where(has_west, west_mid, 0.0), jnp.where(has_east, east_mid, 0.0), jnp.zeros((80, 128), F32)]
    sides = jnp.concatenate(sides, axis=0).T[:members]
    field = tall_field(field_ref, north, south, members, count)
    tall = tall_coefficients(tall_ref, flow_ref, north[2], south[2], count)
    lane = lanes((members, 128))

    def step(rows, r, west_at, east_at):
        w = jnp.where(lane == 0, shifted(sides, -west_at), shifted(rows[r], 1))
        e = jnp.where(lane == 127, shifted(sides, 127 - east_at), shifted(rows[r], -1))
        at = r % EDGE
        return combine([c[at : at + 1, :] for c in tall], rows[r], rows[r - 1], rows[r + 1], w, e)

    middle = {r: step(field, r, r % EDGE, EDGE + r % EDGE) for r in range(-1, count + 1)}
    for r in range(count):
        x = step(middle, r, 2 * EDGE + r, 2 * EDGE + 8 + r)
        mean = jnp.sum(x, axis=0, keepdims=True) * (1.0 / members)
        mean_ref[r : r + 1, :] = mean
        x = x - mean
        high = x.astype(jnp.bfloat16)
        at = slice(128 * r, 128 * (r + 1))
        out_ref[0:members, at] = high
        out_ref[members : 2 * members, at] = (x - high.astype(F32)).astype(jnp.bfloat16)
        out_ref[2 * members :, at] = high


def eliminated(a, members, column_ref):
    size = 8
    lane, sub = lanes((size, 128)), rows_of((size, 128))
    part = [a[size * q : size * (q + 1), :] for q in range(members // size)]
    pivot = []

    def spread(q, c):
        return jnp.broadcast_to(part[q][:, c : c + 1], (size, 128))

    ahead = {(0, c): spread(0, c) for c in range(size)}
    for p in range(len(part)):
        start, end = size * p, size * (p + 1)
        rest = range(p, len(part))
        column = {(q, c): spread(q, c) for q in rest[1:] for c in range(start, end)}
        column.update(ahead)
        more = range(end, end + size if p + 1 < len(part) else end)
        column.update({(q, c): spread(q, c) for q in rest[1:2] for c in more})
        mine = (lane >= start) & (lane < end)
        for q in rest:
            part[q] = jnp.where(mine, 0.0, part[q])
        found = jnp.zeros((size, 128), F32)
        for j in range(size):
            at = start + j
            value = column[p, at][j : j + 1, :]
            found = jnp.where(sub == j, value, found)
            inverse = 1.0 / value
            unit = jnp.where(lane[:1] == at, 1.0, part[p][j : j + 1, :])
            pivots = {c: column[p, c][j : j + 1, :] for c in range(at + 1, end)}
            if more:
                column_ref[at] = column[p + 1, at]
            pivots.update({c: column_ref[at, c - end : c - end + 1, :] for c in more})
            for q in rest:
                factor = column[q, at] * inverse
                for c in range(at + 1, end + (len(more) if q == p + 1 else 0)):
                    column[q, c] = column[q, c] - factor * pivots[c]
                if q == p:
                    factor = jnp.where(sub > j, factor, 0.0)
                part[q] = part[q] - factor * unit
        pivot.append(found)
        ahead = {(p + 1, c): column[p + 1, c] for c in more}
    return jnp.concatenate(part, axis=0), jnp.concatenate(pivot, axis=0)


def thirds(x):
    first = x.astype(jnp.bfloat16)
    rest = x - first.astype(F32)
    second = rest.astype(jnp.bfloat16)
    return first, second, (rest - second.astype(F32)).astype(jnp.bfloat16)


def product(lefts, rights):
    left, right = jnp.concatenate(lefts, axis=1), jnp.concatenate(rights, axis=0)
    return jnp.dot(left, right, preferred_element_type=F32)


def analyse(members, count, f_ref, mean_ref, *refs):
    out_ref, column_ref = refs[-2:]
    scaled = jnp.concatenate([ref[...] for ref in refs[:-2]], axis=0)
    a1, a2, a3 = thirds(scaled)
    t1, t2, t3 = thirds(scaled.T[:members])
    full = product([t1, t2], [a1, a1]) + (product([t1, t2], [a2, a2]) + product([t1, t3], [a3, a1]))
    lane, sub = lanes((members, 128)), rows_of((members, 128))
    a, pivots = eliminated(full + jnp.where(lane == sub, members - 1.0, 0.0), members, column_ref)
    scale = lax.rsqrt(pivots)
    inverse = scale * jnp.where(lane < sub, a, jnp.where(lane == sub, 1.0, 0.0))
    reduced = scale * a[:, members : members + 1]
    weights = jnp.sum(reduced * inverse, axis=0, keepdims=True)
    transform = (jnp.sqrt(members - 1.0) * inverse + weights)[:, :members]
    high = transform.astype(jnp.bfloat16)
    low = (transform - high.astype(F32)).astype(jnp.bfloat16)
    update = product([high, high, low], [f_ref[...]])
    for r in range(count):
        out_ref[pl.ds(r, members, stride=count), :] = update[:, 128 * r : 128 * (r + 1)] + mean_ref[r : r + 1, :]


def swap(x, axis, offset):
    ny, nx = lax.axis_size("gy"), lax.axis_size("gx")
    partner = {i: i for i in range(ny)}
    for i in range(offset, ny - 1, 2):
        partner[i], partner[i + 1] = i + 1, i
    pairs = []
    for a in range(ny):
        for b in range(nx):
            if partner[a] != a:
                pairs.append((a * nx + b, partner[a] * nx + b))
            elif nx % 2 == 0:
                pairs.append((a * nx + b, a * nx + (b ^ 1)))
    return lax.ppermute(x, ("gy", "gx"), pairs)


def two_power(size):
    return size & (size - 1) == 0


def partner(x, flip_y, flip_x):
    ny, nx = lax.axis_size("gy"), lax.axis_size("gx")
    pairs = [(a * nx + b, (a ^ flip_y) * nx + (b ^ flip_x)) for a in range(ny) for b in range(nx)]
    return lax.ppermute(x, ("gy", "gx"), pairs)


def doubled(x, flip_y, flip_x):
    return jnp.concatenate([x, partner(x, flip_y, flip_x)], axis=0)


def row_blocks(block):
    size = step = lax.axis_size("gx")
    if not two_power(size):
        return lax.all_gather(block, "gx", tiled=True)
    while step > 2:
        step //= 2
        block = doubled(block, 0, step | 1)
    return doubled(block, 0, 1) if size > 1 else block


def place_of(tile, size):
    if not two_power(size) or size == 1:
        return tile
    distance = jnp.bitwise_xor(lax.axis_index("gx"), tile)
    place, last, value, bit = 0, distance % 2, 1, size // 2
    while bit > 1:
        chosen = (distance // bit) % 2
        place, last = place + chosen * value, jnp.bitwise_xor(last, chosen)
        value, bit = 2 * value, bit // 2
    return place + last * value


def all_rows(packet):
    ny, nx = lax.axis_size("gy"), lax.axis_size("gx")
    if not two_power(ny) or ny < 4 or nx % 2:
        return [lax.all_gather(packet, "gy", tiled=True)]
    step = ny // 2
    while step > 2:
        packet = doubled(packet, step, 1)
        step //= 2
    pairs = [(a * nx + b, (a ^ (2 - b % 2)) * nx + (b ^ 1)) for a in range(ny) for b in range(nx)]
    near = lax.ppermute(packet, ("gy", "gx"), pairs)
    return [packet, near, partner(packet, 3, 1), partner(near, 0, 1)]


def body(ensemble, flow, obs_cell, obs_value, obs_var):
    members, count, width = ensemble.shape
    n_obs = obs_cell.shape[-1]
    size = lax.axis_size("gx")
    call = functools.partial(pl.pallas_call, compiler_params=PARAMS)

    def shape(*dims):
        return jax.ShapeDtypeStruct(dims + (width,), F32)

    inputs = [
        pltpu.with_memory_space_constraint(x, pltpu.HBM)
        for x in (ensemble, flow, obs_cell.reshape(-1), obs_value.reshape(-1), obs_var.reshape(-1))
    ]
    rows_even, rows_odd = call(
        functools.partial(load, members, count),
        out_shape=[shape(2 * members + 8)] * 2,
        in_specs=[HBM] * 2,
        out_specs=[VMEM] * 2,
        scratch_shapes=[pltpu.SemaphoreType.DMA((6,))],
        name="load",
    )(*inputs[:2])
    tall = pltpu.VMEM((3, EDGE, width), F32)
    field, tile_flow, *ready = call(
        functools.partial(prepare, members, count, n_obs),
        out_shape=[shape(members * count), shape(3, count), shape(members), shape(16)] + [shape(n_obs, EDGE)] * 2,
        in_specs=[HBM] * 5 + [ANY],
        out_specs=[VMEM] * 6,
        scratch_shapes=[pltpu.SMEM((n_obs,), jnp.int32)]
        + [pltpu.SMEM((n_obs,), F32)] * 2
        + [tall, pltpu.SemaphoreType.DMA((count + 4,))],
        cost_estimate=pl.CostEstimate(flops=4 * 10**6, bytes_accessed=6 * 10**5, transcendentals=0),
        name="prepare",
    )(*inputs, rows_even)
    rows_odd = swap(rows_odd, "gy", 1)
    rows_even = swap(rows_even, "gy", 0)
    block = call(
        functools.partial(observe, members, count, n_obs),
        out_shape=shape(BLOCK),
        in_specs=[VMEM] * 8,
        out_specs=VMEM,
        scratch_shapes=[tall],
        name="observe",
    )(field, tile_flow, *ready, rows_odd, rows_even)
    blocks = row_blocks(block)
    packet = call(
        functools.partial(complete, members, n_obs, size),
        out_shape=shape(n_obs * size),
        in_specs=[VMEM],
        out_specs=VMEM,
        name="complete",
    )(blocks)
    anomaly, mean = call(
        functools.partial(forecast, members, count, size),
        out_shape=[jax.ShapeDtypeStruct((3 * members, count * width), jnp.bfloat16), shape(count)],
        in_specs=[VMEM] * 5,
        out_specs=[VMEM] * 2,
        scratch_shapes=[tall],
        cost_estimate=pl.CostEstimate(flops=4 * 10**6, bytes_accessed=6 * 10**5, transcendentals=0),
        name="forecast",
    )(field, tile_flow, rows_odd, rows_even, blocks)
    packets = all_rows(packet)
    out = call(
        functools.partial(analyse, members, count),
        out_shape=shape(members * count),
        in_specs=[VMEM] * (2 + len(packets)),
        out_specs=VMEM,
        scratch_shapes=[pltpu.VMEM((members, 8, width), F32)],
        name="analyse",
    )(anomaly, mean, *packets)
    return out.reshape(ensemble.shape)


def solution(mesh):
    return jax.shard_map(
        body,
        mesh=mesh,
        in_specs=(
            P(None, "gy", "gx"),
            P(None, "gy", "gx"),
            P("gy", "gx", None),
            P("gy", "gx", None),
            P("gy", "gx", None),
        ),
        out_specs=P(None, "gy", "gx"),
        check_vma=False,
    )
```

```python
import functools

import jax
import jax.numpy as jnp
from jax import lax
from jax.experimental import pallas as pl
from jax.experimental.pallas import tpu as pltpu
from jax.sharding import PartitionSpec as P

F32 = jnp.float32
PARAMS = pltpu.CompilerParams(vmem_limit_bytes=24 * 1024 * 1024)
VMEM = pl.BlockSpec(memory_space=pltpu.VMEM)
SMEM = pl.BlockSpec(memory_space=pltpu.SMEM)


def lanes(shape):
    return lax.broadcasted_iota(jnp.int32, shape, len(shape) - 1)


def rows_of(shape):
    return lax.broadcasted_iota(jnp.int32, shape, len(shape) - 2)


def shifted(x, amount):
    return pltpu.roll(x, amount % x.shape[-1], x.ndim - 1)


EDGE = 16
BLOCK = 24
MID, OBS = 8, 16
FORECAST = 4
VALUE, FACTOR, TO_WEST, TO_EAST, WEIGHTS = 64, 65, 66, 67, 72
HBM = pl.BlockSpec(memory_space=pltpu.HBM)
ANY = pl.BlockSpec(memory_space=pl.ANY)


def coefficients(k, u, v):
    return 1.0 - 4.0 * k, k + 0.5 * v, k - 0.5 * v, k + 0.5 * u, k - 0.5 * u


def combine(c, own, north, south, west, east):
    return c[0] * own + c[1] * north + c[2] * south + c[3] * west + c[4] * east


def transposed(x):
    return jnp.concatenate([x, jnp.zeros((128 - x.shape[0], 128), F32)], axis=0).T


def load(members, count, ens_hbm, flow_hbm, even_ref, odd_ref, sems):
    is_even = lax.axis_index("gy") % 2 == 0
    for ref in (even_ref, odd_ref):
        ref[2 * members :, :] = jnp.zeros((8, 128), F32)

    def copies(refs):
        for i, (ref, near, second) in enumerate(zip(refs, (count - 1, 0), (count - 2, 1))):
            yield pltpu.make_async_copy(ens_hbm.at[:, near, :], ref.at[pl.ds(0, members), :], sems.at[3 * i])
            yield pltpu.make_async_copy(ens_hbm.at[:, second, :], ref.at[pl.ds(members, members), :], sems.at[3 * i + 1])
            yield pltpu.make_async_copy(flow_hbm.at[:, near, :], ref.at[pl.ds(2 * members, 3), :], sems.at[3 * i + 2])

    def bring(refs):
        for copy in list(copies(refs)):
            copy.start()
        for copy in list(copies(refs)):
            copy.wait()

    pl.when(is_even)(lambda: bring((even_ref, odd_ref)))
    pl.when(jnp.logical_not(is_even))(lambda: bring((odd_ref, even_ref)))


def halo_rows(even_ref, odd_ref, members):
    at = lax.axis_index("gy")
    is_even = at % 2 == 0
    inside = at > 0, at < lax.axis_size("gy") - 1
    parts = []
    for lo, hi in ((0, members), (members, 2 * members), (2 * members, 2 * members + 3)):
        e, o = even_ref[lo:hi, :], odd_ref[lo:hi, :]
        pair = jnp.where(is_even, o, e), jnp.where(is_even, e, o)
        parts.append([jnp.where(here, x, 0.0) for here, x in zip(inside, pair)])
    return tuple(p[0] for p in parts), tuple(p[1] for p in parts)


def tall_coefficients(scratch, flow_ref, north_flow, south_flow, count):
    for k in range(3):
        scratch[k, 0:count, :] = flow_ref[k]
        scratch[k, count:, :] = jnp.zeros((EDGE - count, 128), F32)
        scratch[k, count : count + 1, :] = south_flow[k : k + 1]
        scratch[k, EDGE - 1 : EDGE, :] = north_flow[k : k + 1]
    return coefficients(*[scratch[k] for k in range(3)])


def tall_field(field_ref, north, south, members, count):
    field = {-2: north[1], -1: north[0], count: south[0], count + 1: south[1]}
    field.update({r: field_ref[r * members : (r + 1) * members, :] for r in range(count)})
    return field


def spread(w, coeffs, lane):
    own, up, down, left, right = coeffs
    to_west, to_east = left * w, right * w
    inside = (
        own * w
        + pltpu.roll(up * w, EDGE - 1, 0)
        + pltpu.roll(down * w, 1, 0)
        + jnp.where(lane == 127, 0.0, shifted(to_west, -1))
        + jnp.where(lane == 0, 0.0, shifted(to_east, 1))
    )
    has_west = lax.axis_index("gx") > 0
    has_east = lax.axis_index("gx") < lax.axis_size("gx") - 1
    return inside, jnp.where(has_west, to_west[:, 0:1], 0.0), jnp.where(has_east, to_east[:, 127:128], 0.0)


def prepare(
    members, count, n_obs, ens_hbm, flow_hbm, cell_hbm, value_hbm, var_hbm, sent_ref,
    field_ref, flow_ref, packed_ref, meta_ref, weight_ref, rest_ref, cell_ref, value_ref, var_ref, tall_ref, sems,
):
    copies = [
        pltpu.make_async_copy(ens_hbm.at[:, r, :], field_ref.at[pl.ds(r * members, members), :], sems.at[r])
        for r in range(count)
    ]
    pairs = ((flow_hbm, flow_ref), (cell_hbm, cell_ref), (value_hbm, value_ref), (var_hbm, var_ref))
    copies += [pltpu.make_async_copy(src, dst, sems.at[count + i]) for i, (src, dst) in enumerate(pairs)]
    for copy in copies:
        copy.start()
    for copy in copies:
        copy.wait()
    lane, sub = lanes((EDGE, 128)), rows_of((EDGE, 128))
    wide = lanes((members, 128))
    nothing = jnp.zeros((3, 128), F32)
    coeffs = tall_coefficients(tall_ref, flow_ref, nothing, nothing, count)
    coeffs = (jnp.where(sub < count, coeffs[0], 0.0),) + coeffs[1:]
    own, up, down, left, right = coeffs
    field = [field_ref[r * members : (r + 1) * members, :] for r in range(count)]
    packed = jnp.zeros((members, 128), F32)
    second = jnp.zeros((members, 128), F32)
    for r, x in enumerate(field):
        packed = jnp.where(wide == r, shifted(x, r), packed)
        packed = jnp.where(wide == 8 + r, shifted(x, 8 + r - 127), packed)
        second = jnp.where(wide == r, shifted(x, r - 1), second)
        second = jnp.where(wide == 8 + r, shifted(x, 8 + r - 126), second)

    def edge_row(low, high):
        both = jnp.where(lane == sub, low[:, 0:1], jnp.where(lane == sub + 8, high[:, 127:128], 0.0))
        return jnp.sum(both, axis=0, keepdims=True)

    middle = (
        edge_row(own, own) * packed
        + edge_row(up, up) * jnp.where(wide % 8 == 0, 0.0, shifted(packed, 1))
        + edge_row(down, down) * jnp.where(wide % 8 == 7, 0.0, shifted(packed, -1))
        + edge_row(right, left) * second
    )
    packed = jnp.where((wide >= 16) & (wide < 32), shifted(middle, 16), packed)
    top_lane, top_sub = lane[:8], sub[:8]
    blocks = []
    for ref, rest in ((value_ref, 0.0), (var_ref, 1.0)):
        block = jnp.full((8, 128), rest, F32)
        for j in range(n_obs):
            block = jnp.where(top_sub == FORECAST + j, ref[j], block)
        blocks.append(block)
    meta = jnp.where(top_lane == VALUE, blocks[0], 0.0)
    meta = jnp.where(top_lane == FACTOR, lax.rsqrt(blocks[1]), meta)
    meta = jnp.where(top_lane == TO_WEST, left[:8, 0:1], meta)
    meta = jnp.where(top_lane == TO_EAST, right[:8, 127:128], meta)
    for j in range(n_obs):
        here = jnp.where((sub < count) & (sub * 128 + lane == cell_ref[j]), 1.0, 0.0)
        first, mid_west, mid_east = spread(here, coeffs, lane)
        w, west, east = spread(first, coeffs, lane)
        weight_ref[j] = first
        rest_ref[j] = w
        total = w[0:1, :] * field[0]
        for r in range(1, count):
            total = total + w[r : r + 1, :] * field[r]
        packed = jnp.where(wide == 32 + FORECAST + j, jnp.sum(total, axis=1, keepdims=True), packed)
        for k, column in ((0, west), (2, east), (4, mid_west), (5, mid_east)):
            meta = jnp.where(top_lane == WEIGHTS + k * n_obs + j, column[:8], meta)
    packed_ref[...] = packed
    meta_ref[0:8, :] = meta
    last = count - 1
    fix = jnp.zeros((8, 128), F32)
    for at, c, r, col in ((16, up, 0, 0), (24, up, 0, 127), (16 + last, down, last, 0), (24 + last, down, last, 127)):
        fix = jnp.where(top_lane == at, c[r : r + 1, col : col + 1], fix)
    meta_ref[8:16, :] = fix


def observe(
    members, count, n_obs, field_ref, flow_ref, packed_ref, meta_ref, weight_ref, rest_ref, odd_ref, even_ref,
    out_ref, tall_ref,
):
    north, south = halo_rows(even_ref, odd_ref, members)
    lane, sub = lanes((EDGE, 128)), rows_of((EDGE, 128))
    wide = lanes((members, 128))
    for k in range(3):
        tall_ref[k] = jnp.zeros((EDGE, 128), F32)
        tall_ref[k, count : count + 1, :] = south[2][k : k + 1]
        tall_ref[k, EDGE - 1 : EDGE, :] = north[2][k : k + 1]
    coeffs = coefficients(*[tall_ref[k] for k in range(3)])
    coeffs = (jnp.where((sub == count) | (sub == EDGE - 1), coeffs[0], 0.0),) + coeffs[1:]
    rows = {-2: north[1], -1: north[0], count: south[0], count + 1: south[1]}
    tile_rows = {r: field_ref[r * members : (r + 1) * members, :] for r in (0, count - 1)}
    packed, meta, fix = packed_ref[...], meta_ref[0:8, :], meta_ref[8:9, :]
    for x, to, at in ((rows[-1], 34, 0), (rows[count], 32, count - 1)):
        packed = jnp.where(wide == to, shifted(x, to), packed)
        packed = jnp.where(wide == to + 1, shifted(x, to + 1 - 127), packed)
        moved = jnp.where(wide == 16 + at, shifted(x, 16 + at), 0.0)
        moved = jnp.where(wide == 24 + at, shifted(x, 24 + at - 127), moved)
        packed = packed + fix * moved
    top_lane, top_sub = lane[:8], sub[:8]
    for j in range(n_obs):
        w, west, east = spread(weight_ref[j], coeffs, lane)
        all_w = w + rest_ref[j]
        total = sum(all_w[r % EDGE : r % EDGE + 1, :] * x for r, x in rows.items())
        total += sum(w[r : r + 1, :] * x for r, x in tile_rows.items())
        packed = jnp.where(wide == 32 + FORECAST + j, packed + jnp.sum(total, axis=1, keepdims=True), packed)
        outer = jnp.zeros((8, 128), F32)
        for at, column, slot in ((0, east, count), (1, west, count), (2, east, EDGE - 1), (3, west, EDGE - 1)):
            outer = jnp.where(top_sub == at, column[slot : slot + 1], outer)
        meta = jnp.where(top_lane == WEIGHTS + n_obs + j, outer, meta)
    turned = jnp.concatenate([packed, jnp.zeros((128 - members, 128), F32)], axis=0).T
    out_ref[0:8, :] = turned[0:8] + shifted(turned[8:16], 64)
    out_ref[MID : MID + 8, :] = turned[16:24] + shifted(turned[24:32], 64)
    out_ref[OBS : OBS + 8, :] = turned[32:40] + meta


def block_rows(ref, start, tile, size):
    return ref[pl.ds(pl.multiple_of(place_of(tile, size) * BLOCK + start, 8), 8), :]


def side_columns(ref, tile, size):
    west, east = jnp.maximum(tile - 1, 0), jnp.minimum(tile + 1, size - 1)
    own = block_rows(ref, 0, tile, size)
    rest = block_rows(ref, OBS, west, size), block_rows(ref, OBS, east, size)
    columns = shifted(block_rows(ref, 0, west, size), 64), block_rows(ref, 0, east, size)
    west_mid = shifted(block_rows(ref, MID, west, size), 64) + rest[0][:, TO_EAST : TO_EAST + 1] * own
    east_mid = block_rows(ref, MID, east, size) + rest[1][:, TO_WEST : TO_WEST + 1] * shifted(own, 64)
    return columns, (west_mid, east_mid), rest


def complete(members, n_obs, size, blocks_ref, out_ref):
    rows = n_obs * size
    lane, sub = lanes((rows, 128)), rows_of((rows, 128))
    at = own = jnp.zeros((rows, 128), F32)
    for tile in range(size):
        columns, mids, rest = side_columns(blocks_ref, jnp.int32(tile), size)
        block = block_rows(blocks_ref, OBS, jnp.int32(tile), size)
        odd = rows_of((8, 128)) % 2 == 1
        terms = [(1, jnp.where(odd, *rest) if 0 < tile < size - 1 else rest[tile == 0])]
        if tile > 0:
            terms += [(0, columns[0]), (4, mids[0])]
        if tile < size - 1:
            terms += [(2, columns[1]), (5, mids[1])]
        for j in range(n_obs):
            total = jnp.zeros((8, 128), F32)
            for k, term in terms:
                place = WEIGHTS + k * n_obs + j
                total = total + block[:, place : place + 1] * term
            observed = block[FORECAST + j : FORECAST + j + 1, :]
            row = jnp.sum(total, axis=0, keepdims=True) + observed
            here = sub == n_obs * tile + j
            at = jnp.where(here, row, at)
            own = jnp.where(here, observed, own)
    at = jnp.where(lane < members, at, 0.0)
    mean = jnp.sum(at, axis=1, keepdims=True) * (1.0 / members)
    raw = jnp.where(lane < members, at - mean, jnp.where(lane == members, own[:, VALUE : VALUE + 1] - mean, 0.0))
    out_ref[...] = raw * own[:, FACTOR : FACTOR + 1]


def forecast(members, count, size, field_ref, flow_ref, odd_ref, even_ref, blocks_ref, out_ref, mean_ref, tall_ref):
    north, south = halo_rows(even_ref, odd_ref, members)
    tile = lax.axis_index("gx")
    inside = tile > 0, tile < size - 1
    sides = [jnp.where(here, x, 0.0) for pair in side_columns(blocks_ref, tile, size) for here, x in zip(inside, pair)]
    sides.append(jnp.zeros((80, 128), F32))
    sides = jnp.concatenate(sides, axis=0).T[:members]
    field = tall_field(field_ref, north, south, members, count)
    tall = tall_coefficients(tall_ref, flow_ref, north[2], south[2], count)
    lane = lanes((members, 128))

    def step(rows, r, west_at, east_at):
        w = jnp.where(lane == 0, shifted(sides, -west_at), shifted(rows[r], 1))
        e = jnp.where(lane == 127, shifted(sides, 127 - east_at), shifted(rows[r], -1))
        at = r % EDGE
        return combine([c[at : at + 1, :] for c in tall], rows[r], rows[r - 1], rows[r + 1], w, e)

    middle = {r: step(field, r, r, 8 + r) for r in range(count)}
    middle.update({-1: step(field, -1, 35, 42), count: step(field, count, 33, 40)})
    for r in range(count):
        x = step(middle, r, 16 + r, 24 + r)
        mean = jnp.sum(x, axis=0, keepdims=True) * (1.0 / members)
        mean_ref[r : r + 1, :] = mean
        x = x - mean
        high = x.astype(jnp.bfloat16)
        at = slice(128 * r, 128 * (r + 1))
        out_ref[0:members, at] = high
        out_ref[members : 2 * members, at] = (x - high.astype(F32)).astype(jnp.bfloat16)
        out_ref[2 * members :, at] = high


def eliminated(a, members, column_ref):
    size = 8
    lane, sub = lanes((size, 128)), rows_of((size, 128))
    part = [a[size * q : size * (q + 1), :] for q in range(members // size)]
    pivot = []

    def spread(q, c):
        return jnp.broadcast_to(part[q][:, c : c + 1], (size, 128))

    ahead = {(0, c): spread(0, c) for c in range(size)}
    for p in range(len(part)):
        start, end = size * p, size * (p + 1)
        rest = range(p, len(part))
        column = {(q, c): spread(q, c) for q in rest[1:] for c in range(start, end)}
        column.update(ahead)
        more = range(end, end + size if p + 1 < len(part) else end)
        column.update({(q, c): spread(q, c) for q in rest[1:2] for c in more})
        mine = (lane >= start) & (lane < end)
        for q in rest:
            part[q] = jnp.where(mine, 0.0, part[q])
        found = jnp.zeros((size, 128), F32)
        for j in range(size):
            at = start + j
            value = column[p, at][j : j + 1, :]
            found = jnp.where(sub == j, value, found)
            inverse = 1.0 / value
            unit = jnp.where(lane[:1] == at, 1.0, part[p][j : j + 1, :])
            pivots = {c: column[p, c][j : j + 1, :] for c in range(at + 1, end)}
            if more:
                column_ref[at] = column[p + 1, at]
            pivots.update({c: column_ref[at, c - end : c - end + 1, :] for c in more})
            for q in rest:
                factor = column[q, at] * inverse
                for c in range(at + 1, end + (len(more) if q == p + 1 else 0)):
                    column[q, c] = column[q, c] - factor * pivots[c]
                if q == p:
                    factor = jnp.where(sub > j, factor, 0.0)
                part[q] = part[q] - factor * unit
        pivot.append(found)
        ahead = {(p + 1, c): column[p + 1, c] for c in more}
    return jnp.concatenate(part, axis=0), jnp.concatenate(pivot, axis=0)


def thirds(x):
    first = x.astype(jnp.bfloat16)
    rest = x - first.astype(F32)
    second = rest.astype(jnp.bfloat16)
    return first, second, (rest - second.astype(F32)).astype(jnp.bfloat16)


def product(lefts, rights):
    left, right = jnp.concatenate(lefts, axis=1), jnp.concatenate(rights, axis=0)
    return jnp.dot(left, right, preferred_element_type=F32)


def analyse(members, count, f_ref, mean_ref, *refs):
    out_ref, column_ref = refs[-2:]
    scaled = jnp.concatenate([ref[...] for ref in refs[:-2]], axis=0)
    a1, a2, a3 = thirds(scaled)
    t1, t2, t3 = thirds(scaled.T[:members])
    full = product([t1, t2], [a1, a1]) + (product([t1, t2], [a2, a2]) + product([t1, t3], [a3, a1]))
    lane, sub = lanes((members, 128)), rows_of((members, 128))
    a, pivots = eliminated(full + jnp.where(lane == sub, members - 1.0, 0.0), members, column_ref)
    scale = lax.rsqrt(pivots)
    inverse = scale * jnp.where(lane < sub, a, jnp.where(lane == sub, 1.0, 0.0))
    reduced = scale * a[:, members : members + 1]
    weights = jnp.sum(reduced * inverse, axis=0, keepdims=True)
    transform = (jnp.sqrt(members - 1.0) * inverse + weights)[:, :members]
    high = transform.astype(jnp.bfloat16)
    low = (transform - high.astype(F32)).astype(jnp.bfloat16)
    update = product([high, high, low], [f_ref[...]])
    for r in range(count):
        out_ref[pl.ds(r, members, stride=count), :] = update[:, 128 * r : 128 * (r + 1)] + mean_ref[r : r + 1, :]


def swap(x, axis, offset):
    ny, nx = lax.axis_size("gy"), lax.axis_size("gx")
    partner = {i: i for i in range(ny)}
    for i in range(offset, ny - 1, 2):
        partner[i], partner[i + 1] = i + 1, i
    pairs = []
    for a in range(ny):
        for b in range(nx):
            if partner[a] != a:
                pairs.append((a * nx + b, partner[a] * nx + b))
            elif nx % 2 == 0:
                pairs.append((a * nx + b, a * nx + (b ^ 1)))
    return lax.ppermute(x, ("gy", "gx"), pairs)


def two_power(size):
    return size & (size - 1) == 0


def partner(x, flip_y, flip_x):
    ny, nx = lax.axis_size("gy"), lax.axis_size("gx")
    pairs = [(a * nx + b, (a ^ flip_y) * nx + (b ^ flip_x)) for a in range(ny) for b in range(nx)]
    return lax.ppermute(x, ("gy", "gx"), pairs)


def doubled(x, flip_y, flip_x):
    return jnp.concatenate([x, partner(x, flip_y, flip_x)], axis=0)


def row_blocks(block):
    size = step = lax.axis_size("gx")
    if not two_power(size):
        return lax.all_gather(block, "gx", tiled=True)
    while step > 2:
        step //= 2
        block = doubled(block, 0, step | 1)
    return doubled(block, 0, 1) if size > 1 else block


def place_of(tile, size):
    if not two_power(size) or size == 1:
        return tile
    distance = jnp.bitwise_xor(lax.axis_index("gx"), tile)
    place, last, value, bit = 0, distance % 2, 1, size // 2
    while bit > 1:
        chosen = (distance // bit) % 2
        place, last = place + chosen * value, jnp.bitwise_xor(last, chosen)
        value, bit = 2 * value, bit // 2
    return place + last * value


def all_rows(packet):
    ny, nx = lax.axis_size("gy"), lax.axis_size("gx")
    if not two_power(ny) or ny < 4 or nx % 2:
        return [lax.all_gather(packet, "gy", tiled=True)]
    step = ny // 2
    while step > 2:
        packet = doubled(packet, step, 1)
        step //= 2
    pairs = [(a * nx + b, (a ^ (2 - b % 2)) * nx + (b ^ 1)) for a in range(ny) for b in range(nx)]
    near = lax.ppermute(packet, ("gy", "gx"), pairs)
    return [packet, near, partner(packet, 3, 1), partner(near, 0, 1)]


def body(ensemble, flow, obs_cell, obs_value, obs_var):
    members, count, width = ensemble.shape
    n_obs = obs_cell.shape[-1]
    size = lax.axis_size("gx")
    call = functools.partial(pl.pallas_call, compiler_params=PARAMS)

    def shape(*dims):
        return jax.ShapeDtypeStruct(dims + (width,), F32)

    inputs = [
        pltpu.with_memory_space_constraint(x, pltpu.HBM)
        for x in (ensemble, flow, obs_cell.reshape(-1), obs_value.reshape(-1), obs_var.reshape(-1))
    ]
    rows_even, rows_odd = call(
        functools.partial(load, members, count),
        out_shape=[shape(2 * members + 8)] * 2,
        in_specs=[HBM] * 2,
        out_specs=[VMEM] * 2,
        scratch_shapes=[pltpu.SemaphoreType.DMA((6,))],
        name="load",
    )(*inputs[:2])
    tall = pltpu.VMEM((3, EDGE, width), F32)
    field, tile_flow, *ready = call(
        functools.partial(prepare, members, count, n_obs),
        out_shape=[shape(members * count), shape(3, count), shape(members), shape(16)] + [shape(n_obs, EDGE)] * 2,
        in_specs=[HBM] * 5 + [ANY],
        out_specs=[VMEM] * 6,
        scratch_shapes=[pltpu.SMEM((n_obs,), jnp.int32)]
        + [pltpu.SMEM((n_obs,), F32)] * 2
        + [tall, pltpu.SemaphoreType.DMA((count + 4,))],
        cost_estimate=pl.CostEstimate(flops=4 * 10**6, bytes_accessed=6 * 10**5, transcendentals=0),
        name="prepare",
    )(*inputs, rows_even)
    rows_odd = swap(rows_odd, "gy", 1)
    rows_even = swap(rows_even, "gy", 0)
    block = call(
        functools.partial(observe, members, count, n_obs),
        out_shape=shape(BLOCK),
        in_specs=[VMEM] * 8,
        out_specs=VMEM,
        scratch_shapes=[tall],
        name="observe",
    )(field, tile_flow, *ready, rows_odd, rows_even)
    blocks = row_blocks(block)
    packet = call(
        functools.partial(complete, members, n_obs, size),
        out_shape=shape(n_obs * size),
        in_specs=[VMEM],
        out_specs=VMEM,
        name="complete",
    )(blocks)
    anomaly, mean = call(
        functools.partial(forecast, members, count, size),
        out_shape=[jax.ShapeDtypeStruct((3 * members, count * width), jnp.bfloat16), shape(count)],
        in_specs=[VMEM] * 5,
        out_specs=[VMEM] * 2,
        scratch_shapes=[tall],
        cost_estimate=pl.CostEstimate(flops=4 * 10**6, bytes_accessed=6 * 10**5, transcendentals=0),
        name="forecast",
    )(field, tile_flow, rows_odd, rows_even, blocks)
    packets = all_rows(packet)
    out = call(
        functools.partial(analyse, members, count),
        out_shape=shape(members * count),
        in_specs=[VMEM] * (2 + len(packets)),
        out_specs=VMEM,
        scratch_shapes=[pltpu.VMEM((members, 8, width), F32)],
        name="analyse",
    )(anomaly, mean, *packets)
    return out.reshape(ensemble.shape)


def solution(mesh):
    return jax.shard_map(
        body,
        mesh=mesh,
        in_specs=(
            P(None, "gy", "gx"),
            P(None, "gy", "gx"),
            P("gy", "gx", None),
            P("gy", "gx", None),
            P("gy", "gx", None),
        ),
        out_specs=P(None, "gy", "gx"),
        check_vma=False,
    )
```

```python
import functools

import jax
import jax.numpy as jnp
from jax import lax
from jax.experimental import pallas as pl
from jax.experimental.pallas import tpu as pltpu
from jax.sharding import PartitionSpec as P

F32 = jnp.float32
PARAMS = pltpu.CompilerParams(vmem_limit_bytes=24 * 1024 * 1024)
VMEM = pl.BlockSpec(memory_space=pltpu.VMEM)
SMEM = pl.BlockSpec(memory_space=pltpu.SMEM)


def lanes(shape):
    return lax.broadcasted_iota(jnp.int32, shape, len(shape) - 1)


def rows_of(shape):
    return lax.broadcasted_iota(jnp.int32, shape, len(shape) - 2)


def shifted(x, amount):
    return pltpu.roll(x, amount % x.shape[-1], x.ndim - 1)


EDGE = 16
BLOCK = 24
MID, OBS = 8, 16
FORECAST = 4
VALUE, FACTOR, TO_WEST, TO_EAST, WEIGHTS = 64, 65, 66, 67, 72
HBM = pl.BlockSpec(memory_space=pltpu.HBM)
ANY = pl.BlockSpec(memory_space=pl.ANY)


def coefficients(k, u, v):
    return 1.0 - 4.0 * k, k + 0.5 * v, k - 0.5 * v, k + 0.5 * u, k - 0.5 * u


def combine(c, own, north, south, west, east):
    return c[0] * own + c[1] * north + c[2] * south + c[3] * west + c[4] * east


def transposed(x):
    return jnp.concatenate([x, jnp.zeros((128 - x.shape[0], 128), F32)], axis=0).T


def load(members, count, ens_hbm, flow_hbm, even_ref, odd_ref, sems):
    is_even = lax.axis_index("gy") % 2 == 0
    for ref in (even_ref, odd_ref):
        ref[2 * members :, :] = jnp.zeros((8, 128), F32)

    def copies(refs):
        for i, (ref, near, second) in enumerate(zip(refs, (count - 1, 0), (count - 2, 1))):
            yield pltpu.make_async_copy(ens_hbm.at[:, near, :], ref.at[pl.ds(0, members), :], sems.at[3 * i])
            yield pltpu.make_async_copy(ens_hbm.at[:, second, :], ref.at[pl.ds(members, members), :], sems.at[3 * i + 1])
            yield pltpu.make_async_copy(flow_hbm.at[:, near, :], ref.at[pl.ds(2 * members, 3), :], sems.at[3 * i + 2])

    def bring(refs):
        for copy in list(copies(refs)):
            copy.start()
        for copy in list(copies(refs)):
            copy.wait()

    pl.when(is_even)(lambda: bring((even_ref, odd_ref)))
    pl.when(jnp.logical_not(is_even))(lambda: bring((odd_ref, even_ref)))


def halo_rows(even_ref, odd_ref, members):
    at = lax.axis_index("gy")
    is_even = at % 2 == 0
    inside = at > 0, at < lax.axis_size("gy") - 1
    parts = []
    for lo, hi in ((0, members), (members, 2 * members), (2 * members, 2 * members + 3)):
        e, o = even_ref[lo:hi, :], odd_ref[lo:hi, :]
        pair = jnp.where(is_even, o, e), jnp.where(is_even, e, o)
        parts.append([jnp.where(here, x, 0.0) for here, x in zip(inside, pair)])
    return tuple(p[0] for p in parts), tuple(p[1] for p in parts)


def tall_coefficients(scratch, flow_ref, north_flow, south_flow, count):
    for k in range(3):
        scratch[k, 0:count, :] = flow_ref[k]
        scratch[k, count:, :] = jnp.zeros((EDGE - count, 128), F32)
        scratch[k, count : count + 1, :] = south_flow[k : k + 1]
        scratch[k, EDGE - 1 : EDGE, :] = north_flow[k : k + 1]
    return coefficients(*[scratch[k] for k in range(3)])


def tall_field(field_ref, north, south, members, count):
    field = {-2: north[1], -1: north[0], count: south[0], count + 1: south[1]}
    field.update({r: field_ref[r * members : (r + 1) * members, :] for r in range(count)})
    return field


def spread(w, coeffs, lane):
    own, up, down, left, right = coeffs
    to_west, to_east = left * w, right * w
    inside = (
        own * w
        + pltpu.roll(up * w, EDGE - 1, 0)
        + pltpu.roll(down * w, 1, 0)
        + jnp.where(lane == 127, 0.0, shifted(to_west, -1))
        + jnp.where(lane == 0, 0.0, shifted(to_east, 1))
    )
    has_west = lax.axis_index("gx") > 0
    has_east = lax.axis_index("gx") < lax.axis_size("gx") - 1
    return inside, jnp.where(has_west, to_west[:, 0:1], 0.0), jnp.where(has_east, to_east[:, 127:128], 0.0)


def prepare(
    members, count, n_obs, ens_hbm, flow_hbm, cell_hbm, value_hbm, var_hbm, sent_ref,
    field_ref, flow_ref, packed_ref, meta_ref, weight_ref, rest_ref, cell_ref, value_ref, var_ref, tall_ref, sems,
):
    copies = [
        pltpu.make_async_copy(ens_hbm.at[:, r, :], field_ref.at[pl.ds(r * members, members), :], sems.at[r])
        for r in range(count)
    ]
    pairs = ((flow_hbm, flow_ref), (cell_hbm, cell_ref), (value_hbm, value_ref), (var_hbm, var_ref))
    copies += [pltpu.make_async_copy(src, dst, sems.at[count + i]) for i, (src, dst) in enumerate(pairs)]
    for copy in copies:
        copy.start()
    for copy in copies:
        copy.wait()
    lane, sub = lanes((EDGE, 128)), rows_of((EDGE, 128))
    wide = lanes((members, 128))
    nothing = jnp.zeros((3, 128), F32)
    coeffs = tall_coefficients(tall_ref, flow_ref, nothing, nothing, count)
    coeffs = (jnp.where(sub < count, coeffs[0], 0.0),) + coeffs[1:]
    own, up, down, left, right = coeffs
    field = [field_ref[r * members : (r + 1) * members, :] for r in range(count)]
    packed = jnp.zeros((members, 128), F32)
    second = jnp.zeros((members, 128), F32)
    for r, x in enumerate(field):
        packed = jnp.where(wide == r, shifted(x, r), packed)
        packed = jnp.where(wide == 8 + r, shifted(x, 8 + r - 127), packed)
        second = jnp.where(wide == r, shifted(x, r - 1), second)
        second = jnp.where(wide == 8 + r, shifted(x, 8 + r - 126), second)

    def edge_row(low, high):
        both = jnp.where(lane == sub, low[:, 0:1], jnp.where(lane == sub + 8, high[:, 127:128], 0.0))
        return jnp.sum(both, axis=0, keepdims=True)

    middle = (
        edge_row(own, own) * packed
        + edge_row(up, up) * jnp.where(wide % 8 == 0, 0.0, shifted(packed, 1))
        + edge_row(down, down) * jnp.where(wide % 8 == 7, 0.0, shifted(packed, -1))
        + edge_row(right, left) * second
    )
    packed = jnp.where((wide >= 16) & (wide < 32), shifted(middle, 16), packed)
    top_lane, top_sub = lane[:8], sub[:8]
    blocks = []
    for ref, rest in ((value_ref, 0.0), (var_ref, 1.0)):
        block = jnp.full((8, 128), rest, F32)
        for j in range(n_obs):
            block = jnp.where(top_sub == FORECAST + j, ref[j], block)
        blocks.append(block)
    meta = jnp.where(top_lane == VALUE, blocks[0], 0.0)
    meta = jnp.where(top_lane == FACTOR, lax.rsqrt(blocks[1]), meta)
    meta = jnp.where(top_lane == TO_WEST, left[:8, 0:1], meta)
    meta = jnp.where(top_lane == TO_EAST, right[:8, 127:128], meta)
    for j in range(n_obs):
        here = jnp.where((sub < count) & (sub * 128 + lane == cell_ref[j]), 1.0, 0.0)
        first, mid_west, mid_east = spread(here, coeffs, lane)
        w, west, east = spread(first, coeffs, lane)
        weight_ref[j] = first
        rest_ref[j] = w
        total = w[0:1, :] * field[0]
        for r in range(1, count):
            total = total + w[r : r + 1, :] * field[r]
        packed = jnp.where(wide == 32 + FORECAST + j, jnp.sum(total, axis=1, keepdims=True), packed)
        for k, column in ((0, west), (2, east), (4, mid_west), (5, mid_east)):
            meta = jnp.where(top_lane == WEIGHTS + k * n_obs + j, column[:8], meta)
    packed_ref[...] = packed
    meta_ref[0:8, :] = meta
    last = count - 1
    fix = jnp.zeros((8, 128), F32)
    for at, c, r, col in ((16, up, 0, 0), (24, up, 0, 127), (16 + last, down, last, 0), (24 + last, down, last, 127)):
        fix = jnp.where(top_lane == at, c[r : r + 1, col : col + 1], fix)
    meta_ref[8:16, :] = fix


def observe(
    members, count, n_obs, field_ref, flow_ref, packed_ref, meta_ref, weight_ref, rest_ref, even_ref, odd_ref,
    out_ref, tall_ref,
):
    north, south = halo_rows(even_ref, odd_ref, members)
    lane, sub = lanes((EDGE, 128)), rows_of((EDGE, 128))
    wide = lanes((members, 128))
    for k in range(3):
        tall_ref[k] = jnp.zeros((EDGE, 128), F32)
        tall_ref[k, count : count + 1, :] = south[2][k : k + 1]
        tall_ref[k, EDGE - 1 : EDGE, :] = north[2][k : k + 1]
    coeffs = coefficients(*[tall_ref[k] for k in range(3)])
    coeffs = (jnp.where((sub == count) | (sub == EDGE - 1), coeffs[0], 0.0),) + coeffs[1:]
    rows = {-2: north[1], -1: north[0], count: south[0], count + 1: south[1]}
    tile_rows = {r: field_ref[r * members : (r + 1) * members, :] for r in (0, count - 1)}
    packed, meta, fix = packed_ref[...], meta_ref[0:8, :], meta_ref[8:9, :]
    for x, to, at in ((rows[-1], 34, 0), (rows[count], 32, count - 1)):
        packed = jnp.where(wide == to, shifted(x, to), packed)
        packed = jnp.where(wide == to + 1, shifted(x, to + 1 - 127), packed)
        moved = jnp.where(wide == 16 + at, shifted(x, 16 + at), 0.0)
        moved = jnp.where(wide == 24 + at, shifted(x, 24 + at - 127), moved)
        packed = packed + fix * moved
    top_lane, top_sub = lane[:8], sub[:8]
    for j in range(n_obs):
        w, west, east = spread(weight_ref[j], coeffs, lane)
        all_w = w + rest_ref[j]
        total = sum(all_w[r % EDGE : r % EDGE + 1, :] * x for r, x in rows.items())
        total += sum(w[r : r + 1, :] * x for r, x in tile_rows.items())
        packed = jnp.where(wide == 32 + FORECAST + j, packed + jnp.sum(total, axis=1, keepdims=True), packed)
        outer = jnp.zeros((8, 128), F32)
        for at, column, slot in ((0, east, count), (1, west, count), (2, east, EDGE - 1), (3, west, EDGE - 1)):
            outer = jnp.where(top_sub == at, column[slot : slot + 1], outer)
        meta = jnp.where(top_lane == WEIGHTS + n_obs + j, outer, meta)
    turned = jnp.concatenate([packed, jnp.zeros((128 - members, 128), F32)], axis=0).T
    out_ref[0:8, :] = turned[0:8] + shifted(turned[8:16], 64)
    out_ref[MID : MID + 8, :] = turned[16:24] + shifted(turned[24:32], 64)
    out_ref[OBS : OBS + 8, :] = turned[32:40] + meta


def block_rows(ref, start, tile, size):
    return ref[pl.ds(pl.multiple_of(place_of(tile, size) * BLOCK + start, 8), 8), :]


def side_columns(ref, tile, size):
    west, east = jnp.maximum(tile - 1, 0), jnp.minimum(tile + 1, size - 1)
    own = block_rows(ref, 0, tile, size)
    rest = block_rows(ref, OBS, west, size), block_rows(ref, OBS, east, size)
    columns = shifted(block_rows(ref, 0, west, size), 64), block_rows(ref, 0, east, size)
    west_mid = shifted(block_rows(ref, MID, west, size), 64) + rest[0][:, TO_EAST : TO_EAST + 1] * own
    east_mid = block_rows(ref, MID, east, size) + rest[1][:, TO_WEST : TO_WEST + 1] * shifted(own, 64)
    return columns, (west_mid, east_mid), rest


def complete(members, n_obs, size, blocks_ref, out_ref):
    rows = n_obs * size
    lane, sub = lanes((rows, 128)), rows_of((rows, 128))
    at = own = jnp.zeros((rows, 128), F32)
    for tile in range(size):
        columns, mids, rest = side_columns(blocks_ref, jnp.int32(tile), size)
        block = block_rows(blocks_ref, OBS, jnp.int32(tile), size)
        odd = rows_of((8, 128)) % 2 == 1
        terms = [(1, jnp.where(odd, *rest) if 0 < tile < size - 1 else rest[tile == 0])]
        if tile > 0:
            terms += [(0, columns[0]), (4, mids[0])]
        if tile < size - 1:
            terms += [(2, columns[1]), (5, mids[1])]
        for j in range(n_obs):
            total = jnp.zeros((8, 128), F32)
            for k, term in terms:
                place = WEIGHTS + k * n_obs + j
                total = total + block[:, place : place + 1] * term
            observed = block[FORECAST + j : FORECAST + j + 1, :]
            row = jnp.sum(total, axis=0, keepdims=True) + observed
            here = sub == n_obs * tile + j
            at = jnp.where(here, row, at)
            own = jnp.where(here, observed, own)
    at = jnp.where(lane < members, at, 0.0)
    mean = jnp.sum(at, axis=1, keepdims=True) * (1.0 / members)
    raw = jnp.where(lane < members, at - mean, jnp.where(lane == members, own[:, VALUE : VALUE + 1] - mean, 0.0))
    out_ref[...] = raw * own[:, FACTOR : FACTOR + 1]


def forecast(members, count, size, field_ref, flow_ref, odd_ref, even_ref, blocks_ref, out_ref, mean_ref, tall_ref):
    north, south = halo_rows(even_ref, odd_ref, members)
    tile = lax.axis_index("gx")
    inside = tile > 0, tile < size - 1
    sides = [jnp.where(here, x, 0.0) for pair in side_columns(blocks_ref, tile, size) for here, x in zip(inside, pair)]
    sides.append(jnp.zeros((80, 128), F32))
    sides = jnp.concatenate(sides, axis=0).T[:members]
    field = tall_field(field_ref, north, south, members, count)
    tall = tall_coefficients(tall_ref, flow_ref, north[2], south[2], count)
    lane = lanes((members, 128))

    def step(rows, r, west_at, east_at):
        w = jnp.where(lane == 0, shifted(sides, -west_at), shifted(rows[r], 1))
        e = jnp.where(lane == 127, shifted(sides, 127 - east_at), shifted(rows[r], -1))
        at = r % EDGE
        return combine([c[at : at + 1, :] for c in tall], rows[r], rows[r - 1], rows[r + 1], w, e)

    middle = {r: step(field, r, r, 8 + r) for r in range(count)}
    middle.update({-1: step(field, -1, 35, 42), count: step(field, count, 33, 40)})
    for r in range(count):
        x = step(middle, r, 16 + r, 24 + r)
        mean = jnp.sum(x, axis=0, keepdims=True) * (1.0 / members)
        mean_ref[r : r + 1, :] = mean
        x = x - mean
        high = x.astype(jnp.bfloat16)
        at = slice(128 * r, 128 * (r + 1))
        out_ref[0:members, at] = high
        out_ref[members : 2 * members, at] = (x - high.astype(F32)).astype(jnp.bfloat16)
        out_ref[2 * members :, at] = high


def eliminated(a, members, column_ref):
    size = 8
    lane, sub = lanes((size, 128)), rows_of((size, 128))
    part = [a[size * q : size * (q + 1), :] for q in range(members // size)]
    pivot = []

    def spread(q, c):
        return jnp.broadcast_to(part[q][:, c : c + 1], (size, 128))

    ahead = {(0, c): spread(0, c) for c in range(size)}
    for p in range(len(part)):
        start, end = size * p, size * (p + 1)
        rest = range(p, len(part))
        column = {(q, c): spread(q, c) for q in rest[1:] for c in range(start, end)}
        column.update(ahead)
        more = range(end, end + size if p + 1 < len(part) else end)
        column.update({(q, c): spread(q, c) for q in rest[1:2] for c in more})
        mine = (lane >= start) & (lane < end)
        for q in rest:
            part[q] = jnp.where(mine, 0.0, part[q])
        found = jnp.zeros((size, 128), F32)
        for j in range(size):
            at = start + j
            value = column[p, at][j : j + 1, :]
            found = jnp.where(sub == j, value, found)
            inverse = 1.0 / value
            unit = jnp.where(lane[:1] == at, 1.0, part[p][j : j + 1, :])
            pivots = {c: column[p, c][j : j + 1, :] for c in range(at + 1, end)}
            if more:
                column_ref[at] = column[p + 1, at]
            pivots.update({c: column_ref[at, c - end : c - end + 1, :] for c in more})
            for q in rest:
                factor = column[q, at] * inverse
                for c in range(at + 1, end + (len(more) if q == p + 1 else 0)):
                    column[q, c] = column[q, c] - factor * pivots[c]
                if q == p:
                    factor = jnp.where(sub > j, factor, 0.0)
                part[q] = part[q] - factor * unit
        pivot.append(found)
        ahead = {(p + 1, c): column[p + 1, c] for c in more}
    return jnp.concatenate(part, axis=0), jnp.concatenate(pivot, axis=0)


def thirds(x):
    first = x.astype(jnp.bfloat16)
    rest = x - first.astype(F32)
    second = rest.astype(jnp.bfloat16)
    return first, second, (rest - second.astype(F32)).astype(jnp.bfloat16)


def product(lefts, rights):
    left, right = jnp.concatenate(lefts, axis=1), jnp.concatenate(rights, axis=0)
    return jnp.dot(left, right, preferred_element_type=F32)


def analyse(members, count, f_ref, mean_ref, *refs):
    out_ref, column_ref = refs[-2:]
    scaled = jnp.concatenate([ref[...] for ref in refs[:-2]], axis=0)
    a1, a2, a3 = thirds(scaled)
    t1, t2, t3 = thirds(scaled.T[:members])
    full = product([t1, t2], [a1, a1]) + (product([t1, t2], [a2, a2]) + product([t1, t3], [a3, a1]))
    lane, sub = lanes((members, 128)), rows_of((members, 128))
    a, pivots = eliminated(full + jnp.where(lane == sub, members - 1.0, 0.0), members, column_ref)
    scale = lax.rsqrt(pivots)
    inverse = scale * jnp.where(lane < sub, a, jnp.where(lane == sub, 1.0, 0.0))
    reduced = scale * a[:, members : members + 1]
    weights = jnp.sum(reduced * inverse, axis=0, keepdims=True)
    transform = (jnp.sqrt(members - 1.0) * inverse + weights)[:, :members]
    high = transform.astype(jnp.bfloat16)
    low = (transform - high.astype(F32)).astype(jnp.bfloat16)
    update = product([high, high, low], [f_ref[...]])
    for r in range(count):
        out_ref[pl.ds(r, members, stride=count), :] = update[:, 128 * r : 128 * (r + 1)] + mean_ref[r : r + 1, :]


def swap(x, axis, offset):
    ny, nx = lax.axis_size("gy"), lax.axis_size("gx")
    partner = {i: i for i in range(ny)}
    for i in range(offset, ny - 1, 2):
        partner[i], partner[i + 1] = i + 1, i
    pairs = []
    for a in range(ny):
        for b in range(nx):
            if partner[a] != a:
                pairs.append((a * nx + b, partner[a] * nx + b))
            elif nx % 2 == 0:
                pairs.append((a * nx + b, a * nx + (b ^ 1)))
    return lax.ppermute(x, ("gy", "gx"), pairs)


def two_power(size):
    return size & (size - 1) == 0


def partner(x, flip_y, flip_x):
    ny, nx = lax.axis_size("gy"), lax.axis_size("gx")
    pairs = [(a * nx + b, (a ^ flip_y) * nx + (b ^ flip_x)) for a in range(ny) for b in range(nx)]
    return lax.ppermute(x, ("gy", "gx"), pairs)


def doubled(x, flip_y, flip_x):
    return jnp.concatenate([x, partner(x, flip_y, flip_x)], axis=0)


def row_blocks(block):
    size = step = lax.axis_size("gx")
    if not two_power(size):
        return lax.all_gather(block, "gx", tiled=True)
    while step > 2:
        step //= 2
        block = doubled(block, 0, step | 1)
    return doubled(block, 0, 1) if size > 1 else block


def place_of(tile, size):
    if not two_power(size) or size == 1:
        return tile
    distance = jnp.bitwise_xor(lax.axis_index("gx"), tile)
    place, last, value, bit = 0, distance % 2, 1, size // 2
    while bit > 1:
        chosen = (distance // bit) % 2
        place, last = place + chosen * value, jnp.bitwise_xor(last, chosen)
        value, bit = 2 * value, bit // 2
    return place + last * value


def all_rows(packet):
    ny, nx = lax.axis_size("gy"), lax.axis_size("gx")
    if not two_power(ny) or ny < 4 or nx % 2:
        return [lax.all_gather(packet, "gy", tiled=True)]
    step = ny // 2
    while step > 2:
        packet = doubled(packet, step, 1)
        step //= 2
    pairs = [(a * nx + b, (a ^ (2 - b % 2)) * nx + (b ^ 1)) for a in range(ny) for b in range(nx)]
    near = lax.ppermute(packet, ("gy", "gx"), pairs)
    return [packet, near, partner(packet, 3, 1), partner(near, 0, 1)]


def body(ensemble, flow, obs_cell, obs_value, obs_var):
    members, count, width = ensemble.shape
    n_obs = obs_cell.shape[-1]
    size = lax.axis_size("gx")
    call = functools.partial(pl.pallas_call, compiler_params=PARAMS)

    def shape(*dims):
        return jax.ShapeDtypeStruct(dims + (width,), F32)

    inputs = [
        pltpu.with_memory_space_constraint(x, pltpu.HBM)
        for x in (ensemble, flow, obs_cell.reshape(-1), obs_value.reshape(-1), obs_var.reshape(-1))
    ]
    rows_even, rows_odd = call(
        functools.partial(load, members, count),
        out_shape=[shape(2 * members + 8)] * 2,
        in_specs=[HBM] * 2,
        out_specs=[VMEM] * 2,
        scratch_shapes=[pltpu.SemaphoreType.DMA((6,))],
        name="load",
    )(*inputs[:2])
    tall = pltpu.VMEM((3, EDGE, width), F32)
    field, tile_flow, *ready = call(
        functools.partial(prepare, members, count, n_obs),
        out_shape=[shape(members * count), shape(3, count), shape(members), shape(16)] + [shape(n_obs, EDGE)] * 2,
        in_specs=[HBM] * 5 + [ANY],
        out_specs=[VMEM] * 6,
        scratch_shapes=[pltpu.SMEM((n_obs,), jnp.int32)]
        + [pltpu.SMEM((n_obs,), F32)] * 2
        + [tall, pltpu.SemaphoreType.DMA((count + 4,))],
        cost_estimate=pl.CostEstimate(flops=4 * 10**6, bytes_accessed=6 * 10**5, transcendentals=0),
        name="prepare",
    )(*inputs, rows_even)
    rows_odd = swap(rows_odd, "gy", 1)
    rows_even = swap(rows_even, "gy", 0)
    block = call(
        functools.partial(observe, members, count, n_obs),
        out_shape=shape(BLOCK),
        in_specs=[VMEM] * 8,
        out_specs=VMEM,
        scratch_shapes=[tall],
        name="observe",
    )(field, tile_flow, *ready, rows_even, rows_odd)
    blocks = row_blocks(block)
    packet = call(
        functools.partial(complete, members, n_obs, size),
        out_shape=shape(n_obs * size),
        in_specs=[VMEM],
        out_specs=VMEM,
        name="complete",
    )(blocks)
    anomaly, mean = call(
        functools.partial(forecast, members, count, size),
        out_shape=[jax.ShapeDtypeStruct((3 * members, count * width), jnp.bfloat16), shape(count)],
        in_specs=[VMEM] * 5,
        out_specs=[VMEM] * 2,
        scratch_shapes=[tall],
        cost_estimate=pl.CostEstimate(flops=4 * 10**6, bytes_accessed=6 * 10**5, transcendentals=0),
        name="forecast",
    )(field, tile_flow, rows_odd, rows_even, blocks)
    packets = all_rows(packet)
    out = call(
        functools.partial(analyse, members, count),
        out_shape=shape(members * count),
        in_specs=[VMEM] * (2 + len(packets)),
        out_specs=VMEM,
        scratch_shapes=[pltpu.VMEM((members, 8, width), F32)],
        name="analyse",
    )(anomaly, mean, *packets)
    return out.reshape(ensemble.shape)


def solution(mesh):
    return jax.shard_map(
        body,
        mesh=mesh,
        in_specs=(
            P(None, "gy", "gx"),
            P(None, "gy", "gx"),
            P("gy", "gx", None),
            P("gy", "gx", None),
            P("gy", "gx", None),
        ),
        out_specs=P(None, "gy", "gx"),
        check_vma=False,
    )
```
